256 devices in a mesh: dp: 8 (over y, core), ctx: 32 (over z, x).
Axes of the slice: x: 4, y: 4, z: 8, core: 2. Of those that a mesh axis runs over, the one named last changes fastest.
Arguments:
- attention_query_rows: bfloat16 [32768, 2560], P(('dp', 'ctx')), parts along dimension 0, may hold values from -24 to 24
- key_rows: bfloat16 [32768, 512], P(('dp', 'ctx')), parts along dimension 0, may hold values from -24 to 24
- attention_value_rows: bfloat16 [32768, 512], P(('dp', 'ctx')), parts along dimension 0, may hold values from -6 to 6
- out_grad: bfloat16 [32768, 2560], P(('dp', 'ctx')), parts along dimension 0, may hold values from -6 to 6
- subset_sizes: int32 [128], P('dp'), parts along dimension 0, may hold values from 1 to 4, 32 in all
- ffn_order: int32 [256, 128], P(('dp', 'ctx')), parts along dimension 0, may hold values from 0 to 127, each once within a row
- attn_order: int32 [256, 128], P(('dp', 'ctx')), parts along dimension 0, may hold values from 0 to 127, each once within a row
Outputs:
- attn_out: bfloat16 [32768, 2560], P(('dp', 'ctx')), parts along dimension 0
- query_grad: bfloat16 [32768, 2560], P(('dp', 'ctx')), parts along dimension 0
- key_grad: bfloat16 [32768, 512], P(('dp', 'ctx')), parts along dimension 0
- value_grad: bfloat16 [32768, 512], P(('dp', 'ctx')), parts along dimension 0
The draws below stay inside these ranges and needn't reach their ends.
There are 8 independent parts, one for each index of `dp`. The reference program is written for one: setup_inputs(seed, part) draws one part's arguments, and reference() takes and returns one part's arrays. A program takes and returns all parts, laid end to end along the dimension named above; each array names one. Nothing has to cross between parts.
Inputs may be any that keep to these rules, and one draw needn't show every extreme that they name: `subset_sizes`: they sum to 32, and the largest equals 4. `ffn_order`: each row holds every number once. `attn_order`: each row holds every number once.
All inputs are finite; a program needn't handle non-finite values.
Results may differ from the reference program's by a relative error of at most 0.028.
Values may be sent and summed in bfloat16 or wider, within the bound.
A program may use at most 64 MiB of HBM per device.

```python
import math
import jax
import jax.numpy as jnp
import numpy as np
from jax import lax

DEVICE_TOKENS = 128
HQ = 20
KEY_VALUE_HEADS = 4
HEAD_SIZE = 128
SUB = 4
QUERY_PER_KEY = 5
ROWS_PEER = 4
NTR = 16
GROUP_TOKENS = 4096
N_CTX = 32


def draw_attention_query_rows(key, part):
    key = jax.random.fold_in(key, 1)
    sampled_values = jnp.clip(jax.random.normal(key, (GROUP_TOKENS, KEY_VALUE_HEADS, QUERY_PER_KEY, HEAD_SIZE), jnp.float32), -4.0, 4.0)
    return sampled_values.reshape(GROUP_TOKENS, HQ * HEAD_SIZE).astype(jnp.bfloat16)


def draw_key_rows(key, part):
    key = jax.random.fold_in(key, 2)
    sampled_values = jnp.clip(jax.random.normal(key, (GROUP_TOKENS, KEY_VALUE_HEADS, HEAD_SIZE), jnp.float32), -4.0, 4.0)
    return sampled_values.reshape(GROUP_TOKENS, KEY_VALUE_HEADS * HEAD_SIZE).astype(jnp.bfloat16)


def shard_levels(own_key, extent, split, smallest, top_value):
    level = 1.0
    for position, parts in split:
        draws = jax.random.uniform(jax.random.fold_in(jax.random.fold_in(own_key, 6), position), (parts,), jnp.float32, smallest / len(split), top_value / len(split))
        level = level * jnp.repeat(jnp.exp(draws), extent[position] // parts).reshape((-1,) + (1,) * (len(extent) - 1 - position))
    return level


def split_up(count, total, reach, slope):
    weights = [(1 << 20) // math.isqrt(rank ** slope) + 1 for rank in range(2, count + 1)]
    spare, holding = total - reach - (count - 1), [1] * (count - 1)
    while spare > 0:
        candidates = [i for i in range(count - 1) if holding[i] < reach]
        whole, remaining = sum([weights[i] for i in candidates]), spare
        for i in candidates:
            addition = min(reach - holding[i], max(1, remaining * weights[i] // whole), spare)
            holding[i] = holding[i] + addition
            spare = spare - addition
    return np.array([reach] + holding)


def uneven_parts(key, count, total, reach, skew):
    if count == 2:
        one = jax.random.randint(key, (), max(1, total - reach), min(reach, total - 1) + 1)
        return jnp.stack([one, total - one])
    lengths = jnp.asarray(split_up(count, total, reach, skew), jnp.int32)
    couples = (count - 1) // 2
    giver, receiver = lengths[1:1 + 2 * couples:2], lengths[2:2 + 2 * couples:2]
    room = jnp.minimum(giver - 1, reach - receiver)
    shifted = jax.random.randint(jax.random.fold_in(key, 1), (couples,), 0, 1 << 20) % (room + 1)
    lengths = lengths.at[1:1 + 2 * couples:2].set(giver - shifted).at[2:2 + 2 * couples:2].set(receiver + shifted)
    return lengths[jax.random.permutation(jax.random.fold_in(key, 2), count)]


def gaussian(own_key, extent, spread, reach, shards=(), kind=jnp.bfloat16):
    drawn = jax.random.normal(own_key, extent, jnp.float32) * spread
    if len(shards) > 0:
        drawn = shard_levels(own_key, extent, shards, -0.22, 0.18) * drawn
    return jnp.clip(drawn, min=-reach, max=reach).astype(kind)


def setup_inputs(seed: int = 0, part: int = 0) -> dict:
    arg_keys = jax.random.split(jax.random.key(seed), 8)
    part_splits = jax.random.split(jax.random.fold_in(arg_keys[7], part), 8)
    return {
        "attention_query_rows": draw_attention_query_rows(jax.random.fold_in(jax.random.fold_in(arg_keys[7], part), 71), part),
        "key_rows": draw_key_rows(jax.random.fold_in(jax.random.fold_in(arg_keys[7], part), 71), part),
        "attention_value_rows": gaussian(part_splits[2], (GROUP_TOKENS, KEY_VALUE_HEADS * HEAD_SIZE), 1.0, 6.0, ((0, 32),)),
        "out_grad": gaussian(part_splits[3], (GROUP_TOKENS, HQ * HEAD_SIZE), 1.0, 6.0, ((0, 32),)),
        "subset_sizes": uneven_parts(part_splits[4], NTR, N_CTX, SUB, 2).astype(jnp.int32),
        "ffn_order": jax.vmap(lambda own: jax.random.permutation(own, DEVICE_TOKENS))(jax.random.split(part_splits[5], N_CTX)).reshape((N_CTX, DEVICE_TOKENS)).astype(jnp.int32),
        "attn_order": jax.vmap(lambda own: jax.random.permutation(own, DEVICE_TOKENS))(jax.random.split(part_splits[6], N_CTX)).reshape((N_CTX, DEVICE_TOKENS)).astype(jnp.int32),
    }


def device_meta(subset_sizes, device, device_count):
    end_points = jnp.cumsum(subset_sizes)
    trace_count = subset_sizes.shape[0]
    trace_id = lax.optimization_barrier(jnp.sum((end_points[None, :] <= device[:, None]).astype(jnp.int32), axis=1))
    one_hot = (jnp.arange(trace_count, dtype=jnp.int32)[None, :] == trace_id[:, None]).astype(jnp.int32)
    span_size = lax.optimization_barrier(jnp.sum(one_hot * subset_sizes[None, :], axis=1))
    first_device = lax.optimization_barrier(jnp.sum(one_hot * (end_points - subset_sizes)[None, :], axis=1))
    in_range = (device >= 0) & (device < device_count)
    return (jnp.where(in_range, trace_id, -1), device - first_device, span_size)

def row_positions(member, span_size, row_count):
    half_rows = row_count // 2
    local_rows = jnp.arange(row_count, dtype=jnp.int32)[None, :]
    first_half = member[:, None] * half_rows + local_rows
    second_half = (2 * span_size[:, None] - 1 - member[:, None]) * half_rows + local_rows - half_rows
    return jnp.where(local_rows < half_rows, first_half, second_half)

def row_maps(ffn_order, attn_order):
    column = jnp.arange(DEVICE_TOKENS, dtype=jnp.int32)
    target = column // ROWS_PEER
    slot_index = column % ROWS_PEER
    source = jnp.arange(N_CTX, dtype=jnp.int32)[:, None]
    ffn_index = source * DEVICE_TOKENS + ffn_order
    att_local = attn_order[target[None, :], source * ROWS_PEER + slot_index[None, :]]
    att_index = target[None, :] * DEVICE_TOKENS + att_local
    return (ffn_index.reshape(-1).astype(jnp.int32), att_index.reshape(-1).astype(jnp.int32))

def reference(attention_query_rows, key_rows, attention_value_rows, out_grad, subset_sizes, ffn_order, attn_order):
    distance = SUB - 1
    rows_of_span = (2 * distance + 1) * DEVICE_TOKENS
    score_scale = 1.0 / math.sqrt(HEAD_SIZE)
    key_value_width = KEY_VALUE_HEADS * HEAD_SIZE
    devices = jnp.arange(-distance, N_CTX + distance, dtype=jnp.int32)
    trace_ids, members, spans = device_meta(subset_sizes, devices, N_CTX)
    key_trace = jnp.repeat(trace_ids, DEVICE_TOKENS)
    key_pos = row_positions(members, spans, DEVICE_TOKENS).reshape(-1)
    padding = ((distance * DEVICE_TOKENS, distance * DEVICE_TOKENS), (0, 0))
    key_padded = jnp.pad(key_rows, padding)
    value_padded = jnp.pad(attention_value_rows, padding)

    def window(device):
        leading_row = device * DEVICE_TOKENS
        heads_of_key = lax.dynamic_slice_in_dim(key_padded, leading_row, rows_of_span, 0).reshape(rows_of_span, KEY_VALUE_HEADS, HEAD_SIZE).astype(jnp.float32)
        heads_of_value = lax.dynamic_slice_in_dim(value_padded, leading_row, rows_of_span, 0).reshape(rows_of_span, KEY_VALUE_HEADS, HEAD_SIZE).astype(jnp.float32)
        heads_of_query = lax.dynamic_slice_in_dim(attention_query_rows, leading_row, DEVICE_TOKENS, 0).reshape(DEVICE_TOKENS, KEY_VALUE_HEADS, QUERY_PER_KEY, HEAD_SIZE).astype(jnp.float32)
        window_trace = lax.dynamic_slice_in_dim(key_trace, leading_row, rows_of_span, 0)
        window_pos = lax.dynamic_slice_in_dim(key_pos, leading_row, rows_of_span, 0)
        query_trace = lax.dynamic_index_in_dim(key_trace, leading_row + distance * DEVICE_TOKENS, 0, keepdims=False)
        query_pos = lax.dynamic_slice_in_dim(key_pos, leading_row + distance * DEVICE_TOKENS, DEVICE_TOKENS, 0)
        allowed = (window_trace[None, :] == query_trace) & (window_trace[None, :] >= 0) & (window_pos[None, :] <= query_pos[:, None])
        scores = jnp.einsum('qhgd,khd->hgqk', heads_of_query, heads_of_key) * score_scale
        scores = jnp.where(allowed[None, None], scores, -jnp.inf)
        row_top = lax.optimization_barrier(jnp.max(scores, axis=-1, keepdims=True))
        weights = jnp.exp(scores - row_top)
        prob = weights / lax.optimization_barrier(jnp.sum(weights, axis=-1, keepdims=True))
        prob_b = lax.optimization_barrier(prob.astype(jnp.bfloat16)).astype(jnp.float32)
        return (heads_of_query, heads_of_key, heads_of_value, prob, prob_b)

    def forward(device):
        pieces = window(device)
        mixed = jnp.einsum('hgqk,khd->qhgd', pieces[4], pieces[2])
        return mixed.reshape(DEVICE_TOKENS, HQ * HEAD_SIZE).astype(jnp.bfloat16)
    attention_apply = lax.map(forward, jnp.arange(N_CTX, dtype=jnp.int32)).reshape(GROUP_TOKENS, HQ * HEAD_SIZE)
    ffn_index, att_index = row_maps(ffn_order, attn_order)
    attn_out = jnp.zeros_like(attention_apply).at[ffn_index].set(attention_apply[att_index])
    attention_gradient = jnp.zeros_like(out_grad).at[att_index].set(out_grad[ffn_index])

    def backward(carry, device):
        heads_of_query, heads_of_key, heads_of_value, prob, prob_b = window(device)
        leading_row = device * DEVICE_TOKENS
        head_gradient = lax.dynamic_slice_in_dim(attention_gradient, leading_row, DEVICE_TOKENS, 0).reshape(DEVICE_TOKENS, KEY_VALUE_HEADS, QUERY_PER_KEY, HEAD_SIZE).astype(jnp.float32)
        output_heads = lax.dynamic_slice_in_dim(attention_apply, leading_row, DEVICE_TOKENS, 0).reshape(DEVICE_TOKENS, KEY_VALUE_HEADS, QUERY_PER_KEY, HEAD_SIZE).astype(jnp.float32)
        delta = lax.optimization_barrier(jnp.sum(head_gradient * output_heads, axis=-1))
        dprob = jnp.einsum('qhgd,khd->hgqk', head_gradient, heads_of_value)
        dscore = prob * (dprob - jnp.transpose(delta, (1, 2, 0))[..., None])
        dscore_b = lax.optimization_barrier(dscore.astype(jnp.bfloat16)).astype(jnp.float32)
        query_part = (jnp.einsum('hgqk,khd->qhgd', dscore_b, heads_of_key) * score_scale).reshape(DEVICE_TOKENS, HQ * HEAD_SIZE).astype(jnp.bfloat16)
        key_part = jnp.einsum('hgqk,qhgd->khd', dscore_b, heads_of_query) * score_scale
        value_part = jnp.einsum('hgqk,qhgd->khd', prob_b, head_gradient)
        term = jnp.concatenate([key_part.reshape(rows_of_span, key_value_width), value_part.reshape(rows_of_span, key_value_width)], axis=1)
        term = lax.optimization_barrier(term.astype(jnp.bfloat16)).astype(jnp.float32)
        earlier = lax.dynamic_slice_in_dim(carry, leading_row, rows_of_span, 0)
        carry = lax.dynamic_update_slice_in_dim(carry, earlier + term, leading_row, 0)
        return (carry, query_part)
    start_carry = jnp.zeros(((N_CTX + 2 * distance) * DEVICE_TOKENS, 2 * key_value_width), jnp.float32)
    grad_sums, query_grad = lax.scan(backward, start_carry, jnp.arange(N_CTX, dtype=jnp.int32))
    grad_sums = grad_sums[distance * DEVICE_TOKENS:distance * DEVICE_TOKENS + GROUP_TOKENS]
    key_grad = grad_sums[:, :key_value_width].astype(jnp.bfloat16)
    value_grad = grad_sums[:, key_value_width:].astype(jnp.bfloat16)
    return (attn_out, query_grad.reshape(GROUP_TOKENS, HQ * HEAD_SIZE), key_grad, value_grad)
```

```python
import math

import jax
import jax.numpy as jnp
from jax import lax
from jax.experimental import pallas as pl
from jax.experimental.pallas import tpu as pltpu
from jax.sharding import PartitionSpec as P

MESH = pl.DeviceIdType.MESH
D = 128
HALF = 64
KV = 4
GR = 5
N = 32
CHUNK = 16
ROWS = N * CHUNK
WIDE = GR * D
KEYS = 4 * D
NEG = -1e30
CHUNKS = ((0, GR),)
BF, F32 = jnp.bfloat16, jnp.float32


def dot(a, b, ca, cb):
    return lax.dot_general(a, b, (((ca,), (cb,)), ((), ())), preferred_element_type=F32)


def iota(shape, dim):
    return lax.broadcasted_iota(jnp.int32, shape, dim)


def picks(c, ul):
    return (ul == ((c >> 2) & 3) * D + (c >> 4) * 4 + (c & 3)).astype(BF)


def scatter_matrix(orders):
    pick = picks(iota((KV * D, ROWS), 1), iota((KV * D, ROWS), 0))
    row, c = iota((D, ROWS), 0), iota((D, ROWS), 1)
    target = dot(orders, pick, 1, 0) + (((c >> 2) & 3) * D).astype(F32)
    row = row.astype(F32)
    return jnp.concatenate([(target == row + float(t * D)).astype(BF) for t in range(KV)], axis=0)


def gather_matrix(orders):
    pick = picks(iota((ROWS, KV * D), 0), iota((ROWS, KV * D), 1))
    c, lane = iota((ROWS, D), 0), iota((ROWS, D), 1)
    target = dot(pick, orders, 1, 1) + (((c >> 2) & 3) * D).astype(F32)
    lane = lane.astype(F32)
    return jnp.concatenate([(target == lane + float(t * D)).astype(BF) for t in range(KV)], axis=1)


def heads(x, lo=0, hi=GR):
    return jnp.concatenate([x[:, a * D : (a + 1) * D] for a in range(lo, hi)], axis=0)


def kernel(
    q_hbm, k_hbm, v_hbm, g_hbm, sizes_hbm, ffn_hbm, att_hbm,
    rcv2, qg, grow, gup, gdn, p_out,
    sizes, ffn_ref, att_ref, qb, kvb, qst, kvw, kall, prob, gin, snd1, rcv1, snd2,
    m_att, mt_att, ott, dos, dsb, dqs, accw, gsend, bias, flag,
    in_sem, att_s, att_r, kv_s, kv_r, q_s, q_r, dq_s, dq_r, g_s, g_r,
    a1_s, a1_r, a2_s, a2_r,
):
    dp = lax.axis_index("dp")
    me = lax.axis_index("ctx")
    z, x = me >> 2, me & 3
    above, below = ((z + 1) & 7) * KV, ((z + 7) & 7) * KV
    scale = 1.0 / math.sqrt(D)

    def remote(src, dst, s, r, peer):
        return pltpu.make_async_remote_copy(
            src_ref=src, dst_ref=dst, send_sem=s, recv_sem=r,
            device_id=(dp, peer), device_id_type=MESH,
        )

    def lanes(i, width):
        return pl.ds(pl.multiple_of(i * width, D), width)

    barrier = pltpu.get_barrier_semaphore()

    def greet(i, _):
        pl.semaphore_signal(
            barrier, inc=1, device_id=(dp, lax.rem(me + i, N)), device_id_type=MESH
        )
        return 0

    lax.fori_loop(1, N, greet, 0)

    local = [
        pltpu.make_async_copy(ffn_hbm, ffn_ref, in_sem.at[0]),
        pltpu.make_async_copy(g_hbm, gin, in_sem.at[1]),
        pltpu.make_async_copy(att_hbm, att_ref.at[x], in_sem.at[2]),
        pltpu.make_async_copy(sizes_hbm, sizes, in_sem.at[3]),
    ]
    for g in range(KV):
        cols = slice(g * D, (g + 1) * D)
        local += [
            pltpu.make_async_copy(k_hbm.at[:, cols], kvb.at[g, :, 0:D], in_sem.at[4 + 3 * g]),
            pltpu.make_async_copy(v_hbm.at[:, cols], kvb.at[g, :, D:], in_sem.at[5 + 3 * g]),
            pltpu.make_async_copy(
                q_hbm.at[:, g * WIDE : (g + 1) * WIDE], qb.at[g], in_sem.at[6 + 3 * g]
            ),
        ]
    for c in local:
        c.start()

    local[0].wait()
    order = ffn_ref[...].astype(F32)
    p_ffn = (order == iota((D, D), 0).astype(F32)).astype(BF)
    p_out[...] = p_ffn
    gather_ffn = p_ffn.T
    local[1].wait()
    for g in range(KV):
        snd1[g * D : (g + 1) * D, :] = dot(
            gather_ffn, gin[:, g * WIDE : (g + 1) * WIDE], 1, 0
        ).astype(BF)

    for c in local[2:]:
        c.wait()
    kvw[4 + x] = kvb[x]
    qst[x] = qb[x]

    pl.semaphore_wait(barrier, N - 1)

    def order_copy(i):
        return remote(att_ref.at[x], att_ref.at[x], att_s.at[i], att_r.at[i], z * KV + ((x + i) & 3))

    def order_arrived(i):
        u = (x + 4 - i) & 3
        return remote(att_ref.at[u], att_ref.at[u], att_s.at[i], att_r.at[i], me ^ 1)

    for i in (1, 2, 3):
        order_copy(i).start()

    def kv_copy(i, what):
        g = (x + i) & 3
        s = kv_s.at[i, what]
        if what == 0:
            return remote(kvb.at[g], kvw.at[4 + x], s, kv_r.at[4 + x], z * KV + g)
        if what == 1:
            return remote(kvb.at[g], kvw.at[8 + x], s, kv_r.at[8 + x], below + g)
        return remote(kvb.at[g, 0:HALF], kvw.at[x, 0:HALF], s, kv_r.at[x], above + g)

    def kv_all(action):
        for i in (2, 1, 3):
            action(kv_copy(i, 0))
        for i in (2, 1, 3, 0):

            @pl.when(x <= 2)
            def _():
                action(kv_copy(i, 1))

            @pl.when(x >= 1)
            def _():
                action(kv_copy(i, 2))

    kv_all(lambda c: c.start())

    def q_copy(i):
        g = (x + i) & 3
        return remote(qb.at[g], qst.at[x], q_s.at[i], q_r.at[x], z * KV + g)

    for i in (2, 1, 3):
        q_copy(i).start()

    def rows_at(i):
        return pl.ds(pl.multiple_of(i * CHUNK, CHUNK), CHUNK)

    def token_row(peer):
        return pl.ds(pl.multiple_of((peer & 3) * D + (peer >> 2) * CHUNK, CHUNK), CHUNK)

    def send1(i, _):
        peer = lax.rem(me + i, N)
        remote(snd1.at[token_row(peer)], rcv1.at[rows_at(me)], a1_s, a1_r, peer).start()
        return 0

    lax.fori_loop(1, N, send1, 0)
    rcv1[rows_at(me), :] = snd1[token_row(me), :]

    def whole(src, dst, s, r):
        n = ROWS - CHUNK
        return remote(src.at[:n], dst.at[:n], s, r, lax.rem(me + 1, N))

    kk, qq = iota((D, D), 0), iota((D, D), 1)
    for u in range(KV):
        d = z * KV + u
        first, end, start = 0, 0, 0
        for t in range(16):
            stop = start + sizes[t]
            inside = (start <= d) & (d < stop)
            first = jnp.where(inside, start, first)
            end = jnp.where(inside, stop, end)
            start = stop
        bias[u, 0:D, :] = jnp.where(kk <= qq, 0.0, NEG)
        for r in (1, 2, 3):
            flag[u * KV + r] = jnp.where(d + r < end, 1, 0)
            later = jnp.where(d + r < end, 0.0, NEG)
            earlier = jnp.where(d + r - 4 >= first, 0.0, NEG)
            bias[u, r * D : (r + 1) * D, :] = jnp.maximum(
                jnp.where(qq >= HALF, later, NEG), jnp.where(kk < HALF, earlier, NEG)
            )
    accw[...] = jnp.zeros_like(accw)

    for i in (1, 2, 3):
        order_arrived(i).wait_recv()
    orders = jnp.concatenate([att_ref[u] for u in range(KV)], axis=1)
    orders = jnp.broadcast_to(orders.astype(F32).astype(BF), (D, KV * D))
    m_att[...] = scatter_matrix(orders)
    mt_att[...] = gather_matrix(orders)

    for e in range(1, 11):
        rows = slice(0, HALF) if e < 4 else slice(0, D)
        c = remote(kvb.at[0, rows], kvw.at[e, rows], kv_s.at[0, 0], kv_r.at[e], me ^ 1)
        if 4 <= e < 8:
            pl.when(x != e - 4)(c.wait_recv)
        else:
            c.wait_recv()

    def forward(i, _):
        u = (x + i) & 3

        @pl.when(i > 0)
        def _():
            remote(qb.at[0], qst.at[u], q_s.at[0], q_r.at[u], me ^ 1).wait_recv()

        kall[u, 0:D, :] = kvw[4 + u]
        for r in (1, 2, 3):
            kall[u, r * D : r * D + HALF, :] = jnp.where(
                flag[u * KV + r] > 0, kvw[4 + u + r, 0:HALF, :], kvw[u + r, 0:HALF, :]
            )
            kall[u, r * D + HALF : (r + 1) * D, :] = kvw[4 + u + r, HALF:D, :]
        keys, values = kall[u, :, 0:D], kall[u, :, D : 2 * D]
        values_t = values.T
        c = scale * math.log2(math.e)
        for lo, hi in CHUNKS:
            s = dot(keys, heads(qst[u], lo, hi), 1, 1)
            s = s + jnp.concatenate([bias[u]] * (hi - lo), axis=1)
            top = jnp.max(s, axis=0, keepdims=True)
            p = jnp.exp2(s * c - top * c)
            p = (p * (1.0 / jnp.sum(p, axis=0, keepdims=True))).astype(BF)
            prob[u, :, lo * D : hi * D] = p
            o = dot(values_t, p, 1, 0).astype(BF)
            for a in range(lo, hi):
                ott[a * D : (a + 1) * D, lanes(u, D)] = o[:, (a - lo) * D : (a - lo + 1) * D]
        return 0

    lax.fori_loop(0, KV, forward, 0)

    snd2[...] = dot(mt_att[...], ott[...], 1, 1).astype(BF)

    def send2(i, _):
        peer = lax.rem(me + i, N)
        remote(snd2.at[rows_at(peer)], rcv2.at[token_row(me)], a2_s, a2_r, peer).start()
        return 0

    lax.fori_loop(1, N, send2, 0)
    rcv2[token_row(me), :] = snd2[rows_at(me), :]

    whole(snd1, rcv1, a1_s, a1_r).wait_recv()
    for u in range(KV):
        dos[u] = dot(m_att[u * D : (u + 1) * D, :], rcv1[...], 1, 0).astype(BF)

    def dq_copy(u):
        return remote(dqs.at[u], qg.at[x], dq_s.at[u], dq_r.at[x], z * KV + u)

    def backward(i, _):
        u = (x + 1 + i) & 3
        keys, values = kall[u, :, 0:D], kall[u, :, D : 2 * D]
        keys_t = keys.T
        for lo, hi in CHUNKS:
            dp_t = dot(values, heads(dos[u], lo, hi), 1, 1)
            pf = prob[u, :, lo * D : hi * D].astype(F32)
            t = pf * dp_t
            ds = (t - pf * jnp.sum(t, axis=0, keepdims=True)).astype(BF)
            dsb[:, lo * D : hi * D] = ds
            dq = dot(keys_t, ds, 1, 0) * scale
            for a in range(lo, hi):
                dqs[u, :, a * D : (a + 1) * D] = (
                    dq[:, (a - lo) * D : (a - lo + 1) * D].T.astype(BF)
                )

        @pl.when(i < 3)
        def _():
            dq_copy(u).start()

        kpart = dot(dsb[...], heads(qst[u]), 1, 0) * scale
        vpart = dot(prob[u], heads(dos[u]), 1, 0)
        part = jnp.concatenate([kpart, vpart], axis=1)
        accw[4 + u] += part[0:D]
        for r in (1, 2, 3):
            later = flag[u * KV + r] > 0
            accw[4 + u + r] += jnp.where(later, part[r * D : (r + 1) * D], 0.0)
            accw[u + r, 0:HALF, :] += jnp.where(later, 0.0, part[r * D : r * D + HALF])
        return 0

    lax.fori_loop(0, KV, backward, 0)
    qg[x] = dqs[x]

    for e in range(1, 11):
        gsend[e] = accw[e].astype(BF)

    def g_copy(e):
        g = e & 3
        if e < 4:
            return remote(gsend.at[e, 0:HALF], gdn.at[x], g_s.at[e], g_r.at[0, x], below + g)
        if e < 8:
            return remote(gsend.at[e], grow.at[x], g_s.at[e], g_r.at[1, x], z * KV + g)
        return remote(gsend.at[e], gup.at[x], g_s.at[e], g_r.at[2, x], above + g)

    for e in (8, 9, 10, 1, 2, 3):
        g_copy(e).start()
    for e in range(4, 8):
        pl.when(x != e - 4)(g_copy(e).start)
    grow[x] = gsend[4 + x]

    whole(snd2, rcv2, a2_s, a2_r).wait_recv()
    for g in range(KV):
        pl.when(x != g)(
            remote(gsend.at[4], grow.at[g], g_s.at[0], g_r.at[1, g], me ^ 1).wait_recv
        )
        pl.when(x <= 2)(remote(gsend.at[4], gup.at[g], g_s.at[0], g_r.at[2, g], me ^ 1).wait_recv)
        pl.when(x >= 1)(
            remote(gsend.at[4, 0:HALF], gdn.at[g], g_s.at[0], g_r.at[0, g], me ^ 1).wait_recv
        )

    for i in (1, 2, 3):
        order_copy(i).wait_send()
        q_copy(i).wait_send()
    kv_all(lambda c: c.wait_send())
    whole(snd1, rcv1, a1_s, a1_r).wait_send()
    whole(snd2, rcv2, a2_s, a2_r).wait_send()
    for e in (8, 9, 10, 1, 2, 3):
        g_copy(e).wait_send()
    for u in range(KV):

        @pl.when(x != u)
        def _():
            g_copy(4 + u).wait_send()
            dq_copy(u).wait_send()
            remote(dqs.at[u], qg.at[u], dq_s.at[u], dq_r.at[u], me ^ 1).wait_recv()


def finish(
    got, qg, grow, gup, gdn, p_ffn,
    out_hbm, qg_hbm, kg_hbm, vg_hbm,
    out_v, kg_v, vg_v, sem,
):
    x = lax.axis_index("ctx") & 3
    outs = []

    def send(src, dst):
        outs.append(pltpu.make_async_copy(src, dst, sem.at[len(outs)]))
        outs[-1].start()

    for g in range(KV):
        send(qg.at[g], qg_hbm.at[:, g * WIDE : (g + 1) * WIDE])
    for g in range(KV):
        total = grow[g].astype(F32) + jnp.where(x <= 2, gup[g].astype(F32), 0.0)
        low = total[0:HALF] + jnp.where(x >= 1, gdn[g].astype(F32), 0.0)
        high = total[HALF:D]
        cols = slice(g * D, (g + 1) * D)
        for ref, lane in ((kg_v, 0), (vg_v, D)):
            ref[0:HALF, cols] = low[:, lane : lane + D].astype(BF)
            ref[HALF:D, cols] = high[:, lane : lane + D].astype(BF)
    send(kg_v, kg_hbm)
    send(vg_v, vg_hbm)
    for g in range(KV):
        cols = slice(g * WIDE, (g + 1) * WIDE)
        out_v[:, cols] = dot(p_ffn[...], got[g * D : (g + 1) * D, :], 1, 0).astype(BF)
        send(out_v.at[:, cols], out_hbm.at[:, cols])
    for c in outs:
        c.wait()


def body(q, k, v, g, sizes, ffn_order, attn_order):
    hbm = pl.BlockSpec(memory_space=pltpu.HBM)
    vmem = pl.BlockSpec(memory_space=pltpu.VMEM)
    dma = pltpu.SemaphoreType.DMA
    vm = pltpu.VMEM
    got, qg, row, up, down, p_ffn = pl.pallas_call(
        kernel,
        out_shape=(
            vm((ROWS, WIDE), BF),
            vm((KV, D, WIDE), BF),
            vm((KV, D, 2 * D), BF),
            vm((KV, D, 2 * D), BF),
            vm((KV, HALF, 2 * D), BF),
            vm((D, D), BF),
        ),
        in_specs=[hbm] * 7,
        out_specs=(vmem,) * 6,
        scratch_shapes=[
            pltpu.SMEM((16,), jnp.int32),
            vm((1, D), jnp.int32),
            vm((KV, 1, D), jnp.int32),
            vm((KV, D, WIDE), BF),
            vm((KV, D, 2 * D), BF),
            vm((KV, D, WIDE), BF),
            vm((12, D, 2 * D), BF),
            vm((KV, KEYS, 2 * D), BF),
            vm((KV, KEYS, WIDE), BF),
            vm((D, KV * WIDE), BF),
            vm((ROWS, WIDE), BF),
            vm((ROWS, WIDE), BF),
            vm((ROWS, WIDE), BF),
            vm((KV * D, ROWS), BF),
            vm((ROWS, KV * D), BF),
            vm((WIDE, KV * D), BF),
            vm((KV, D, WIDE), BF),
            vm((KEYS, WIDE), BF),
            vm((KV, D, WIDE), BF),
            vm((12, D, 2 * D), F32),
            vm((12, D, 2 * D), BF),
            vm((KV, KEYS, D), F32),
            pltpu.SMEM((KV * KV,), jnp.int32),
            dma((16,)),
            dma((4,)),
            dma((4,)),
            dma((4, 3)),
            dma((12,)),
            dma((4,)),
            dma((4,)),
            dma((4,)),
            dma((4,)),
            dma((12,)),
            dma((3, 4)),
            dma,
            dma,
            dma,
            dma,
        ],
        compiler_params=pltpu.CompilerParams(
            collective_id=0, has_side_effects=True, vmem_limit_bytes=56 * 1024 * 1024
        ),
    )(q, k, v, g, sizes, ffn_order, attn_order)
    return pl.pallas_call(
        finish,
        out_shape=(
            jax.ShapeDtypeStruct((D, KV * WIDE), BF),
            jax.ShapeDtypeStruct((D, KV * WIDE), BF),
            jax.ShapeDtypeStruct((D, KV * D), BF),
            jax.ShapeDtypeStruct((D, KV * D), BF),
        ),
        in_specs=[vmem] * 6,
        out_specs=(hbm,) * 4,
        scratch_shapes=[
            vm((D, KV * WIDE), BF),
            vm((D, KV * D), BF),
            vm((D, KV * D), BF),
            dma((10,)),
        ],
        compiler_params=pltpu.CompilerParams(vmem_limit_bytes=8 * 1024 * 1024),
    )(got, qg, row, up, down, p_ffn)


def solution(mesh):
    rows = P(("dp", "ctx"), None)
    return jax.shard_map(
        body,
        mesh=mesh,
        in_specs=(rows, rows, rows, rows, P("dp"), rows, rows),
        out_specs=(rows,) * 4,
        check_vma=False,
    )
```

```python
import math

import jax
import jax.numpy as jnp
from jax import lax
from jax.experimental import pallas as pl
from jax.experimental.pallas import tpu as pltpu
from jax.sharding import PartitionSpec as P

MESH = pl.DeviceIdType.MESH
D = 128
HALF = 64
KV = 4
GR = 5
N = 32
CHUNK = 16
ROWS = N * CHUNK
WIDE = GR * D
KEYS = 4 * D
NEG = -1e30
STEP = 32
BF, F32 = jnp.bfloat16, jnp.float32


def dot(a, b, ca, cb):
    return lax.dot_general(a, b, (((ca,), (cb,)), ((), ())), preferred_element_type=F32)


def iota(shape, dim):
    return lax.broadcasted_iota(jnp.int32, shape, dim)


def picks(c, ul):
    return (ul == ((c >> 2) & 3) * D + (c >> 4) * 4 + (c & 3)).astype(BF)


def scatter_matrix(orders):
    pick = picks(iota((KV * D, ROWS), 1), iota((KV * D, ROWS), 0))
    row, c = iota((D, ROWS), 0), iota((D, ROWS), 1)
    target = dot(orders, pick, 1, 0) + (((c >> 2) & 3) * D).astype(F32)
    row = row.astype(F32)
    return jnp.concatenate([(target == row + float(t * D)).astype(BF) for t in range(KV)], axis=0)


def gather_matrix(orders):
    pick = picks(iota((ROWS, KV * D), 0), iota((ROWS, KV * D), 1))
    c, lane = iota((ROWS, D), 0), iota((ROWS, D), 1)
    target = dot(pick, orders, 1, 1) + (((c >> 2) & 3) * D).astype(F32)
    lane = lane.astype(F32)
    return jnp.concatenate([(target == lane + float(t * D)).astype(BF) for t in range(KV)], axis=1)


def heads(x):
    return jnp.concatenate([x[:, a * D : (a + 1) * D] for a in range(GR)], axis=0)


def kernel(
    q_hbm, k_hbm, v_hbm, g_hbm, sizes_hbm, ffn_hbm, att_hbm,
    rcv2, qg, grow, gup, gdn, p_out,
    sizes, ffn_ref, att_ref, qb, kvb, qst, kvw, kall, prob, gin, snd1, rcv1, snd2,
    m_att, mt_att, ott, dos, sc, dsb, dqs, accw, gsend, bias, invs, flag,
    in_sem, att_s, att_r, kv_s, kv_r, q_s, q_r, dq_s, dq_r, g_s, g_r,
    a1_s, a1_r, a2_s, a2_r,
):
    dp = lax.axis_index("dp")
    me = lax.axis_index("ctx")
    z, x = me >> 2, me & 3
    above, below = ((z + 1) & 7) * KV, ((z + 7) & 7) * KV
    scale = 1.0 / math.sqrt(D)

    def remote(src, dst, s, r, peer):
        return pltpu.make_async_remote_copy(
            src_ref=src, dst_ref=dst, send_sem=s, recv_sem=r,
            device_id=(dp, peer), device_id_type=MESH,
        )

    def lanes(i, width):
        return pl.ds(pl.multiple_of(i * width, D), width)

    barrier = pltpu.get_barrier_semaphore()

    def greet(i, _):
        pl.semaphore_signal(
            barrier, inc=1, device_id=(dp, lax.rem(me + i, N)), device_id_type=MESH
        )
        return 0

    lax.fori_loop(1, N, greet, 0)

    local = [
        pltpu.make_async_copy(ffn_hbm, ffn_ref, in_sem.at[0]),
        pltpu.make_async_copy(g_hbm, gin, in_sem.at[1]),
        pltpu.make_async_copy(att_hbm, att_ref.at[x], in_sem.at[2]),
        pltpu.make_async_copy(sizes_hbm, sizes, in_sem.at[3]),
    ]
    for g in range(KV):
        cols = slice(g * D, (g + 1) * D)
        local += [
            pltpu.make_async_copy(k_hbm.at[:, cols], kvb.at[g, :, 0:D], in_sem.at[4 + 3 * g]),
            pltpu.make_async_copy(v_hbm.at[:, cols], kvb.at[g, :, D:], in_sem.at[5 + 3 * g]),
            pltpu.make_async_copy(
                q_hbm.at[:, g * WIDE : (g + 1) * WIDE], qb.at[g], in_sem.at[6 + 3 * g]
            ),
        ]
    for c in local[4:] + local[:4]:
        c.start()

    for c in local[2:]:
        c.wait()
    kvw[4 + x] = kvb[x]
    qst[x] = qb[x]

    pl.semaphore_wait(barrier, N - 1)

    def order_copy(i):
        return remote(att_ref.at[x], att_ref.at[x], att_s.at[i], att_r.at[i], z * KV + ((x + i) & 3))

    def order_arrived(i):
        u = (x + 4 - i) & 3
        return remote(att_ref.at[u], att_ref.at[u], att_s.at[i], att_r.at[i], me ^ 1)

    for i in (1, 2, 3):
        order_copy(i).start()

    def kv_copy(i, what):
        g = (x + i) & 3
        s = kv_s.at[i, what]
        if what == 0:
            return remote(kvb.at[g], kvw.at[4 + x], s, kv_r.at[4 + x], z * KV + g)
        if what == 1:
            return remote(kvb.at[g], kvw.at[8 + x], s, kv_r.at[8 + x], below + g)
        return remote(kvb.at[g, 0:HALF], kvw.at[x, 0:HALF], s, kv_r.at[x], above + g)

    def kv_all(action):
        for i in (2, 1, 3):
            action(kv_copy(i, 0))
        for i in (2, 1, 3, 0):

            @pl.when(x <= 2)
            def _():
                action(kv_copy(i, 1))

            @pl.when(x >= 1)
            def _():
                action(kv_copy(i, 2))

    kv_all(lambda c: c.start())

    def q_copy(i):
        g = (x + i) & 3
        return remote(qb.at[g], qst.at[x], q_s.at[i], q_r.at[x], z * KV + g)

    for i in (2, 1, 3):
        q_copy(i).start()

    local[0].wait()
    order = ffn_ref[...].astype(F32)
    p_ffn = (order == iota((D, D), 0).astype(F32)).astype(BF)
    p_out[...] = p_ffn
    gather_ffn = p_ffn.T
    local[1].wait()
    packed = dot(gather_ffn, gin[...], 1, 0).astype(BF)
    for g in range(KV):
        snd1[g * D : (g + 1) * D, :] = packed[:, g * WIDE : (g + 1) * WIDE]

    def rows_at(i):
        return pl.ds(pl.multiple_of(i * CHUNK, CHUNK), CHUNK)

    def token_row(peer):
        return pl.ds(pl.multiple_of((peer & 3) * D + (peer >> 2) * CHUNK, CHUNK), CHUNK)

    def send1(i, _):
        peer = lax.rem(me + i, N)
        remote(snd1.at[token_row(peer)], rcv1.at[rows_at(me)], a1_s, a1_r, peer).start()
        return 0

    lax.fori_loop(1, N, send1, 0)
    rcv1[rows_at(me), :] = snd1[token_row(me), :]

    def whole(src, dst, s, r):
        n = ROWS - CHUNK
        return remote(src.at[:n], dst.at[:n], s, r, lax.rem(me + 1, N))

    kk, qq = iota((D, D), 0), iota((D, D), 1)
    for u in range(KV):
        d = z * KV + u
        first, end, start = 0, 0, 0
        for t in range(16):
            stop = start + sizes[t]
            inside = (start <= d) & (d < stop)
            first = jnp.where(inside, start, first)
            end = jnp.where(inside, stop, end)
            start = stop
        bias[u, 0:D, :] = jnp.where(kk <= qq, 0.0, NEG)
        for r in (1, 2, 3):
            flag[u * KV + r] = jnp.where(d + r < end, 1, 0)
            later = jnp.where(d + r < end, 0.0, NEG)
            earlier = jnp.where(d + r - 4 >= first, 0.0, NEG)
            bias[u, r * D : (r + 1) * D, :] = jnp.maximum(
                jnp.where(qq >= HALF, later, NEG), jnp.where(kk < HALF, earlier, NEG)
            )
    accw[...] = jnp.zeros_like(accw)
    invs[...] = jnp.zeros_like(invs)

    for i in (1, 2, 3):
        order_arrived(i).wait_recv()
    orders = jnp.concatenate([att_ref[u] for u in range(KV)], axis=1)
    orders = jnp.broadcast_to(orders.astype(F32).astype(BF), (D, KV * D))
    m_att[...] = scatter_matrix(orders)
    mt_att[...] = gather_matrix(orders)

    for e in range(1, 11):
        rows = slice(0, HALF) if e < 4 else slice(0, D)
        c = remote(kvb.at[0, rows], kvw.at[e, rows], kv_s.at[0, 0], kv_r.at[e], me ^ 1)
        if 4 <= e < 8:
            pl.when(x != e - 4)(c.wait_recv)
        else:
            c.wait_recv()

    def forward(i, _):
        u = (x + i) & 3

        @pl.when(i > 0)
        def _():
            remote(qb.at[0], qst.at[u], q_s.at[0], q_r.at[u], me ^ 1).wait_recv()

        kall[u, 0:D, :] = kvw[4 + u]
        for r in (1, 2, 3):
            kall[u, r * D : r * D + HALF, :] = jnp.where(
                flag[u * KV + r] > 0, kvw[4 + u + r, 0:HALF, :], kvw[u + r, 0:HALF, :]
            )
            kall[u, r * D + HALF : (r + 1) * D, :] = kvw[4 + u + r, HALF:D, :]
        keys, values = kall[u, :, 0:D], kall[u, :, D : 2 * D]
        sc[...] = dot(keys, heads(qst[u]), 1, 1)

        def masked(b):
            rows = pl.ds(pl.multiple_of(b * STEP, STEP), STEP)
            return sc[rows, :] + jnp.concatenate([bias[u, rows, :]] * GR, axis=1)

        def largest(b, top):
            return jnp.maximum(top, jnp.max(masked(b).reshape(STEP // 8, 8, WIDE), axis=0))

        top = lax.fori_loop(0, KEYS // STEP, largest, jnp.full((8, WIDE), NEG, F32))
        top = jnp.max(top, axis=0, keepdims=True)

        def weigh(b, total):
            p = jnp.exp2((masked(b) - top) * (scale * math.log2(math.e)))
            prob[u, pl.ds(pl.multiple_of(b * STEP, STEP), STEP), :] = p.astype(BF)
            return total + jnp.sum(p.reshape(STEP // 8, 8, WIDE), axis=0)

        total = lax.fori_loop(0, KEYS // STEP, weigh, jnp.zeros((8, WIDE), F32))
        inv = 1.0 / jnp.sum(total, axis=0, keepdims=True)
        o = (dot(values.T, prob[u], 1, 0) * inv).astype(BF)
        for a in range(GR):
            cols = slice(a * D, (a + 1) * D)
            ott[cols, lanes(u, D)] = o[:, cols]
            invs[u, a : a + 1, :] = inv[:, cols]
        return 0

    lax.fori_loop(0, KV, forward, 0)

    snd2[...] = dot(mt_att[...], ott[...], 1, 1).astype(BF)

    def send2(i, _):
        peer = lax.rem(me + i, N)
        remote(snd2.at[rows_at(peer)], rcv2.at[token_row(me)], a2_s, a2_r, peer).start()
        return 0

    lax.fori_loop(1, N, send2, 0)
    rcv2[token_row(me), :] = snd2[rows_at(me), :]

    whole(snd1, rcv1, a1_s, a1_r).wait_recv()
    for u in range(KV):
        up = dot(m_att[u * D : (u + 1) * D, :], rcv1[...], 1, 0)
        inv = invs[u].T
        for a in range(GR):
            cols = slice(a * D, (a + 1) * D)
            dos[u, :, cols] = (up[:, cols] * inv[:, a : a + 1]).astype(BF)

    def dq_copy(u):
        return remote(dqs.at[u], qg.at[x], dq_s.at[u], dq_r.at[x], z * KV + u)

    def backward(i, _):
        u = (x + 1 + i) & 3
        keys, values = kall[u, :, 0:D], kall[u, :, D : 2 * D]
        sc[...] = dot(values, heads(dos[u]), 1, 1)

        def blocks(b):
            rows = pl.ds(pl.multiple_of(b * STEP, STEP), STEP)
            return prob[u, rows, :].astype(F32), sc[rows, :]

        def add(b, total):
            p, dp_t = blocks(b)
            return total + jnp.sum((p * dp_t).reshape(STEP // 8, 8, WIDE), axis=0)

        total = lax.fori_loop(0, KEYS // STEP, add, jnp.zeros((8, WIDE), F32))
        inv = jnp.concatenate([invs[u, a : a + 1, :] for a in range(GR)], axis=1)
        delta = jnp.sum(total, axis=0, keepdims=True) * inv

        def score(b, _):
            p, dp_t = blocks(b)
            dsb[pl.ds(pl.multiple_of(b * STEP, STEP), STEP), :] = (p * (dp_t - delta)).astype(BF)
            return 0

        lax.fori_loop(0, KEYS // STEP, score, 0)
        dq = dot(keys.T, dsb[...], 1, 0) * scale
        for a in range(GR):
            cols = slice(a * D, (a + 1) * D)
            dqs[u, :, cols] = dq[:, cols].T.astype(BF)

        @pl.when(i < 3)
        def _():
            dq_copy(u).start()

        kpart = dot(dsb[...], heads(qst[u]), 1, 0) * scale
        vpart = dot(prob[u], heads(dos[u]), 1, 0)
        part = jnp.concatenate([kpart, vpart], axis=1)
        accw[4 + u] += part[0:D]
        for r in (1, 2, 3):
            later = flag[u * KV + r] > 0
            accw[4 + u + r] += jnp.where(later, part[r * D : (r + 1) * D], 0.0)
            accw[u + r, 0:HALF, :] += jnp.where(later, 0.0, part[r * D : r * D + HALF])
        return 0

    lax.fori_loop(0, KV, backward, 0)
    qg[x] = dqs[x]

    for e in range(1, 11):
        gsend[e] = accw[e].astype(BF)

    def g_copy(e):
        g = e & 3
        if e < 4:
            return remote(gsend.at[e, 0:HALF], gdn.at[x], g_s.at[e], g_r.at[0, x], below + g)
        if e < 8:
            return remote(gsend.at[e], grow.at[x], g_s.at[e], g_r.at[1, x], z * KV + g)
        return remote(gsend.at[e], gup.at[x], g_s.at[e], g_r.at[2, x], above + g)

    for e in (8, 9, 10, 1, 2, 3):
        g_copy(e).start()
    for e in range(4, 8):
        pl.when(x != e - 4)(g_copy(e).start)
    grow[x] = gsend[4 + x]

    whole(snd2, rcv2, a2_s, a2_r).wait_recv()
    for g in range(KV):
        pl.when(x != g)(
            remote(gsend.at[4], grow.at[g], g_s.at[0], g_r.at[1, g], me ^ 1).wait_recv
        )
        pl.when(x <= 2)(remote(gsend.at[4], gup.at[g], g_s.at[0], g_r.at[2, g], me ^ 1).wait_recv)
        pl.when(x >= 1)(
            remote(gsend.at[4, 0:HALF], gdn.at[g], g_s.at[0], g_r.at[0, g], me ^ 1).wait_recv
        )

    for i in (1, 2, 3):
        order_copy(i).wait_send()
        q_copy(i).wait_send()
    kv_all(lambda c: c.wait_send())
    whole(snd1, rcv1, a1_s, a1_r).wait_send()
    whole(snd2, rcv2, a2_s, a2_r).wait_send()
    for e in (8, 9, 10, 1, 2, 3):
        g_copy(e).wait_send()
    for u in range(KV):

        @pl.when(x != u)
        def _():
            g_copy(4 + u).wait_send()
            dq_copy(u).wait_send()
            remote(dqs.at[u], qg.at[u], dq_s.at[u], dq_r.at[u], me ^ 1).wait_recv()


def finish(
    got, qg, grow, gup, gdn, p_ffn,
    out_hbm, qg_hbm, kg_hbm, vg_hbm,
    out_v, kg_v, vg_v, sem,
):
    x = lax.axis_index("ctx") & 3
    outs = []

    def send(src, dst):
        outs.append(pltpu.make_async_copy(src, dst, sem.at[len(outs)]))
        outs[-1].start()

    for g in range(KV):
        send(qg.at[g], qg_hbm.at[:, g * WIDE : (g + 1) * WIDE])
    for g in range(KV):
        total = grow[g].astype(F32) + jnp.where(x <= 2, gup[g].astype(F32), 0.0)
        low = total[0:HALF] + jnp.where(x >= 1, gdn[g].astype(F32), 0.0)
        high = total[HALF:D]
        cols = slice(g * D, (g + 1) * D)
        for ref, lane in ((kg_v, 0), (vg_v, D)):
            ref[0:HALF, cols] = low[:, lane : lane + D].astype(BF)
            ref[HALF:D, cols] = high[:, lane : lane + D].astype(BF)
    send(kg_v, kg_hbm)
    send(vg_v, vg_hbm)
    for g in range(KV):
        cols = slice(g * WIDE, (g + 1) * WIDE)
        out_v[:, cols] = dot(p_ffn[...], got[g * D : (g + 1) * D, :], 1, 0).astype(BF)
        send(out_v.at[:, cols], out_hbm.at[:, cols])
    for c in outs:
        c.wait()


def body(q, k, v, g, sizes, ffn_order, attn_order):
    hbm = pl.BlockSpec(memory_space=pltpu.HBM)
    vmem = pl.BlockSpec(memory_space=pltpu.VMEM)
    dma = pltpu.SemaphoreType.DMA
    vm = pltpu.VMEM
    got, qg, row, up, down, p_ffn = pl.pallas_call(
        kernel,
        out_shape=(
            vm((ROWS, WIDE), BF),
            vm((KV, D, WIDE), BF),
            vm((KV, D, 2 * D), BF),
            vm((KV, D, 2 * D), BF),
            vm((KV, HALF, 2 * D), BF),
            vm((D, D), BF),
        ),
        in_specs=[hbm] * 7,
        out_specs=(vmem,) * 6,
        scratch_shapes=[
            pltpu.SMEM((16,), jnp.int32),
            vm((1, D), jnp.int32),
            vm((KV, 1, D), jnp.int32),
            vm((KV, D, WIDE), BF),
            vm((KV, D, 2 * D), BF),
            vm((KV, D, WIDE), BF),
            vm((12, D, 2 * D), BF),
            vm((KV, KEYS, 2 * D), BF),
            vm((KV, KEYS, WIDE), BF),
            vm((D, KV * WIDE), BF),
            vm((ROWS, WIDE), BF),
            vm((ROWS, WIDE), BF),
            vm((ROWS, WIDE), BF),
            vm((KV * D, ROWS), BF),
            vm((ROWS, KV * D), BF),
            vm((WIDE, KV * D), BF),
            vm((KV, D, WIDE), BF),
            vm((KEYS, WIDE), F32),
            vm((KEYS, WIDE), BF),
            vm((KV, D, WIDE), BF),
            vm((12, D, 2 * D), F32),
            vm((12, D, 2 * D), BF),
            vm((KV, KEYS, D), F32),
            vm((KV, 8, D), F32),
            pltpu.SMEM((KV * KV,), jnp.int32),
            dma((16,)),
            dma((4,)),
            dma((4,)),
            dma((4, 3)),
            dma((12,)),
            dma((4,)),
            dma((4,)),
            dma((4,)),
            dma((4,)),
            dma((12,)),
            dma((3, 4)),
            dma,
            dma,
            dma,
            dma,
        ],
        compiler_params=pltpu.CompilerParams(
            collective_id=0, has_side_effects=True, vmem_limit_bytes=56 * 1024 * 1024
        ),
    )(q, k, v, g, sizes, ffn_order, attn_order)
    return pl.pallas_call(
        finish,
        out_shape=(
            jax.ShapeDtypeStruct((D, KV * WIDE), BF),
            jax.ShapeDtypeStruct((D, KV * WIDE), BF),
            jax.ShapeDtypeStruct((D, KV * D), BF),
            jax.ShapeDtypeStruct((D, KV * D), BF),
        ),
        in_specs=[vmem] * 6,
        out_specs=(hbm,) * 4,
        scratch_shapes=[
            vm((D, KV * WIDE), BF),
            vm((D, KV * D), BF),
            vm((D, KV * D), BF),
            dma((10,)),
        ],
        compiler_params=pltpu.CompilerParams(vmem_limit_bytes=8 * 1024 * 1024),
    )(got, qg, row, up, down, p_ffn)


def solution(mesh):
    rows = P(("dp", "ctx"), None)
    return jax.shard_map(
        body,
        mesh=mesh,
        in_specs=(rows, rows, rows, rows, P("dp"), rows, rows),
        out_specs=(rows,) * 4,
        check_vma=False,
    )
```

```python
import math

import jax
import jax.numpy as jnp
from jax import lax
from jax.experimental import pallas as pl
from jax.experimental.pallas import tpu as pltpu
from jax.sharding import PartitionSpec as P

MESH = pl.DeviceIdType.MESH
D = 128
HALF = 64
KV = 4
GR = 5
N = 32
CHUNK = 16
ROWS = N * CHUNK
WIDE = GR * D
KEYS = 4 * D
NEG = -1e30
TURN = 13
STEP = 32
BF, F32 = jnp.bfloat16, jnp.float32


def dot(a, b, ca, cb):
    return lax.dot_general(a, b, (((ca,), (cb,)), ((), ())), preferred_element_type=F32)


def iota(shape, dim):
    return lax.broadcasted_iota(jnp.int32, shape, dim)


def picks(c, ul):
    return (ul == ((c >> 2) & 3) * D + (c >> 4) * 4 + (c & 3)).astype(BF)


def scatter_matrix(orders):
    pick = picks(iota((KV * D, ROWS), 1), iota((KV * D, ROWS), 0))
    row, c = iota((D, ROWS), 0), iota((D, ROWS), 1)
    target = dot(orders, pick, 1, 0) + (((c >> 2) & 3) * D).astype(F32)
    row = row.astype(F32)
    return jnp.concatenate([(target == row + float(t * D)).astype(BF) for t in range(KV)], axis=0)


def gather_matrix(orders):
    pick = picks(iota((ROWS, KV * D), 0), iota((ROWS, KV * D), 1))
    c, lane = iota((ROWS, D), 0), iota((ROWS, D), 1)
    target = dot(pick, orders, 1, 1) + (((c >> 2) & 3) * D).astype(F32)
    lane = lane.astype(F32)
    return jnp.concatenate([(target == lane + float(t * D)).astype(BF) for t in range(KV)], axis=1)


def heads(x):
    return jnp.concatenate([x[:, a * D : (a + 1) * D] for a in range(GR)], axis=0)


def kernel(
    q_hbm, k_hbm, v_hbm, g_hbm, sizes_hbm, ffn_hbm, att_hbm,
    rcv2, qg, grow, gup, gdn, p_out,
    sizes, ffn_ref, att_ref, qb, kvb, qst, kvw, kall, prob, gin, snd1, rcv1, snd2,
    m_att, mt_att, ott, dos, sc, dsb, dqs, accw, gsend, bias, invs, flag,
    in_sem, att_s, att_r, kv_s, kv_r, q_s, q_r, dq_s, dq_r, g_s, g_r,
    a1_s, a1_r, a2_s, a2_r,
):
    dp = lax.axis_index("dp")
    me = lax.axis_index("ctx")
    z, x = me >> 2, me & 3
    above, below = ((z + 1) & 7) * KV, ((z + 7) & 7) * KV
    scale = 1.0 / math.sqrt(D)

    def remote(src, dst, s, r, peer):
        return pltpu.make_async_remote_copy(
            src_ref=src, dst_ref=dst, send_sem=s, recv_sem=r,
            device_id=(dp, peer), device_id_type=MESH,
        )

    def lanes(i, width):
        return pl.ds(pl.multiple_of(i * width, D), width)

    barrier = pltpu.get_barrier_semaphore()

    def greet(i, _):
        pl.semaphore_signal(
            barrier, inc=1, device_id=(dp, lax.rem(me + i, N)), device_id_type=MESH
        )
        return 0

    lax.fori_loop(1, N, greet, 0)

    local = [
        pltpu.make_async_copy(ffn_hbm, ffn_ref, in_sem.at[0]),
        pltpu.make_async_copy(g_hbm, gin, in_sem.at[1]),
        pltpu.make_async_copy(att_hbm, att_ref.at[x], in_sem.at[2]),
        pltpu.make_async_copy(sizes_hbm, sizes, in_sem.at[3]),
    ]
    for g in range(KV):
        cols = slice(g * D, (g + 1) * D)
        local += [
            pltpu.make_async_copy(k_hbm.at[:, cols], kvb.at[g, :, 0:D], in_sem.at[4 + 3 * g]),
            pltpu.make_async_copy(v_hbm.at[:, cols], kvb.at[g, :, D:], in_sem.at[5 + 3 * g]),
            pltpu.make_async_copy(
                q_hbm.at[:, g * WIDE : (g + 1) * WIDE], qb.at[g], in_sem.at[6 + 3 * g]
            ),
        ]
    for c in local[4:] + local[:4]:
        c.start()

    local[0].wait()
    order = ffn_ref[...].astype(F32)
    p_ffn = (order == iota((D, D), 0).astype(F32)).astype(BF)
    p_out[...] = p_ffn
    gather_ffn = p_ffn.T
    local[1].wait()
    packed = dot(gather_ffn, gin[...], 1, 0).astype(BF)
    for g in range(KV):
        snd1[g * D : (g + 1) * D, :] = packed[:, g * WIDE : (g + 1) * WIDE]

    for c in local[2:]:
        c.wait()
    kvw[4 + x] = kvb[x]
    qst[x] = qb[x]

    pl.semaphore_wait(barrier, N - 1)

    def order_copy(i):
        return remote(att_ref.at[x], att_ref.at[x], att_s.at[i], att_r.at[i], z * KV + ((x + i) & 3))

    def order_arrived(i):
        u = (x + 4 - i) & 3
        return remote(att_ref.at[u], att_ref.at[u], att_s.at[i], att_r.at[i], me ^ 1)

    for i in (1, 2, 3):
        order_copy(i).start()

    def kv_copy(i, what):
        g = (x + i) & 3
        s = kv_s.at[i, what]
        if what == 0:
            return remote(kvb.at[g], kvw.at[4 + x], s, kv_r.at[4 + x], z * KV + g)
        if what == 1:
            return remote(kvb.at[g], kvw.at[8 + x], s, kv_r.at[8 + x], below + g)
        return remote(kvb.at[g, 0:HALF], kvw.at[x, 0:HALF], s, kv_r.at[x], above + g)

    def kv_all(action):
        for i in (2, 1, 3):
            action(kv_copy(i, 0))
        for i in (2, 1, 3, 0):

            @pl.when(x <= 2)
            def _():
                action(kv_copy(i, 1))

            @pl.when(x >= 1)
            def _():
                action(kv_copy(i, 2))

    kv_all(lambda c: c.start())

    def q_copy(i):
        g = (x + i) & 3
        return remote(qb.at[g], qst.at[x], q_s.at[i], q_r.at[x], z * KV + g)

    for i in (2, 1, 3):
        q_copy(i).start()

    def rows_at(i):
        return pl.ds(pl.multiple_of(i * CHUNK, CHUNK), CHUNK)

    def token_row(peer):
        return pl.ds(pl.multiple_of((peer & 3) * D + (peer >> 2) * CHUNK, CHUNK), CHUNK)

    def send1(i, _):
        peer = (me + TURN * i) & (N - 1)
        remote(snd1.at[token_row(peer)], rcv1.at[rows_at(me)], a1_s, a1_r, peer).start()
        return 0

    lax.fori_loop(1, N, send1, 0)
    rcv1[rows_at(me), :] = snd1[token_row(me), :]

    def whole(src, dst, s, r):
        n = ROWS - CHUNK
        return remote(src.at[:n], dst.at[:n], s, r, lax.rem(me + 1, N))

    kk, qq = iota((D, D), 0), iota((D, D), 1)
    for u in range(KV):
        d = z * KV + u
        first, end, start = 0, 0, 0
        for t in range(16):
            stop = start + sizes[t]
            inside = (start <= d) & (d < stop)
            first = jnp.where(inside, start, first)
            end = jnp.where(inside, stop, end)
            start = stop
        bias[u, 0:D, :] = jnp.where(kk <= qq, 0.0, NEG)
        for r in (1, 2, 3):
            flag[u * KV + r] = jnp.where(d + r < end, 1, 0)
            later = jnp.where(d + r < end, 0.0, NEG)
            earlier = jnp.where(d + r - 4 >= first, 0.0, NEG)
            bias[u, r * D : (r + 1) * D, :] = jnp.maximum(
                jnp.where(qq >= HALF, later, NEG), jnp.where(kk < HALF, earlier, NEG)
            )
    accw[...] = jnp.zeros_like(accw)
    invs[...] = jnp.zeros_like(invs)

    for i in (1, 2, 3):
        order_arrived(i).wait_recv()
    orders = jnp.concatenate([att_ref[u] for u in range(KV)], axis=1)
    orders = jnp.broadcast_to(orders.astype(F32).astype(BF), (D, KV * D))
    m_att[...] = scatter_matrix(orders)
    mt_att[...] = gather_matrix(orders)

    for e in range(1, 11):
        rows = slice(0, HALF) if e < 4 else slice(0, D)
        c = remote(kvb.at[0, rows], kvw.at[e, rows], kv_s.at[0, 0], kv_r.at[e], me ^ 1)
        if 4 <= e < 8:
            pl.when(x != e - 4)(c.wait_recv)
        else:
            c.wait_recv()

    def forward(i, _):
        u = (x + i) & 3

        @pl.when(i > 0)
        def _():
            remote(qb.at[0], qst.at[u], q_s.at[0], q_r.at[u], me ^ 1).wait_recv()

        kall[u, 0:D, :] = kvw[4 + u]
        for r in (1, 2, 3):
            kall[u, r * D : r * D + HALF, :] = jnp.where(
                flag[u * KV + r] > 0, kvw[4 + u + r, 0:HALF, :], kvw[u + r, 0:HALF, :]
            )
            kall[u, r * D + HALF : (r + 1) * D, :] = kvw[4 + u + r, HALF:D, :]
        keys, values = kall[u, :, 0:D], kall[u, :, D : 2 * D]
        sc[...] = dot(keys, heads(qst[u]), 1, 1)

        def masked(b):
            rows = pl.ds(pl.multiple_of(b * STEP, STEP), STEP)
            return sc[rows, :] + jnp.concatenate([bias[u, rows, :]] * GR, axis=1)

        def largest(b, top):
            return jnp.maximum(top, jnp.max(masked(b).reshape(STEP // 8, 8, WIDE), axis=0))

        top = lax.fori_loop(0, KEYS // STEP, largest, jnp.full((8, WIDE), NEG, F32))
        top = jnp.max(top, axis=0, keepdims=True)

        def weigh(b, total):
            p = jnp.exp2((masked(b) - top) * (scale * math.log2(math.e)))
            prob[u, pl.ds(pl.multiple_of(b * STEP, STEP), STEP), :] = p.astype(BF)
            return total + jnp.sum(p.reshape(STEP // 8, 8, WIDE), axis=0)

        total = lax.fori_loop(0, KEYS // STEP, weigh, jnp.zeros((8, WIDE), F32))
        inv = 1.0 / jnp.sum(total, axis=0, keepdims=True)
        o = (dot(values.T, prob[u], 1, 0) * inv).astype(BF)
        for a in range(GR):
            cols = slice(a * D, (a + 1) * D)
            ott[cols, lanes(u, D)] = o[:, cols]
            invs[u, a : a + 1, :] = inv[:, cols]
        return 0

    lax.fori_loop(0, KV, forward, 0)

    snd2[...] = dot(mt_att[...], ott[...], 1, 1).astype(BF)

    def send2(i, _):
        peer = (me + TURN * i) & (N - 1)
        remote(snd2.at[rows_at(peer)], rcv2.at[token_row(me)], a2_s, a2_r, peer).start()
        return 0

    lax.fori_loop(1, N, send2, 0)
    rcv2[token_row(me), :] = snd2[rows_at(me), :]

    whole(snd1, rcv1, a1_s, a1_r).wait_recv()
    for u in range(KV):
        up = dot(m_att[u * D : (u + 1) * D, :], rcv1[...], 1, 0)
        inv = invs[u].T
        for a in range(GR):
            cols = slice(a * D, (a + 1) * D)
            dos[u, :, cols] = (up[:, cols] * inv[:, a : a + 1]).astype(BF)

    def dq_copy(u):
        return remote(dqs.at[u], qg.at[x], dq_s.at[u], dq_r.at[x], z * KV + u)

    def backward(i, _):
        u = (x + 1 + i) & 3
        keys, values = kall[u, :, 0:D], kall[u, :, D : 2 * D]
        sc[...] = dot(values, heads(dos[u]), 1, 1)

        def blocks(b):
            rows = pl.ds(pl.multiple_of(b * STEP, STEP), STEP)
            return prob[u, rows, :].astype(F32), sc[rows, :]

        def add(b, total):
            p, dp_t = blocks(b)
            return total + jnp.sum((p * dp_t).reshape(STEP // 8, 8, WIDE), axis=0)

        total = lax.fori_loop(0, KEYS // STEP, add, jnp.zeros((8, WIDE), F32))
        inv = jnp.concatenate([invs[u, a : a + 1, :] for a in range(GR)], axis=1)
        delta = jnp.sum(total, axis=0, keepdims=True) * inv

        def score(b, _):
            p, dp_t = blocks(b)
            dsb[pl.ds(pl.multiple_of(b * STEP, STEP), STEP), :] = (p * (dp_t - delta)).astype(BF)
            return 0

        lax.fori_loop(0, KEYS // STEP, score, 0)
        dq = dot(keys.T, dsb[...], 1, 0) * scale
        for a in range(GR):
            cols = slice(a * D, (a + 1) * D)
            dqs[u, :, cols] = dq[:, cols].T.astype(BF)

        @pl.when(i < 3)
        def _():
            dq_copy(u).start()

        kpart = dot(dsb[...], heads(qst[u]), 1, 0) * scale
        vpart = dot(prob[u], heads(dos[u]), 1, 0)
        part = jnp.concatenate([kpart, vpart], axis=1)
        accw[4 + u] += part[0:D]
        for r in (1, 2, 3):
            later = flag[u * KV + r] > 0
            accw[4 + u + r] += jnp.where(later, part[r * D : (r + 1) * D], 0.0)
            accw[u + r, 0:HALF, :] += jnp.where(later, 0.0, part[r * D : r * D + HALF])
        return 0

    lax.fori_loop(0, KV, backward, 0)
    qg[x] = dqs[x]

    for e in range(1, 11):
        gsend[e] = accw[e].astype(BF)

    def g_copy(e):
        g = e & 3
        if e < 4:
            return remote(gsend.at[e, 0:HALF], gdn.at[x], g_s.at[e], g_r.at[0, x], below + g)
        if e < 8:
            return remote(gsend.at[e], grow.at[x], g_s.at[e], g_r.at[1, x], z * KV + g)
        return remote(gsend.at[e], gup.at[x], g_s.at[e], g_r.at[2, x], above + g)

    for e in (8, 9, 10, 1, 2, 3):
        g_copy(e).start()
    for e in range(4, 8):
        pl.when(x != e - 4)(g_copy(e).start)
    grow[x] = gsend[4 + x]

    whole(snd2, rcv2, a2_s, a2_r).wait_recv()
    for g in range(KV):
        pl.when(x != g)(
            remote(gsend.at[4], grow.at[g], g_s.at[0], g_r.at[1, g], me ^ 1).wait_recv
        )
        pl.when(x <= 2)(remote(gsend.at[4], gup.at[g], g_s.at[0], g_r.at[2, g], me ^ 1).wait_recv)
        pl.when(x >= 1)(
            remote(gsend.at[4, 0:HALF], gdn.at[g], g_s.at[0], g_r.at[0, g], me ^ 1).wait_recv
        )

    for i in (1, 2, 3):
        order_copy(i).wait_send()
        q_copy(i).wait_send()
    kv_all(lambda c: c.wait_send())
    whole(snd1, rcv1, a1_s, a1_r).wait_send()
    whole(snd2, rcv2, a2_s, a2_r).wait_send()
    for e in (8, 9, 10, 1, 2, 3):
        g_copy(e).wait_send()
    for u in range(KV):

        @pl.when(x != u)
        def _():
            g_copy(4 + u).wait_send()
            dq_copy(u).wait_send()
            remote(dqs.at[u], qg.at[u], dq_s.at[u], dq_r.at[u], me ^ 1).wait_recv()


def finish(
    got, qg, grow, gup, gdn, p_ffn,
    out_hbm, qg_hbm, kg_hbm, vg_hbm,
    out_v, kg_v, vg_v, sem,
):
    x = lax.axis_index("ctx") & 3
    outs = []

    def send(src, dst):
        outs.append(pltpu.make_async_copy(src, dst, sem.at[len(outs)]))
        outs[-1].start()

    for g in range(KV):
        send(qg.at[g], qg_hbm.at[:, g * WIDE : (g + 1) * WIDE])
    for g in range(KV):
        total = grow[g].astype(F32) + jnp.where(x <= 2, gup[g].astype(F32), 0.0)
        low = total[0:HALF] + jnp.where(x >= 1, gdn[g].astype(F32), 0.0)
        high = total[HALF:D]
        cols = slice(g * D, (g + 1) * D)
        for ref, lane in ((kg_v, 0), (vg_v, D)):
            ref[0:HALF, cols] = low[:, lane : lane + D].astype(BF)
            ref[HALF:D, cols] = high[:, lane : lane + D].astype(BF)
    send(kg_v, kg_hbm)
    send(vg_v, vg_hbm)
    for g in range(KV):
        cols = slice(g * WIDE, (g + 1) * WIDE)
        out_v[:, cols] = dot(p_ffn[...], got[g * D : (g + 1) * D, :], 1, 0).astype(BF)
        send(out_v.at[:, cols], out_hbm.at[:, cols])
    for c in outs:
        c.wait()


def body(q, k, v, g, sizes, ffn_order, attn_order):
    hbm = pl.BlockSpec(memory_space=pltpu.HBM)
    vmem = pl.BlockSpec(memory_space=pltpu.VMEM)
    dma = pltpu.SemaphoreType.DMA
    vm = pltpu.VMEM
    got, qg, row, up, down, p_ffn = pl.pallas_call(
        kernel,
        out_shape=(
            vm((ROWS, WIDE), BF),
            vm((KV, D, WIDE), BF),
            vm((KV, D, 2 * D), BF),
            vm((KV, D, 2 * D), BF),
            vm((KV, HALF, 2 * D), BF),
            vm((D, D), BF),
        ),
        in_specs=[hbm] * 7,
        out_specs=(vmem,) * 6,
        scratch_shapes=[
            pltpu.SMEM((16,), jnp.int32),
            vm((1, D), jnp.int32),
            vm((KV, 1, D), jnp.int32),
            vm((KV, D, WIDE), BF),
            vm((KV, D, 2 * D), BF),
            vm((KV, D, WIDE), BF),
            vm((12, D, 2 * D), BF),
            vm((KV, KEYS, 2 * D), BF),
            vm((KV, KEYS, WIDE), BF),
            vm((D, KV * WIDE), BF),
            vm((ROWS, WIDE), BF),
            vm((ROWS, WIDE), BF),
            vm((ROWS, WIDE), BF),
            vm((KV * D, ROWS), BF),
            vm((ROWS, KV * D), BF),
            vm((WIDE, KV * D), BF),
            vm((KV, D, WIDE), BF),
            vm((KEYS, WIDE), F32),
            vm((KEYS, WIDE), BF),
            vm((KV, D, WIDE), BF),
            vm((12, D, 2 * D), F32),
            vm((12, D, 2 * D), BF),
            vm((KV, KEYS, D), F32),
            vm((KV, 8, D), F32),
            pltpu.SMEM((KV * KV,), jnp.int32),
            dma((16,)),
            dma((4,)),
            dma((4,)),
            dma((4, 3)),
            dma((12,)),
            dma((4,)),
            dma((4,)),
            dma((4,)),
            dma((4,)),
            dma((12,)),
            dma((3, 4)),
            dma,
            dma,
            dma,
            dma,
        ],
        compiler_params=pltpu.CompilerParams(
            collective_id=0, has_side_effects=True, vmem_limit_bytes=56 * 1024 * 1024
        ),
    )(q, k, v, g, sizes, ffn_order, attn_order)
    return pl.pallas_call(
        finish,
        out_shape=(
            jax.ShapeDtypeStruct((D, KV * WIDE), BF),
            jax.ShapeDtypeStruct((D, KV * WIDE), BF),
            jax.ShapeDtypeStruct((D, KV * D), BF),
            jax.ShapeDtypeStruct((D, KV * D), BF),
        ),
        in_specs=[vmem] * 6,
        out_specs=(hbm,) * 4,
        scratch_shapes=[
            vm((D, KV * WIDE), BF),
            vm((D, KV * D), BF),
            vm((D, KV * D), BF),
            dma((10,)),
        ],
        compiler_params=pltpu.CompilerParams(vmem_limit_bytes=8 * 1024 * 1024),
    )(got, qg, row, up, down, p_ffn)


def solution(mesh):
    rows = P(("dp", "ctx"), None)
    return jax.shard_map(
        body,
        mesh=mesh,
        in_specs=(rows, rows, rows, rows, P("dp"), rows, rows),
        out_specs=(rows,) * 4,
        check_vma=False,
    )
```

```python
import math

import jax
import jax.numpy as jnp
from jax import lax
from jax.experimental import pallas as pl
from jax.experimental.pallas import tpu as pltpu
from jax.sharding import PartitionSpec as P

MESH = pl.DeviceIdType.MESH
D = 128
HALF = 64
KV = 4
GR = 5
N = 32
CHUNK = 16
ROWS = N * CHUNK
WIDE = GR * D
KEYS = 4 * D
NEG = -1e30
TURN = 13
STEP = 32
BF, F32 = jnp.bfloat16, jnp.float32


def dot(a, b, ca, cb):
    return lax.dot_general(a, b, (((ca,), (cb,)), ((), ())), preferred_element_type=F32)


def iota(shape, dim):
    return lax.broadcasted_iota(jnp.int32, shape, dim)


def picks(c, ul):
    return (ul == ((c >> 2) & 3) * D + (c >> 4) * 4 + (c & 3)).astype(BF)


def scatter_matrix(orders):
    pick = picks(iota((KV * D, ROWS), 1), iota((KV * D, ROWS), 0))
    row, c = iota((D, ROWS), 0), iota((D, ROWS), 1)
    target = dot(orders, pick, 1, 0) + (((c >> 2) & 3) * D).astype(F32)
    row = row.astype(F32)
    return jnp.concatenate([(target == row + float(t * D)).astype(BF) for t in range(KV)], axis=0)


def gather_matrix(orders):
    pick = picks(iota((ROWS, KV * D), 0), iota((ROWS, KV * D), 1))
    c, lane = iota((ROWS, D), 0), iota((ROWS, D), 1)
    target = dot(pick, orders, 1, 1) + (((c >> 2) & 3) * D).astype(F32)
    lane = lane.astype(F32)
    return jnp.concatenate([(target == lane + float(t * D)).astype(BF) for t in range(KV)], axis=1)


def heads(x):
    return jnp.concatenate([x[:, a * D : (a + 1) * D] for a in range(GR)], axis=0)


def kernel(
    q_hbm, k_hbm, v_hbm, g_hbm, sizes_hbm, ffn_hbm, att_hbm,
    rcv2, qg, grow, gup, gdn, p_out,
    sizes, ffn_ref, att_ref, qb, kvb, qst, kvw, kall, prob, gin, snd1, rcv1, snd2,
    m_att, mt_att, ott, dos, sc, dsb, dqs, accw, gsend, bias, invs, flag,
    in_sem, att_s, att_r, kv_s, kv_r, q_s, q_r, dq_s, dq_r, g_s, g_r,
    a1_s, a1_r, a2_s, a2_r,
):
    dp = lax.axis_index("dp")
    me = lax.axis_index("ctx")
    z, x = me >> 2, me & 3
    above, below = ((z + 1) & 7) * KV, ((z + 7) & 7) * KV
    scale = 1.0 / math.sqrt(D)

    def remote(src, dst, s, r, peer):
        return pltpu.make_async_remote_copy(
            src_ref=src, dst_ref=dst, send_sem=s, recv_sem=r,
            device_id=(dp, peer), device_id_type=MESH,
        )

    def lanes(i, width):
        return pl.ds(pl.multiple_of(i * width, D), width)

    barrier = pltpu.get_barrier_semaphore()

    def greet(i, _):
        pl.semaphore_signal(
            barrier, inc=1, device_id=(dp, lax.rem(me + i, N)), device_id_type=MESH
        )
        return 0

    lax.fori_loop(1, N, greet, 0)

    local = [
        pltpu.make_async_copy(ffn_hbm, ffn_ref, in_sem.at[0]),
        pltpu.make_async_copy(g_hbm, gin, in_sem.at[1]),
        pltpu.make_async_copy(att_hbm, att_ref.at[x], in_sem.at[2]),
        pltpu.make_async_copy(sizes_hbm, sizes, in_sem.at[3]),
    ]
    for g in range(KV):
        cols = slice(g * D, (g + 1) * D)
        local += [
            pltpu.make_async_copy(k_hbm.at[:, cols], kvb.at[g, :, 0:D], in_sem.at[4 + 3 * g]),
            pltpu.make_async_copy(v_hbm.at[:, cols], kvb.at[g, :, D:], in_sem.at[5 + 3 * g]),
            pltpu.make_async_copy(
                q_hbm.at[:, g * WIDE : (g + 1) * WIDE], qb.at[g], in_sem.at[6 + 3 * g]
            ),
        ]
    for c in local[4:] + local[:4]:
        c.start()

    local[0].wait()
    order = ffn_ref[...].astype(F32)
    p_ffn = (order == iota((D, D), 0).astype(F32)).astype(BF)
    p_out[...] = p_ffn
    gather_ffn = p_ffn.T
    local[1].wait()
    packed = dot(gather_ffn, gin[...], 1, 0).astype(BF)
    for g in range(KV):
        snd1[g * D : (g + 1) * D, :] = packed[:, g * WIDE : (g + 1) * WIDE]

    for c in local[2:]:
        c.wait()
    kvw[4 + x] = kvb[x]
    qst[x] = qb[x]

    pl.semaphore_wait(barrier, N - 1)

    def order_copy(i):
        return remote(att_ref.at[x], att_ref.at[x], att_s.at[i], att_r.at[i], z * KV + ((x + i) & 3))

    def order_arrived(i):
        u = (x + 4 - i) & 3
        return remote(att_ref.at[u], att_ref.at[u], att_s.at[i], att_r.at[i], me ^ 1)

    for i in (1, 2, 3):
        order_copy(i).start()

    def kv_copy(i, what):
        g = (x + i) & 3
        s = kv_s.at[i, what]
        if what == 0:
            return remote(kvb.at[g], kvw.at[4 + x], s, kv_r.at[4 + x], z * KV + g)
        if what == 1:
            return remote(kvb.at[g], kvw.at[8 + x], s, kv_r.at[8 + x], below + g)
        return remote(kvb.at[g, 0:HALF], kvw.at[x, 0:HALF], s, kv_r.at[x], above + g)

    def kv_all(action):
        for i in (2, 1, 3):
            action(kv_copy(i, 0))
        for i in (2, 1, 3, 0):

            @pl.when(x <= 2)
            def _():
                action(kv_copy(i, 1))

            @pl.when(x >= 1)
            def _():
                action(kv_copy(i, 2))

    kv_all(lambda c: c.start())

    def q_copy(i):
        g = (x + i) & 3
        return remote(qb.at[g], qst.at[x], q_s.at[i], q_r.at[x], z * KV + g)

    for i in (2, 1, 3):
        q_copy(i).start()

    def rows_at(i):
        return pl.ds(pl.multiple_of(i * CHUNK, CHUNK), CHUNK)

    def token_row(peer):
        return pl.ds(pl.multiple_of((peer & 3) * D + (peer >> 2) * CHUNK, CHUNK), CHUNK)

    def send1(i, _):
        peer = (me + TURN * i) & (N - 1)
        remote(snd1.at[token_row(peer)], rcv1.at[rows_at(me)], a1_s, a1_r, peer).start()
        return 0

    lax.fori_loop(1, N, send1, 0)
    rcv1[rows_at(me), :] = snd1[token_row(me), :]

    def whole(src, dst, s, r):
        n = ROWS - CHUNK
        return remote(src.at[:n], dst.at[:n], s, r, lax.rem(me + 1, N))

    kk, qq = iota((D, D), 0), iota((D, D), 1)
    for u in range(KV):
        d = z * KV + u
        first, end, start = 0, 0, 0
        for t in range(16):
            stop = start + sizes[t]
            inside = (start <= d) & (d < stop)
            first = jnp.where(inside, start, first)
            end = jnp.where(inside, stop, end)
            start = stop
        bias[u, 0:D, :] = jnp.where(kk <= qq, 0.0, NEG)
        for r in (1, 2, 3):
            flag[u * KV + r] = jnp.where(d + r < end, 1, 0)
            later = jnp.where(d + r < end, 0.0, NEG)
            earlier = jnp.where(d + r - 4 >= first, 0.0, NEG)
            bias[u, r * D : (r + 1) * D, :] = jnp.maximum(
                jnp.where(qq >= HALF, later, NEG), jnp.where(kk < HALF, earlier, NEG)
            )
    accw[...] = jnp.zeros_like(accw)
    invs[...] = jnp.zeros_like(invs)

    for i in (1, 2, 3):
        order_arrived(i).wait_recv()
    orders = jnp.concatenate([att_ref[u] for u in range(KV)], axis=1)
    orders = jnp.broadcast_to(orders.astype(F32).astype(BF), (D, KV * D))
    m_att[...] = scatter_matrix(orders)
    mt_att[...] = gather_matrix(orders)

    for e in range(1, 11):
        rows = slice(0, HALF) if e < 4 else slice(0, D)
        c = remote(kvb.at[0, rows], kvw.at[e, rows], kv_s.at[0, 0], kv_r.at[e], me ^ 1)
        if 4 <= e < 8:
            pl.when(x != e - 4)(c.wait_recv)
        else:
            c.wait_recv()

    def forward(i, _):
        u = (x + i) & 3

        @pl.when(i > 0)
        def _():
            remote(qb.at[0], qst.at[u], q_s.at[0], q_r.at[u], me ^ 1).wait_recv()

        kall[u, 0:D, :] = kvw[4 + u]
        for r in (1, 2, 3):
            kall[u, r * D : r * D + HALF, :] = jnp.where(
                flag[u * KV + r] > 0, kvw[4 + u + r, 0:HALF, :], kvw[u + r, 0:HALF, :]
            )
            kall[u, r * D + HALF : (r + 1) * D, :] = kvw[4 + u + r, HALF:D, :]
        keys, values = kall[u, :, 0:D], kall[u, :, D : 2 * D]
        sc[...] = dot(keys, heads(qst[u]), 1, 1)

        blocks = [slice(b, b + STEP) for b in range(0, KEYS, STEP)]

        def masked(rows):
            return sc[rows, :] + jnp.concatenate([bias[u, rows, :]] * GR, axis=1)

        top = jnp.full((8, WIDE), NEG, F32)
        for rows in blocks:
            top = jnp.maximum(top, jnp.max(masked(rows).reshape(STEP // 8, 8, WIDE), axis=0))
        top = jnp.max(top, axis=0, keepdims=True)
        total = jnp.zeros((8, WIDE), F32)
        for rows in blocks:
            p = jnp.exp2((masked(rows) - top) * (scale * math.log2(math.e)))
            prob[u, rows, :] = p.astype(BF)
            total = total + jnp.sum(p.reshape(STEP // 8, 8, WIDE), axis=0)
        inv = 1.0 / jnp.sum(total, axis=0, keepdims=True)
        o = (dot(values.T, prob[u], 1, 0) * inv).astype(BF)
        for a in range(GR):
            cols = slice(a * D, (a + 1) * D)
            ott[cols, lanes(u, D)] = o[:, cols]
            invs[u, a : a + 1, :] = inv[:, cols]
        return 0

    lax.fori_loop(0, KV, forward, 0)

    snd2[...] = dot(mt_att[...], ott[...], 1, 1).astype(BF)

    def send2(i, _):
        peer = (me + TURN * i) & (N - 1)
        remote(snd2.at[rows_at(peer)], rcv2.at[token_row(me)], a2_s, a2_r, peer).start()
        return 0

    lax.fori_loop(1, N, send2, 0)
    rcv2[token_row(me), :] = snd2[rows_at(me), :]

    whole(snd1, rcv1, a1_s, a1_r).wait_recv()
    every = dot(m_att[...], rcv1[...], 1, 0)
    for u in range(KV):
        up = every[u * D : (u + 1) * D]
        inv = invs[u].T
        for a in range(GR):
            cols = slice(a * D, (a + 1) * D)
            dos[u, :, cols] = (up[:, cols] * inv[:, a : a + 1]).astype(BF)

    def dq_copy(u):
        return remote(dqs.at[u], qg.at[x], dq_s.at[u], dq_r.at[x], z * KV + u)

    def backward(i, _):
        u = (x + 1 + i) & 3
        keys, values = kall[u, :, 0:D], kall[u, :, D : 2 * D]
        sc[...] = dot(values, heads(dos[u]), 1, 1)

        blocks = [slice(b, b + STEP) for b in range(0, KEYS, STEP)]
        total = jnp.zeros((8, WIDE), F32)
        for rows in blocks:
            t = prob[u, rows, :].astype(F32) * sc[rows, :]
            total = total + jnp.sum(t.reshape(STEP // 8, 8, WIDE), axis=0)
        inv = jnp.concatenate([invs[u, a : a + 1, :] for a in range(GR)], axis=1)
        delta = jnp.sum(total, axis=0, keepdims=True) * inv

        for rows in blocks:
            dsb[rows, :] = (prob[u, rows, :].astype(F32) * (sc[rows, :] - delta)).astype(BF)
        dq = dot(keys.T, dsb[...], 1, 0) * scale
        for a in range(GR):
            cols = slice(a * D, (a + 1) * D)
            dqs[u, :, cols] = dq[:, cols].T.astype(BF)

        @pl.when(i < 3)
        def _():
            dq_copy(u).start()

        kpart = dot(dsb[...], heads(qst[u]), 1, 0) * scale
        vpart = dot(prob[u], heads(dos[u]), 1, 0)
        part = jnp.concatenate([kpart, vpart], axis=1)
        accw[4 + u] += part[0:D]
        for r in (1, 2, 3):
            later = flag[u * KV + r] > 0
            accw[4 + u + r] += jnp.where(later, part[r * D : (r + 1) * D], 0.0)
            accw[u + r, 0:HALF, :] += jnp.where(later, 0.0, part[r * D : r * D + HALF])
        return 0

    lax.fori_loop(0, KV, backward, 0)
    qg[x] = dqs[x]

    for e in range(1, 11):
        gsend[e] = accw[e].astype(BF)

    def g_copy(e):
        g = e & 3
        if e < 4:
            return remote(gsend.at[e, 0:HALF], gdn.at[x], g_s.at[e], g_r.at[0, x], below + g)
        if e < 8:
            return remote(gsend.at[e], grow.at[x], g_s.at[e], g_r.at[1, x], z * KV + g)
        return remote(gsend.at[e], gup.at[x], g_s.at[e], g_r.at[2, x], above + g)

    for e in (8, 9, 10, 1, 2, 3):
        g_copy(e).start()
    for e in range(4, 8):
        pl.when(x != e - 4)(g_copy(e).start)
    grow[x] = gsend[4 + x]

    whole(snd2, rcv2, a2_s, a2_r).wait_recv()
    for g in range(KV):
        pl.when(x != g)(
            remote(gsend.at[4], grow.at[g], g_s.at[0], g_r.at[1, g], me ^ 1).wait_recv
        )
        pl.when(x <= 2)(remote(gsend.at[4], gup.at[g], g_s.at[0], g_r.at[2, g], me ^ 1).wait_recv)
        pl.when(x >= 1)(
            remote(gsend.at[4, 0:HALF], gdn.at[g], g_s.at[0], g_r.at[0, g], me ^ 1).wait_recv
        )

    for i in (1, 2, 3):
        order_copy(i).wait_send()
        q_copy(i).wait_send()
    kv_all(lambda c: c.wait_send())
    whole(snd1, rcv1, a1_s, a1_r).wait_send()
    whole(snd2, rcv2, a2_s, a2_r).wait_send()
    for e in (8, 9, 10, 1, 2, 3):
        g_copy(e).wait_send()
    for u in range(KV):

        @pl.when(x != u)
        def _():
            g_copy(4 + u).wait_send()
            dq_copy(u).wait_send()
            remote(dqs.at[u], qg.at[u], dq_s.at[u], dq_r.at[u], me ^ 1).wait_recv()


def finish(
    got, qg, grow, gup, gdn, p_ffn,
    out_hbm, qg_hbm, kg_hbm, vg_hbm,
    out_v, kg_v, vg_v, sem,
):
    x = lax.axis_index("ctx") & 3
    outs = []

    def send(src, dst):
        outs.append(pltpu.make_async_copy(src, dst, sem.at[len(outs)]))
        outs[-1].start()

    for g in range(KV):
        send(qg.at[g], qg_hbm.at[:, g * WIDE : (g + 1) * WIDE])
    for g in range(KV):
        total = grow[g].astype(F32) + jnp.where(x <= 2, gup[g].astype(F32), 0.0)
        low = total[0:HALF] + jnp.where(x >= 1, gdn[g].astype(F32), 0.0)
        high = total[HALF:D]
        cols = slice(g * D, (g + 1) * D)
        for ref, lane in ((kg_v, 0), (vg_v, D)):
            ref[0:HALF, cols] = low[:, lane : lane + D].astype(BF)
            ref[HALF:D, cols] = high[:, lane : lane + D].astype(BF)
    send(kg_v, kg_hbm)
    send(vg_v, vg_hbm)
    for g in range(KV):
        cols = slice(g * WIDE, (g + 1) * WIDE)
        out_v[:, cols] = dot(p_ffn[...], got[g * D : (g + 1) * D, :], 1, 0).astype(BF)
        send(out_v.at[:, cols], out_hbm.at[:, cols])
    for c in outs:
        c.wait()


def body(q, k, v, g, sizes, ffn_order, attn_order):
    hbm = pl.BlockSpec(memory_space=pltpu.HBM)
    vmem = pl.BlockSpec(memory_space=pltpu.VMEM)
    dma = pltpu.SemaphoreType.DMA
    vm = pltpu.VMEM
    got, qg, row, up, down, p_ffn = pl.pallas_call(
        kernel,
        out_shape=(
            vm((ROWS, WIDE), BF),
            vm((KV, D, WIDE), BF),
            vm((KV, D, 2 * D), BF),
            vm((KV, D, 2 * D), BF),
            vm((KV, HALF, 2 * D), BF),
            vm((D, D), BF),
        ),
        in_specs=[hbm] * 7,
        out_specs=(vmem,) * 6,
        scratch_shapes=[
            pltpu.SMEM((16,), jnp.int32),
            vm((1, D), jnp.int32),
            vm((KV, 1, D), jnp.int32),
            vm((KV, D, WIDE), BF),
            vm((KV, D, 2 * D), BF),
            vm((KV, D, WIDE), BF),
            vm((12, D, 2 * D), BF),
            vm((KV, KEYS, 2 * D), BF),
            vm((KV, KEYS, WIDE), BF),
            vm((D, KV * WIDE), BF),
            vm((ROWS, WIDE), BF),
            vm((ROWS, WIDE), BF),
            vm((ROWS, WIDE), BF),
            vm((KV * D, ROWS), BF),
            vm((ROWS, KV * D), BF),
            vm((WIDE, KV * D), BF),
            vm((KV, D, WIDE), BF),
            vm((KEYS, WIDE), F32),
            vm((KEYS, WIDE), BF),
            vm((KV, D, WIDE), BF),
            vm((12, D, 2 * D), F32),
            vm((12, D, 2 * D), BF),
            vm((KV, KEYS, D), F32),
            vm((KV, 8, D), F32),
            pltpu.SMEM((KV * KV,), jnp.int32),
            dma((16,)),
            dma((4,)),
            dma((4,)),
            dma((4, 3)),
            dma((12,)),
            dma((4,)),
            dma((4,)),
            dma((4,)),
            dma((4,)),
            dma((12,)),
            dma((3, 4)),
            dma,
            dma,
            dma,
            dma,
        ],
        compiler_params=pltpu.CompilerParams(
            collective_id=0, has_side_effects=True, vmem_limit_bytes=56 * 1024 * 1024
        ),
    )(q, k, v, g, sizes, ffn_order, attn_order)
    return pl.pallas_call(
        finish,
        out_shape=(
            jax.ShapeDtypeStruct((D, KV * WIDE), BF),
            jax.ShapeDtypeStruct((D, KV * WIDE), BF),
            jax.ShapeDtypeStruct((D, KV * D), BF),
            jax.ShapeDtypeStruct((D, KV * D), BF),
        ),
        in_specs=[vmem] * 6,
        out_specs=(hbm,) * 4,
        scratch_shapes=[
            vm((D, KV * WIDE), BF),
            vm((D, KV * D), BF),
            vm((D, KV * D), BF),
            dma((10,)),
        ],
        compiler_params=pltpu.CompilerParams(vmem_limit_bytes=8 * 1024 * 1024),
    )(got, qg, row, up, down, p_ffn)


def solution(mesh):
    rows = P(("dp", "ctx"), None)
    return jax.shard_map(
        body,
        mesh=mesh,
        in_specs=(rows, rows, rows, rows, P("dp"), rows, rows),
        out_specs=(rows,) * 4,
        check_vma=False,
    )
```

```python
import math

import jax
import jax.numpy as jnp
from jax import lax
from jax.experimental import pallas as pl
from jax.experimental.pallas import tpu as pltpu
from jax.sharding import PartitionSpec as P

MESH = pl.DeviceIdType.MESH
D = 128
HALF = 64
KV = 4
GR = 5
N = 32
CHUNK = 16
ROWS = N * CHUNK
WIDE = GR * D
KEYS = 4 * D
NEG = -1e30
STEP = 32
BF, F32 = jnp.bfloat16, jnp.float32


def dot(a, b, ca, cb):
    return lax.dot_general(a, b, (((ca,), (cb,)), ((), ())), preferred_element_type=F32)


def iota(shape, dim):
    return lax.broadcasted_iota(jnp.int32, shape, dim)


def picks():
    c, l = iota((ROWS, D), 0), iota((ROWS, D), 1)
    entry = (l == (c >> 4) * 4 + (c & 3)).astype(F32)
    device = (c >> 2) & 3
    return jnp.concatenate(
        [jnp.where(device == u, entry, 0.0).astype(BF) for u in range(KV)], axis=1
    )


def scatter_matrix(orders, pick):
    row, c = iota((D, ROWS), 0), iota((D, ROWS), 1)
    target = dot(orders, pick, 1, 1) + (((c >> 2) & 3) * D).astype(F32)
    row = row.astype(F32)
    return jnp.concatenate([(target == row + float(t * D)).astype(BF) for t in range(KV)], axis=0)


def gather_matrix(orders, pick):
    c, lane = iota((ROWS, D), 0), iota((ROWS, D), 1)
    target = dot(pick, orders, 1, 1) + (((c >> 2) & 3) * D).astype(F32)
    lane = lane.astype(F32)
    return jnp.concatenate([(target == lane + float(t * D)).astype(BF) for t in range(KV)], axis=1)


def heads(x):
    return jnp.concatenate([x[:, a * D : (a + 1) * D] for a in range(GR)], axis=0)


def kernel(
    q_hbm, k_hbm, v_hbm, g_hbm, sizes_hbm, ffn_hbm, att_hbm,
    rcv2, qg, grow, gup, gdn, p_out,
    sizes, ffn_ref, att_ref, qb, kvb, qst, kvw, kall, prob, gin, snd1, rcv1, snd2,
    m_att, mt_att, ott, dos, sc, dsb, dqs, accw, gsend, bias, invs, flag,
    in_sem, att_s, att_r, kv_s, kv_r, kz_s, kz_r, q_s, q_r, dq_s, dq_r, g_s, g_r,
    a1_s, a1_r, a2_s, a2_r,
):
    dp = lax.axis_index("dp")
    me = lax.axis_index("ctx")
    z, x = me >> 2, me & 3
    above, below = ((z + 1) & 7) * KV, ((z + 7) & 7) * KV
    scale = 1.0 / math.sqrt(D)

    def remote(src, dst, s, r, peer):
        return pltpu.make_async_remote_copy(
            src_ref=src, dst_ref=dst, send_sem=s, recv_sem=r,
            device_id=(dp, peer), device_id_type=MESH,
        )

    def lanes(i, width):
        return pl.ds(pl.multiple_of(i * width, D), width)

    barrier = pltpu.get_barrier_semaphore()

    def greet(i, _):
        pl.semaphore_signal(
            barrier, inc=1, device_id=(dp, lax.rem(me + i, N)), device_id_type=MESH
        )
        return 0

    lax.fori_loop(1, N, greet, 0)

    local = [
        pltpu.make_async_copy(ffn_hbm, ffn_ref, in_sem.at[0]),
        pltpu.make_async_copy(g_hbm, gin, in_sem.at[1]),
        pltpu.make_async_copy(att_hbm, att_ref.at[x], in_sem.at[2]),
        pltpu.make_async_copy(sizes_hbm, sizes, in_sem.at[3]),
    ]
    for g in range(KV):
        cols = slice(g * D, (g + 1) * D)
        local += [
            pltpu.make_async_copy(k_hbm.at[:, cols], kvb.at[g, :, 0:D], in_sem.at[4 + 3 * g]),
            pltpu.make_async_copy(v_hbm.at[:, cols], kvb.at[g, :, D:], in_sem.at[5 + 3 * g]),
            pltpu.make_async_copy(
                q_hbm.at[:, g * WIDE : (g + 1) * WIDE], qb.at[g], in_sem.at[6 + 3 * g]
            ),
        ]
    for c in local[4:] + local[:4]:
        c.start()

    local[0].wait()
    order = ffn_ref[...].astype(F32)
    p_ffn = (order == iota((D, D), 0).astype(F32)).astype(BF)
    p_out[...] = p_ffn
    gather_ffn = p_ffn.T
    local[1].wait()
    packed = dot(gather_ffn, gin[...], 1, 0).astype(BF)
    for g in range(KV):
        snd1[g * D : (g + 1) * D, :] = packed[:, g * WIDE : (g + 1) * WIDE]

    for c in local[2:]:
        c.wait()
    kvw[4 + x] = kvb[x]
    qst[x] = qb[x]

    pl.semaphore_wait(barrier, N - 1)

    def order_copy(i):
        return remote(att_ref.at[x], att_ref.at[x], att_s.at[i], att_r.at[i], z * KV + ((x + i) & 3))

    def order_arrived(i):
        u = (x + 4 - i) & 3
        return remote(att_ref.at[u], att_ref.at[u], att_s.at[i], att_r.at[i], me ^ 1)

    for i in (1, 2, 3):
        order_copy(i).start()

    def kv_copy(i):
        g = (x + i) & 3
        return remote(kvb.at[g], kvw.at[4 + x], kv_s.at[i], kv_r.at[x], z * KV + g)

    def kv_arrived(i):
        u = (x + i) & 3
        remote(kvb.at[u], kvw.at[4 + u], kv_s.at[i], kv_r.at[u], z * KV + u).wait_recv()

    kv_down = remote(kvw.at[4:7], kvw.at[8:11], kz_s.at[0], kz_r.at[0], below + x)
    kv_up = remote(kvw.at[5:8, 0:HALF], kvw.at[1:4, 0:HALF], kz_s.at[1], kz_r.at[1], above + x)

    for i in (2, 1, 3):
        kv_copy(i).start()

    def q_copy(i):
        g = (x + i) & 3
        return remote(qb.at[g], qst.at[x], q_s.at[i], q_r.at[x], z * KV + g)

    for i in (1, 3):
        q_copy(i).start()

    def rows_at(i):
        return pl.ds(pl.multiple_of(i * CHUNK, CHUNK), CHUNK)

    def token_row(peer):
        return pl.ds(pl.multiple_of((peer & 3) * D + (peer >> 2) * CHUNK, CHUNK), CHUNK)

    def send_column(src, dst, src_at, dst_at, s, r, dx):
        def one(i, _):
            peer = ((z + (0x07162534 >> (4 * i))) & 7) * KV + ((x + dx) & 3)
            remote(src.at[src_at(peer)], dst.at[dst_at(me)], s, r, peer).start()
            return 0

        lax.fori_loop(0, 8 if dx else 7, one, 0)

    def send1(dx):
        send_column(snd1, rcv1, token_row, rows_at, a1_s, a1_r, dx)

    send1(0)
    rcv1[rows_at(me), :] = snd1[token_row(me), :]

    def whole(src, dst, s, r):
        n = ROWS - CHUNK
        return remote(src.at[:n], dst.at[:n], s, r, lax.rem(me + 1, N))

    kk, qq = iota((D, D), 0), iota((D, D), 1)
    for u in range(KV):
        d = z * KV + u
        first, end, start = 0, 0, 0
        for t in range(16):
            stop = start + sizes[t]
            inside = (start <= d) & (d < stop)
            first = jnp.where(inside, start, first)
            end = jnp.where(inside, stop, end)
            start = stop
        bias[u, 0:D, :] = jnp.where(kk <= qq, 0.0, NEG)
        for r in (1, 2, 3):
            flag[u * KV + r] = jnp.where(d + r < end, 1, 0)
            later = jnp.where(d + r < end, 0.0, NEG)
            earlier = jnp.where(d + r - 4 >= first, 0.0, NEG)
            bias[u, r * D : (r + 1) * D, :] = jnp.maximum(
                jnp.where(qq >= HALF, later, NEG), jnp.where(kk < HALF, earlier, NEG)
            )
    for i in (1, 3, 2):
        kv_arrived(i)
    kv_down.start()
    kv_up.start()
    q_copy(2).start()
    for dx in (1, 3, 2):
        send1(dx)
    accw[...] = jnp.zeros_like(accw)
    invs[...] = jnp.zeros_like(invs)

    for i in (1, 2, 3):
        order_arrived(i).wait_recv()
    orders = jnp.concatenate([att_ref[u] for u in range(KV)], axis=1)
    orders = jnp.broadcast_to(orders.astype(F32).astype(BF), (D, KV * D))
    pick = picks()
    m_att[...] = scatter_matrix(orders, pick)
    mt_att[...] = gather_matrix(orders, pick)

    kv_down.wait_recv()
    kv_up.wait_recv()

    def forward(i, _):
        u = (x + (0xB4 >> (2 * i))) & 3

        @pl.when(i > 0)
        def _():
            remote(qb.at[0], qst.at[u], q_s.at[0], q_r.at[u], me ^ 1).wait_recv()

        kall[u, 0:D, :] = kvw[4 + u]
        for r in (1, 2, 3):
            kall[u, r * D : r * D + HALF, :] = jnp.where(
                flag[u * KV + r] > 0, kvw[4 + u + r, 0:HALF, :], kvw[u + r, 0:HALF, :]
            )
            kall[u, r * D + HALF : (r + 1) * D, :] = kvw[4 + u + r, HALF:D, :]
        keys, values = kall[u, :, 0:D], kall[u, :, D : 2 * D]
        sc[...] = dot(keys, heads(qst[u]), 1, 1)

        blocks = [slice(b, b + STEP) for b in range(0, KEYS, STEP)]

        def masked(rows):
            return sc[rows, :] + jnp.concatenate([bias[u, rows, :]] * GR, axis=1)

        top = jnp.full((8, WIDE), NEG, F32)
        for rows in blocks:
            top = jnp.maximum(top, jnp.max(masked(rows).reshape(STEP // 8, 8, WIDE), axis=0))
        top = jnp.max(top, axis=0, keepdims=True)
        total = jnp.zeros((8, WIDE), F32)
        for rows in blocks:
            p = jnp.exp2((masked(rows) - top) * (scale * math.log2(math.e)))
            prob[u, rows, :] = p.astype(BF)
            total = total + jnp.sum(p.reshape(STEP // 8, 8, WIDE), axis=0)
        inv = 1.0 / jnp.sum(total, axis=0, keepdims=True)
        o = (dot(values.T, prob[u], 1, 0) * inv).astype(BF)
        for a in range(GR):
            cols = slice(a * D, (a + 1) * D)
            ott[cols, lanes(u, D)] = o[:, cols]
            invs[u, a : a + 1, :] = inv[:, cols]
        return 0

    lax.fori_loop(0, KV, forward, 0)

    snd2[...] = dot(mt_att[...], ott[...], 1, 1).astype(BF)

    for dx in (2, 1, 3, 0):
        send_column(snd2, rcv2, rows_at, token_row, a2_s, a2_r, dx)
    rcv2[token_row(me), :] = snd2[rows_at(me), :]

    whole(snd1, rcv1, a1_s, a1_r).wait_recv()
    every = dot(m_att[...], rcv1[...], 1, 0)
    for u in range(KV):
        up = every[u * D : (u + 1) * D]
        inv = invs[u].T
        for a in range(GR):
            cols = slice(a * D, (a + 1) * D)
            dos[u, :, cols] = (up[:, cols] * inv[:, a : a + 1]).astype(BF)

    def dq_copy(u):
        return remote(dqs.at[u], qg.at[x], dq_s.at[u], dq_r.at[x], z * KV + u)

    def backward(i, _):
        u = (x + 1 + i) & 3
        keys, values = kall[u, :, 0:D], kall[u, :, D : 2 * D]
        sc[...] = dot(values, heads(dos[u]), 1, 1)

        blocks = [slice(b, b + STEP) for b in range(0, KEYS, STEP)]
        total = jnp.zeros((8, WIDE), F32)
        for rows in blocks:
            t = prob[u, rows, :].astype(F32) * sc[rows, :]
            total = total + jnp.sum(t.reshape(STEP // 8, 8, WIDE), axis=0)
        inv = jnp.concatenate([invs[u, a : a + 1, :] for a in range(GR)], axis=1)
        delta = jnp.sum(total, axis=0, keepdims=True) * inv

        for rows in blocks:
            dsb[rows, :] = (prob[u, rows, :].astype(F32) * (sc[rows, :] - delta)).astype(BF)
        dq = dot(keys.T, dsb[...], 1, 0) * scale
        for a in range(GR):
            cols = slice(a * D, (a + 1) * D)
            dqs[u, :, cols] = dq[:, cols].T.astype(BF)

        @pl.when(i < 3)
        def _():
            dq_copy(u).start()

        kpart = dot(dsb[...], heads(qst[u]), 1, 0) * scale
        vpart = dot(prob[u], heads(dos[u]), 1, 0)
        part = jnp.concatenate([kpart, vpart], axis=1)
        accw[4 + u] += part[0:D]
        for r in (1, 2, 3):
            later = flag[u * KV + r] > 0
            accw[4 + u + r] += jnp.where(later, part[r * D : (r + 1) * D], 0.0)
            accw[u + r, 0:HALF, :] += jnp.where(later, 0.0, part[r * D : r * D + HALF])
        return 0

    lax.fori_loop(0, KV, backward, 0)
    qg[x] = dqs[x]

    for e in range(1, 11):
        gsend[e] = accw[e].astype(BF)

    def g_copy(e):
        g = e & 3
        if e < 4:
            return remote(gsend.at[e, 0:HALF], gdn.at[x], g_s.at[e], g_r.at[0, x], below + g)
        if e < 8:
            return remote(gsend.at[e], grow.at[x], g_s.at[e], g_r.at[1, x], z * KV + g)
        return remote(gsend.at[e], gup.at[x], g_s.at[e], g_r.at[2, x], above + g)

    for e in (8, 9, 10, 1, 2, 3):
        g_copy(e).start()
    for e in range(4, 8):
        pl.when(x != e - 4)(g_copy(e).start)
    grow[x] = gsend[4 + x]

    whole(snd2, rcv2, a2_s, a2_r).wait_recv()
    for g in range(KV):
        pl.when(x != g)(
            remote(gsend.at[4], grow.at[g], g_s.at[0], g_r.at[1, g], me ^ 1).wait_recv
        )
        pl.when(x <= 2)(remote(gsend.at[4], gup.at[g], g_s.at[0], g_r.at[2, g], me ^ 1).wait_recv)
        pl.when(x >= 1)(
            remote(gsend.at[4, 0:HALF], gdn.at[g], g_s.at[0], g_r.at[0, g], me ^ 1).wait_recv
        )

    for i in (1, 2, 3):
        order_copy(i).wait_send()
        kv_copy(i).wait_send()
        q_copy(i).wait_send()
    kv_down.wait_send()
    kv_up.wait_send()
    whole(snd1, rcv1, a1_s, a1_r).wait_send()
    whole(snd2, rcv2, a2_s, a2_r).wait_send()
    for e in (8, 9, 10, 1, 2, 3):
        g_copy(e).wait_send()
    for u in range(KV):

        @pl.when(x != u)
        def _():
            g_copy(4 + u).wait_send()
            dq_copy(u).wait_send()
            remote(dqs.at[u], qg.at[u], dq_s.at[u], dq_r.at[u], me ^ 1).wait_recv()


def finish(
    got, qg, grow, gup, gdn, p_ffn,
    out_hbm, qg_hbm, kg_hbm, vg_hbm,
    out_v, kg_v, vg_v, sem,
):
    x = lax.axis_index("ctx") & 3
    outs = []

    def send(src, dst):
        outs.append(pltpu.make_async_copy(src, dst, sem.at[len(outs)]))
        outs[-1].start()

    for g in range(KV):
        send(qg.at[g], qg_hbm.at[:, g * WIDE : (g + 1) * WIDE])
    for g in range(KV):
        total = grow[g].astype(F32) + jnp.where(x <= 2, gup[g].astype(F32), 0.0)
        low = total[0:HALF] + jnp.where(x >= 1, gdn[g].astype(F32), 0.0)
        high = total[HALF:D]
        cols = slice(g * D, (g + 1) * D)
        for ref, lane in ((kg_v, 0), (vg_v, D)):
            ref[0:HALF, cols] = low[:, lane : lane + D].astype(BF)
            ref[HALF:D, cols] = high[:, lane : lane + D].astype(BF)
    send(kg_v, kg_hbm)
    send(vg_v, vg_hbm)
    for g in range(KV):
        cols = slice(g * WIDE, (g + 1) * WIDE)
        out_v[:, cols] = dot(p_ffn[...], got[g * D : (g + 1) * D, :], 1, 0).astype(BF)
        send(out_v.at[:, cols], out_hbm.at[:, cols])
    for c in outs:
        c.wait()


def body(q, k, v, g, sizes, ffn_order, attn_order):
    hbm = pl.BlockSpec(memory_space=pltpu.HBM)
    vmem = pl.BlockSpec(memory_space=pltpu.VMEM)
    dma = pltpu.SemaphoreType.DMA
    vm = pltpu.VMEM
    got, qg, row, up, down, p_ffn = pl.pallas_call(
        kernel,
        out_shape=(
            vm((ROWS, WIDE), BF),
            vm((KV, D, WIDE), BF),
            vm((KV, D, 2 * D), BF),
            vm((KV, D, 2 * D), BF),
            vm((KV, HALF, 2 * D), BF),
            vm((D, D), BF),
        ),
        in_specs=[hbm] * 7,
        out_specs=(vmem,) * 6,
        scratch_shapes=[
            pltpu.SMEM((16,), jnp.int32),
            vm((1, D), jnp.int32),
            vm((KV, 1, D), jnp.int32),
            vm((KV, D, WIDE), BF),
            vm((KV, D, 2 * D), BF),
            vm((KV, D, WIDE), BF),
            vm((12, D, 2 * D), BF),
            vm((KV, KEYS, 2 * D), BF),
            vm((KV, KEYS, WIDE), BF),
            vm((D, KV * WIDE), BF),
            vm((ROWS, WIDE), BF),
            vm((ROWS, WIDE), BF),
            vm((ROWS, WIDE), BF),
            vm((KV * D, ROWS), BF),
            vm((ROWS, KV * D), BF),
            vm((WIDE, KV * D), BF),
            vm((KV, D, WIDE), BF),
            vm((KEYS, WIDE), F32),
            vm((KEYS, WIDE), BF),
            vm((KV, D, WIDE), BF),
            vm((12, D, 2 * D), F32),
            vm((12, D, 2 * D), BF),
            vm((KV, KEYS, D), F32),
            vm((KV, 8, D), F32),
            pltpu.SMEM((KV * KV,), jnp.int32),
            dma((16,)),
            dma((4,)),
            dma((4,)),
            dma((4,)),
            dma((4,)),
            dma((2,)),
            dma((2,)),
            dma((4,)),
            dma((4,)),
            dma((4,)),
            dma((4,)),
            dma((12,)),
            dma((3, 4)),
            dma,
            dma,
            dma,
            dma,
        ],
        compiler_params=pltpu.CompilerParams(
            collective_id=0, has_side_effects=True, vmem_limit_bytes=56 * 1024 * 1024
        ),
    )(q, k, v, g, sizes, ffn_order, attn_order)
    return pl.pallas_call(
        finish,
        out_shape=(
            jax.ShapeDtypeStruct((D, KV * WIDE), BF),
            jax.ShapeDtypeStruct((D, KV * WIDE), BF),
            jax.ShapeDtypeStruct((D, KV * D), BF),
            jax.ShapeDtypeStruct((D, KV * D), BF),
        ),
        in_specs=[vmem] * 6,
        out_specs=(hbm,) * 4,
        scratch_shapes=[
            vm((D, KV * WIDE), BF),
            vm((D, KV * D), BF),
            vm((D, KV * D), BF),
            dma((10,)),
        ],
        compiler_params=pltpu.CompilerParams(vmem_limit_bytes=8 * 1024 * 1024),
    )(got, qg, row, up, down, p_ffn)


def solution(mesh):
    rows = P(("dp", "ctx"), None)
    return jax.shard_map(
        body,
        mesh=mesh,
        in_specs=(rows, rows, rows, rows, P("dp"), rows, rows),
        out_specs=(rows,) * 4,
        check_vma=False,
    )
```

```python
import math

import jax
import jax.numpy as jnp
from jax import lax
from jax.experimental import pallas as pl
from jax.experimental.pallas import tpu as pltpu
from jax.sharding import PartitionSpec as P

MESH = pl.DeviceIdType.MESH
D = 128
HALF = 64
KV = 4
GR = 5
N = 32
CHUNK = 16
ROWS = N * CHUNK
WIDE = GR * D
KEYS = 4 * D
NEG = -1e30
STEP = 32
BF, F32 = jnp.bfloat16, jnp.float32


def dot(a, b, ca, cb):
    return lax.dot_general(a, b, (((ca,), (cb,)), ((), ())), preferred_element_type=F32)


def iota(shape, dim):
    return lax.broadcasted_iota(jnp.int32, shape, dim)


def picks():
    c, l = iota((ROWS, D), 0), iota((ROWS, D), 1)
    entry = (l == (c >> 4) * 4 + (c & 3)).astype(F32)
    device = (c >> 2) & 3
    return jnp.concatenate(
        [jnp.where(device == u, entry, 0.0).astype(BF) for u in range(KV)], axis=1
    )


def scatter_matrix(orders, pick):
    row, c = iota((D, ROWS), 0), iota((D, ROWS), 1)
    target = dot(orders, pick, 1, 1) + (((c >> 2) & 3) * D).astype(F32)
    row = row.astype(F32)
    return jnp.concatenate([(target == row + float(t * D)).astype(BF) for t in range(KV)], axis=0)


def gather_matrix(orders, pick):
    c, lane = iota((ROWS, D), 0), iota((ROWS, D), 1)
    target = dot(pick, orders, 1, 1) + (((c >> 2) & 3) * D).astype(F32)
    lane = lane.astype(F32)
    return jnp.concatenate([(target == lane + float(t * D)).astype(BF) for t in range(KV)], axis=1)


def heads(x):
    return jnp.concatenate([x[:, a * D : (a + 1) * D] for a in range(GR)], axis=0)


def kernel(
    q_hbm, k_hbm, v_hbm, g_hbm, sizes_hbm, ffn_hbm, att_hbm,
    rcv2, qg, grow, gup, gdn, p_out,
    sizes, ffn_ref, att_ref, qb, kvb, qst, kvw, kall, prob, gin, snd1, rcv1, snd2,
    m_att, mt_att, ott, dos, sc, dsb, dqs, accw, gsend, bias, invs, flag,
    in_sem, att_s, att_r, kv_s, kv_r, kz_s, kz_r, f_s, f_r, q_s, q_r, dq_s, dq_r, g_s, g_r,
    a1_s, a1_r, a2_s, a2_r,
):
    dp = lax.axis_index("dp")
    me = lax.axis_index("ctx")
    z, x = me >> 2, me & 3
    above, below = ((z + 1) & 7) * KV, ((z + 7) & 7) * KV
    scale = 1.0 / math.sqrt(D)

    def remote(src, dst, s, r, peer):
        return pltpu.make_async_remote_copy(
            src_ref=src, dst_ref=dst, send_sem=s, recv_sem=r,
            device_id=(dp, peer), device_id_type=MESH,
        )

    def lanes(i, width):
        return pl.ds(pl.multiple_of(i * width, D), width)

    barrier = pltpu.get_barrier_semaphore()

    def greet(i, _):
        pl.semaphore_signal(
            barrier, inc=1, device_id=(dp, lax.rem(me + i, N)), device_id_type=MESH
        )
        return 0

    lax.fori_loop(1, N, greet, 0)

    local = [
        pltpu.make_async_copy(ffn_hbm, ffn_ref, in_sem.at[0]),
        pltpu.make_async_copy(g_hbm, gin, in_sem.at[1]),
        pltpu.make_async_copy(att_hbm, att_ref.at[x], in_sem.at[2]),
        pltpu.make_async_copy(sizes_hbm, sizes, in_sem.at[3]),
    ]
    for g in range(KV):
        cols = slice(g * D, (g + 1) * D)
        local += [
            pltpu.make_async_copy(k_hbm.at[:, cols], kvb.at[g, :, 0:D], in_sem.at[4 + 3 * g]),
            pltpu.make_async_copy(v_hbm.at[:, cols], kvb.at[g, :, D:], in_sem.at[5 + 3 * g]),
            pltpu.make_async_copy(
                q_hbm.at[:, g * WIDE : (g + 1) * WIDE], qb.at[g], in_sem.at[6 + 3 * g]
            ),
        ]
    for c in local[4:] + local[:4]:
        c.start()

    for c in local[2:]:
        c.wait()
    kvw[4 + x] = kvb[x]
    qst[x] = qb[x]

    pl.semaphore_wait(barrier, N - 1)

    def order_copy(i):
        return remote(att_ref.at[x], att_ref.at[x], att_s.at[i], att_r.at[i], z * KV + ((x + i) & 3))

    def order_arrived(i):
        u = (x + 4 - i) & 3
        return remote(att_ref.at[u], att_ref.at[u], att_s.at[i], att_r.at[i], me ^ 1)

    for i in (1, 2, 3):
        order_copy(i).start()

    def kv_copy(i):
        g = (x + i) & 3
        return remote(kvb.at[g], kvw.at[4 + x], kv_s.at[i], kv_r.at[x], z * KV + g)

    def kv_arrived(i):
        u = (x + i) & 3
        remote(kvb.at[u], kvw.at[4 + u], kv_s.at[i], kv_r.at[u], z * KV + u).wait_recv()

    kv_down = remote(kvw.at[4:7], kvw.at[8:11], kz_s.at[0], kz_r.at[0], below + x)
    kv_up = remote(kvw.at[5:8, 0:HALF], kvw.at[1:4, 0:HALF], kz_s.at[1], kz_r.at[1], above + x)

    for i in (2, 1, 3):
        kv_copy(i).start()

    def q_copy(i):
        g = (x + i) & 3
        return remote(qb.at[g], qst.at[x], q_s.at[i], q_r.at[x], z * KV + g)

    QUARTER = D // 4

    def far_copy(k):
        rows = slice(k * QUARTER, (k + 1) * QUARTER)
        g = x ^ 2
        return remote(qb.at[g, rows], qst.at[x, rows], f_s.at[k], f_r.at[k], z * KV + g)

    for i in (1, 3):
        q_copy(i).start()

    local[0].wait()
    order = ffn_ref[...].astype(F32)
    p_ffn = (order == iota((D, D), 0).astype(F32)).astype(BF)
    p_out[...] = p_ffn
    gather_ffn = p_ffn.T
    local[1].wait()
    packed = dot(gather_ffn, gin[...], 1, 0).astype(BF)
    for g in range(KV):
        snd1[g * D : (g + 1) * D, :] = packed[:, g * WIDE : (g + 1) * WIDE]

    def rows_at(i):
        return pl.ds(pl.multiple_of(i * CHUNK, CHUNK), CHUNK)

    def token_row(peer):
        return pl.ds(pl.multiple_of((peer & 3) * D + (peer >> 2) * CHUNK, CHUNK), CHUNK)

    def send_column(src, dst, src_at, dst_at, s, r, dx):
        def one(i, _):
            peer = ((z + (0x07162534 >> (4 * i))) & 7) * KV + ((x + dx) & 3)
            remote(src.at[src_at(peer)], dst.at[dst_at(me)], s, r, peer).start()
            return 0

        lax.fori_loop(0, 8 if dx else 7, one, 0)

    def send1(dx):
        send_column(snd1, rcv1, token_row, rows_at, a1_s, a1_r, dx)

    send1(0)
    rcv1[rows_at(me), :] = snd1[token_row(me), :]

    def whole(src, dst, s, r):
        n = ROWS - CHUNK
        return remote(src.at[:n], dst.at[:n], s, r, lax.rem(me + 1, N))

    kk, qq = iota((D, D), 0), iota((D, D), 1)
    for u in range(KV):
        d = z * KV + u
        first, end, start = 0, 0, 0
        for t in range(16):
            stop = start + sizes[t]
            inside = (start <= d) & (d < stop)
            first = jnp.where(inside, start, first)
            end = jnp.where(inside, stop, end)
            start = stop
        bias[u, 0:D, :] = jnp.where(kk <= qq, 0.0, NEG)
        for r in (1, 2, 3):
            flag[u * KV + r] = jnp.where(d + r < end, 1, 0)
            later = jnp.where(d + r < end, 0.0, NEG)
            earlier = jnp.where(d + r - 4 >= first, 0.0, NEG)
            bias[u, r * D : (r + 1) * D, :] = jnp.maximum(
                jnp.where(qq >= HALF, later, NEG), jnp.where(kk < HALF, earlier, NEG)
            )
    for i in (1, 3, 2):
        kv_arrived(i)
    kv_down.start()
    kv_up.start()
    for k in range(4):
        far_copy(k).start()
    for dx in (1, 3, 2):
        send1(dx)
    accw[...] = jnp.zeros_like(accw)
    invs[...] = jnp.zeros_like(invs)

    for i in (1, 2, 3):
        order_arrived(i).wait_recv()
    orders = jnp.concatenate([att_ref[u] for u in range(KV)], axis=1)
    orders = jnp.broadcast_to(orders.astype(F32).astype(BF), (D, KV * D))
    pick = picks()
    m_att[...] = scatter_matrix(orders, pick)
    mt_att[...] = gather_matrix(orders, pick)

    kv_down.wait_recv()
    kv_up.wait_recv()

    def forward(i, _):
        u = (x + (0xB4 >> (2 * i))) & 3

        @pl.when((i == 1) | (i == 2))
        def _():
            remote(qb.at[0], qst.at[u], q_s.at[0], q_r.at[u], me ^ 1).wait_recv()

        @pl.when(i == 3)
        def _():
            for k in range(4):
                far_copy(k).wait_recv()

        kall[u, 0:D, :] = kvw[4 + u]
        for r in (1, 2, 3):
            kall[u, r * D : r * D + HALF, :] = jnp.where(
                flag[u * KV + r] > 0, kvw[4 + u + r, 0:HALF, :], kvw[u + r, 0:HALF, :]
            )
            kall[u, r * D + HALF : (r + 1) * D, :] = kvw[4 + u + r, HALF:D, :]
        keys, values = kall[u, :, 0:D], kall[u, :, D : 2 * D]
        sc[...] = dot(keys, heads(qst[u]), 1, 1)

        blocks = [slice(b, b + STEP) for b in range(0, KEYS, STEP)]

        def masked(rows):
            return sc[rows, :] + jnp.concatenate([bias[u, rows, :]] * GR, axis=1)

        top = jnp.full((8, WIDE), NEG, F32)
        for rows in blocks:
            top = jnp.maximum(top, jnp.max(masked(rows).reshape(STEP // 8, 8, WIDE), axis=0))
        top = jnp.max(top, axis=0, keepdims=True)
        total = jnp.zeros((8, WIDE), F32)
        for rows in blocks:
            p = jnp.exp2((masked(rows) - top) * (scale * math.log2(math.e)))
            prob[u, rows, :] = p.astype(BF)
            total = total + jnp.sum(p.reshape(STEP // 8, 8, WIDE), axis=0)
        inv = 1.0 / jnp.sum(total, axis=0, keepdims=True)
        o = (dot(values.T, prob[u], 1, 0) * inv).astype(BF)
        for a in range(GR):
            cols = slice(a * D, (a + 1) * D)
            ott[cols, lanes(u, D)] = o[:, cols]
            invs[u, a : a + 1, :] = inv[:, cols]
        return 0

    lax.fori_loop(0, KV, forward, 0)

    snd2[...] = dot(mt_att[...], ott[...], 1, 1).astype(BF)

    for dx in (2, 1, 3, 0):
        send_column(snd2, rcv2, rows_at, token_row, a2_s, a2_r, dx)
    rcv2[token_row(me), :] = snd2[rows_at(me), :]

    whole(snd1, rcv1, a1_s, a1_r).wait_recv()
    every = dot(m_att[...], rcv1[...], 1, 0)
    for u in range(KV):
        up = every[u * D : (u + 1) * D]
        inv = invs[u].T
        for a in range(GR):
            cols = slice(a * D, (a + 1) * D)
            dos[u, :, cols] = (up[:, cols] * inv[:, a : a + 1]).astype(BF)

    def dq_copy(u):
        return remote(dqs.at[u], qg.at[x], dq_s.at[u], dq_r.at[x], z * KV + u)

    def add_part(part, u, term):
        accw[part, 4 + u] += term[0:D]
        for r in (1, 2, 3):
            later = flag[u * KV + r] > 0
            accw[part, 4 + u + r] += jnp.where(later, term[r * D : (r + 1) * D], 0.0)
            accw[part, u + r, 0:HALF, :] += jnp.where(later, 0.0, term[r * D : r * D + HALF])

    def g_copy(part, e):
        g, s = e & 3, g_s.at[part, e]
        if e < 4:
            return remote(gsend.at[part, e, 0:HALF], gdn.at[x, part], s, g_r.at[0, part, x], below + g)
        if e < 8:
            return remote(gsend.at[part, e], grow.at[x, part], s, g_r.at[1, part, x], z * KV + g)
        return remote(gsend.at[part, e], gup.at[x, part], s, g_r.at[2, part, x], above + g)

    def g_all(part, action):
        for e in (8, 9, 10, 1, 2, 3):
            action(g_copy(part, e))
        for e in range(4, 8):

            @pl.when(x != e - 4)
            def _():
                action(g_copy(part, e))

    def send_terms(part):
        for e in range(1, 11):
            gsend[part, e] = accw[part, e].astype(BF)
        g_all(part, lambda c: c.start())
        grow[x, part] = gsend[part, 4 + x]

    def value_terms(u, _):
        add_part(1, u, dot(prob[u], heads(dos[u]), 1, 0))
        return 0

    lax.fori_loop(0, KV, value_terms, 0)
    send_terms(1)

    def backward(i, _):
        u = (x + 1 + i) & 3
        keys, values = kall[u, :, 0:D], kall[u, :, D : 2 * D]
        sc[...] = dot(values, heads(dos[u]), 1, 1)

        blocks = [slice(b, b + STEP) for b in range(0, KEYS, STEP)]
        total = jnp.zeros((8, WIDE), F32)
        for rows in blocks:
            t = prob[u, rows, :].astype(F32) * sc[rows, :]
            total = total + jnp.sum(t.reshape(STEP // 8, 8, WIDE), axis=0)
        inv = jnp.concatenate([invs[u, a : a + 1, :] for a in range(GR)], axis=1)
        delta = jnp.sum(total, axis=0, keepdims=True) * inv

        for rows in blocks:
            dsb[rows, :] = (prob[u, rows, :].astype(F32) * (sc[rows, :] - delta)).astype(BF)
        dq = dot(keys.T, dsb[...], 1, 0) * scale
        for a in range(GR):
            cols = slice(a * D, (a + 1) * D)
            dqs[u, :, cols] = dq[:, cols].T.astype(BF)

        @pl.when(i < 3)
        def _():
            dq_copy(u).start()

        add_part(0, u, dot(dsb[...], heads(qst[u]), 1, 0) * scale)
        return 0

    lax.fori_loop(0, KV, backward, 0)
    qg[x] = dqs[x]

    send_terms(0)

    whole(snd2, rcv2, a2_s, a2_r).wait_recv()
    for part in (1, 0):
        for g in range(KV):
            pl.when(x != g)(
                remote(
                    gsend.at[0, 4], grow.at[g, part], g_s.at[0, 0], g_r.at[1, part, g], me ^ 1
                ).wait_recv
            )
            pl.when(x <= 2)(
                remote(
                    gsend.at[0, 4], gup.at[g, part], g_s.at[0, 0], g_r.at[2, part, g], me ^ 1
                ).wait_recv
            )
            pl.when(x >= 1)(
                remote(
                    gsend.at[0, 4, 0:HALF], gdn.at[g, part], g_s.at[0, 0], g_r.at[0, part, g], me ^ 1
                ).wait_recv
            )

    for i in (1, 2, 3):
        order_copy(i).wait_send()
        kv_copy(i).wait_send()
    for i in (1, 3):
        q_copy(i).wait_send()
    for k in range(4):
        far_copy(k).wait_send()
    kv_down.wait_send()
    kv_up.wait_send()
    whole(snd1, rcv1, a1_s, a1_r).wait_send()
    whole(snd2, rcv2, a2_s, a2_r).wait_send()
    for part in (0, 1):
        g_all(part, lambda c: c.wait_send())
    for u in range(KV):

        @pl.when(x != u)
        def _():
            dq_copy(u).wait_send()
            remote(dqs.at[u], qg.at[u], dq_s.at[u], dq_r.at[u], me ^ 1).wait_recv()


def finish(
    got, qg, grow, gup, gdn, p_ffn,
    out_hbm, qg_hbm, kg_hbm, vg_hbm,
    out_v, kg_v, vg_v, sem,
):
    x = lax.axis_index("ctx") & 3
    outs = []

    def send(src, dst):
        outs.append(pltpu.make_async_copy(src, dst, sem.at[len(outs)]))
        outs[-1].start()

    for g in range(KV):
        send(qg.at[g], qg_hbm.at[:, g * WIDE : (g + 1) * WIDE])
    for g in range(KV):
        cols = slice(g * D, (g + 1) * D)
        for part, ref in ((0, kg_v), (1, vg_v)):
            total = grow[g, part].astype(F32) + jnp.where(x <= 2, gup[g, part].astype(F32), 0.0)
            low = total[0:HALF] + jnp.where(x >= 1, gdn[g, part].astype(F32), 0.0)
            ref[0:HALF, cols] = low.astype(BF)
            ref[HALF:D, cols] = total[HALF:D].astype(BF)
    send(kg_v, kg_hbm)
    send(vg_v, vg_hbm)
    for g in range(KV):
        cols = slice(g * WIDE, (g + 1) * WIDE)
        out_v[:, cols] = dot(p_ffn[...], got[g * D : (g + 1) * D, :], 1, 0).astype(BF)
        send(out_v.at[:, cols], out_hbm.at[:, cols])
    for c in outs:
        c.wait()


def body(q, k, v, g, sizes, ffn_order, attn_order):
    hbm = pl.BlockSpec(memory_space=pltpu.HBM)
    vmem = pl.BlockSpec(memory_space=pltpu.VMEM)
    dma = pltpu.SemaphoreType.DMA
    vm = pltpu.VMEM
    got, qg, row, up, down, p_ffn = pl.pallas_call(
        kernel,
        out_shape=(
            vm((ROWS, WIDE), BF),
            vm((KV, D, WIDE), BF),
            vm((KV, 2, D, D), BF),
            vm((KV, 2, D, D), BF),
            vm((KV, 2, HALF, D), BF),
            vm((D, D), BF),
        ),
        in_specs=[hbm] * 7,
        out_specs=(vmem,) * 6,
        scratch_shapes=[
            pltpu.SMEM((16,), jnp.int32),
            vm((1, D), jnp.int32),
            vm((KV, 1, D), jnp.int32),
            vm((KV, D, WIDE), BF),
            vm((KV, D, 2 * D), BF),
            vm((KV, D, WIDE), BF),
            vm((12, D, 2 * D), BF),
            vm((KV, KEYS, 2 * D), BF),
            vm((KV, KEYS, WIDE), BF),
            vm((D, KV * WIDE), BF),
            vm((ROWS, WIDE), BF),
            vm((ROWS, WIDE), BF),
            vm((ROWS, WIDE), BF),
            vm((KV * D, ROWS), BF),
            vm((ROWS, KV * D), BF),
            vm((WIDE, KV * D), BF),
            vm((KV, D, WIDE), BF),
            vm((KEYS, WIDE), F32),
            vm((KEYS, WIDE), BF),
            vm((KV, D, WIDE), BF),
            vm((2, 12, D, D), F32),
            vm((2, 12, D, D), BF),
            vm((KV, KEYS, D), F32),
            vm((KV, 8, D), F32),
            pltpu.SMEM((KV * KV,), jnp.int32),
            dma((16,)),
            dma((4,)),
            dma((4,)),
            dma((4,)),
            dma((4,)),
            dma((2,)),
            dma((2,)),
            dma((4,)),
            dma((4,)),
            dma((4,)),
            dma((4,)),
            dma((4,)),
            dma((4,)),
            dma((2, 12)),
            dma((3, 2, 4)),
            dma,
            dma,
            dma,
            dma,
        ],
        compiler_params=pltpu.CompilerParams(
            collective_id=0, has_side_effects=True, vmem_limit_bytes=56 * 1024 * 1024
        ),
    )(q, k, v, g, sizes, ffn_order, attn_order)
    return pl.pallas_call(
        finish,
        out_shape=(
            jax.ShapeDtypeStruct((D, KV * WIDE), BF),
            jax.ShapeDtypeStruct((D, KV * WIDE), BF),
            jax.ShapeDtypeStruct((D, KV * D), BF),
            jax.ShapeDtypeStruct((D, KV * D), BF),
        ),
        in_specs=[vmem] * 6,
        out_specs=(hbm,) * 4,
        scratch_shapes=[
            vm((D, KV * WIDE), BF),
            vm((D, KV * D), BF),
            vm((D, KV * D), BF),
            dma((10,)),
        ],
        compiler_params=pltpu.CompilerParams(vmem_limit_bytes=8 * 1024 * 1024),
    )(got, qg, row, up, down, p_ffn)


def solution(mesh):
    rows = P(("dp", "ctx"), None)
    return jax.shard_map(
        body,
        mesh=mesh,
        in_specs=(rows, rows, rows, rows, P("dp"), rows, rows),
        out_specs=(rows,) * 4,
        check_vma=False,
    )
```

```python
import math

import jax
import jax.numpy as jnp
from jax import lax
from jax.experimental import pallas as pl
from jax.experimental.pallas import tpu as pltpu
from jax.sharding import PartitionSpec as P

MESH = pl.DeviceIdType.MESH
D = 128
HALF = 64
KV = 4
GR = 5
N = 32
CHUNK = 16
ROWS = N * CHUNK
WIDE = GR * D
KEYS = 4 * D
NEG = -1e30
STEP = 32
BF, F32 = jnp.bfloat16, jnp.float32


def dot(a, b, ca, cb):
    return lax.dot_general(a, b, (((ca,), (cb,)), ((), ())), preferred_element_type=F32)


def iota(shape, dim):
    return lax.broadcasted_iota(jnp.int32, shape, dim)


def picks():
    c, l = iota((ROWS, D), 0), iota((ROWS, D), 1)
    entry = (l == (c >> 4) * 4 + (c & 3)).astype(F32)
    device = (c >> 2) & 3
    return jnp.concatenate(
        [jnp.where(device == u, entry, 0.0).astype(BF) for u in range(KV)], axis=1
    )


def scatter_matrix(orders, pick):
    row, c = iota((D, ROWS), 0), iota((D, ROWS), 1)
    target = dot(orders, pick, 1, 1) + (((c >> 2) & 3) * D).astype(F32)
    row = row.astype(F32)
    return jnp.concatenate([(target == row + float(t * D)).astype(BF) for t in range(KV)], axis=0)


def gather_matrix(orders, pick):
    c, lane = iota((ROWS, D), 0), iota((ROWS, D), 1)
    target = dot(pick, orders, 1, 1) + (((c >> 2) & 3) * D).astype(F32)
    lane = lane.astype(F32)
    return jnp.concatenate([(target == lane + float(t * D)).astype(BF) for t in range(KV)], axis=1)


def heads(x):
    return jnp.concatenate([x[:, a * D : (a + 1) * D] for a in range(GR)], axis=0)


def kernel(
    q_hbm, k_hbm, v_hbm, g_hbm, sizes_hbm, ffn_hbm, att_hbm,
    rcv2, qg, grow, gup, gdn, p_out,
    sizes, ffn_ref, att_ref, qb, kvb, qst, kvw, kall, prob, gin, snd1, rcv1, snd2,
    m_att, mt_att, ott, dos, sc, dsb, dqs, accw, gsend, bias, invs, flag,
    in_sem, att_s, att_r, kv_s, kv_r, kz_s, kz_r, f_s, f_r, q_s, q_r, dq_s, dq_r, g_s, g_r,
    a1_s, a1_r, a2_s, a2_r,
):
    dp = lax.axis_index("dp")
    me = lax.axis_index("ctx")
    z, x = me >> 2, me & 3
    above, below = ((z + 1) & 7) * KV, ((z + 7) & 7) * KV
    scale = 1.0 / math.sqrt(D)

    def remote(src, dst, s, r, peer):
        return pltpu.make_async_remote_copy(
            src_ref=src, dst_ref=dst, send_sem=s, recv_sem=r,
            device_id=(dp, peer), device_id_type=MESH,
        )

    def lanes(i, width):
        return pl.ds(pl.multiple_of(i * width, D), width)

    barrier = pltpu.get_barrier_semaphore()

    def greet(i, _):
        pl.semaphore_signal(
            barrier, inc=1, device_id=(dp, lax.rem(me + i, N)), device_id_type=MESH
        )
        return 0

    lax.fori_loop(1, N, greet, 0)

    local = [
        pltpu.make_async_copy(ffn_hbm, ffn_ref, in_sem.at[0]),
        pltpu.make_async_copy(g_hbm, gin, in_sem.at[1]),
        pltpu.make_async_copy(att_hbm, att_ref.at[x], in_sem.at[2]),
        pltpu.make_async_copy(sizes_hbm, sizes, in_sem.at[3]),
    ]
    for g in range(KV):
        cols = slice(g * D, (g + 1) * D)
        local += [
            pltpu.make_async_copy(k_hbm.at[:, cols], kvb.at[g, :, 0:D], in_sem.at[4 + 3 * g]),
            pltpu.make_async_copy(v_hbm.at[:, cols], kvb.at[g, :, D:], in_sem.at[5 + 3 * g]),
            pltpu.make_async_copy(
                q_hbm.at[:, g * WIDE : (g + 1) * WIDE], qb.at[g], in_sem.at[6 + 3 * g]
            ),
        ]
    for c in local[4:] + local[:4]:
        c.start()

    for c in local[2:]:
        c.wait()
    kvw[4 + x] = kvb[x]
    qst[x] = qb[x]

    pl.semaphore_wait(barrier, N - 1)

    def order_copy(i):
        return remote(att_ref.at[x], att_ref.at[x], att_s.at[i], att_r.at[i], z * KV + ((x + i) & 3))

    def order_arrived(i):
        u = (x + 4 - i) & 3
        return remote(att_ref.at[u], att_ref.at[u], att_s.at[i], att_r.at[i], me ^ 1)

    for i in (1, 2, 3):
        order_copy(i).start()

    def kv_copy(i):
        g = (x + i) & 3
        return remote(kvb.at[g], kvw.at[4 + x], kv_s.at[i], kv_r.at[x], z * KV + g)

    def kv_arrived(i):
        u = (x + i) & 3
        remote(kvb.at[u], kvw.at[4 + u], kv_s.at[i], kv_r.at[u], z * KV + u).wait_recv()

    kv_down = remote(kvw.at[4:7], kvw.at[8:11], kz_s.at[0], kz_r.at[0], below + x)
    kv_up = remote(kvw.at[5:8, 0:HALF], kvw.at[1:4, 0:HALF], kz_s.at[1], kz_r.at[1], above + x)

    for i in (2, 1, 3):
        kv_copy(i).start()

    def q_copy(i):
        g = (x + i) & 3
        return remote(qb.at[g], qst.at[x], q_s.at[i], q_r.at[x], z * KV + g)

    QUARTER = D // 4

    def far_copy(k):
        rows = slice(k * QUARTER, (k + 1) * QUARTER)
        g = x ^ 2
        return remote(qb.at[g, rows], qst.at[x, rows], f_s.at[k], f_r.at[k], z * KV + g)

    for i in (1, 3):
        q_copy(i).start()

    local[0].wait()
    order = ffn_ref[...].astype(F32)
    p_ffn = (order == iota((D, D), 0).astype(F32)).astype(BF)
    p_out[...] = p_ffn
    gather_ffn = p_ffn.T
    local[1].wait()
    packed = dot(gather_ffn, gin[...], 1, 0).astype(BF)
    for g in range(KV):
        snd1[g * D : (g + 1) * D, :] = packed[:, g * WIDE : (g + 1) * WIDE]

    def rows_at(i):
        return pl.ds(pl.multiple_of(i * CHUNK, CHUNK), CHUNK)

    def token_row(peer):
        return pl.ds(pl.multiple_of((peer & 3) * D + (peer >> 2) * CHUNK, CHUNK), CHUNK)

    def send_column(src, dst, src_at, dst_at, s, r, dx):
        def one(i, _):
            peer = ((z + (0x07162534 >> (4 * i))) & 7) * KV + ((x + dx) & 3)
            remote(src.at[src_at(peer)], dst.at[dst_at(me)], s, r, peer).start()
            return 0

        lax.fori_loop(0, 8 if dx else 7, one, 0)

    def send1(dx):
        send_column(snd1, rcv1, token_row, rows_at, a1_s, a1_r, dx)

    send1(0)
    rcv1[rows_at(me), :] = snd1[token_row(me), :]

    def whole(src, dst, s, r):
        n = ROWS - CHUNK
        return remote(src.at[:n], dst.at[:n], s, r, lax.rem(me + 1, N))

    kk, qq = iota((D, D), 0), iota((D, D), 1)
    for u in range(KV):
        d = z * KV + u
        first, end, start = 0, 0, 0
        for t in range(16):
            stop = start + sizes[t]
            inside = (start <= d) & (d < stop)
            first = jnp.where(inside, start, first)
            end = jnp.where(inside, stop, end)
            start = stop
        bias[u, 0:D, :] = jnp.where(kk <= qq, 0.0, NEG)
        for r in (1, 2, 3):
            flag[u * KV + r] = jnp.where(d + r < end, 1, 0)
            later = jnp.where(d + r < end, 0.0, NEG)
            earlier = jnp.where(d + r - 4 >= first, 0.0, NEG)
            bias[u, r * D : (r + 1) * D, :] = jnp.maximum(
                jnp.where(qq >= HALF, later, NEG), jnp.where(kk < HALF, earlier, NEG)
            )
    for i in (1, 3, 2):
        kv_arrived(i)
    kv_down.start()
    kv_up.start()
    for k in range(4):
        far_copy(k).start()
    accw[...] = jnp.zeros_like(accw)
    invs[...] = jnp.zeros_like(invs)

    for i in (1, 2, 3):
        order_arrived(i).wait_recv()
    orders = jnp.concatenate([att_ref[u] for u in range(KV)], axis=1)
    orders = jnp.broadcast_to(orders.astype(F32).astype(BF), (D, KV * D))
    pick = picks()
    m_att[...] = scatter_matrix(orders, pick)
    mt_att[...] = gather_matrix(orders, pick)

    kv_down.wait_recv()
    kv_up.wait_recv()
    for dx in (1, 3, 2):
        send1(dx)

    def forward(i, _):
        u = (x + (0xB4 >> (2 * i))) & 3

        @pl.when((i == 1) | (i == 2))
        def _():
            remote(qb.at[0], qst.at[u], q_s.at[0], q_r.at[u], me ^ 1).wait_recv()

        @pl.when(i == 3)
        def _():
            for k in range(4):
                far_copy(k).wait_recv()

        kall[u, 0:D, :] = kvw[4 + u]
        for r in (1, 2, 3):
            kall[u, r * D : r * D + HALF, :] = jnp.where(
                flag[u * KV + r] > 0, kvw[4 + u + r, 0:HALF, :], kvw[u + r, 0:HALF, :]
            )
            kall[u, r * D + HALF : (r + 1) * D, :] = kvw[4 + u + r, HALF:D, :]
        keys, values = kall[u, :, 0:D], kall[u, :, D : 2 * D]
        sc[...] = dot(keys, heads(qst[u]), 1, 1)

        blocks = [slice(b, b + STEP) for b in range(0, KEYS, STEP)]

        def masked(rows):
            return sc[rows, :] + jnp.concatenate([bias[u, rows, :]] * GR, axis=1)

        top = jnp.full((8, WIDE), NEG, F32)
        for rows in blocks:
            top = jnp.maximum(top, jnp.max(masked(rows).reshape(STEP // 8, 8, WIDE), axis=0))
        top = jnp.max(top, axis=0, keepdims=True)
        total = jnp.zeros((8, WIDE), F32)
        for rows in blocks:
            p = jnp.exp2((masked(rows) - top) * (scale * math.log2(math.e)))
            prob[u, rows, :] = p.astype(BF)
            total = total + jnp.sum(p.reshape(STEP // 8, 8, WIDE), axis=0)
        inv = 1.0 / jnp.sum(total, axis=0, keepdims=True)
        o = (dot(values.T, prob[u], 1, 0) * inv).astype(BF)
        for a in range(GR):
            cols = slice(a * D, (a + 1) * D)
            ott[cols, lanes(u, D)] = o[:, cols]
            invs[u, a : a + 1, :] = inv[:, cols]
        return 0

    lax.fori_loop(0, KV, forward, 0)

    snd2[...] = dot(mt_att[...], ott[...], 1, 1).astype(BF)

    for dx in (2, 1, 3, 0):
        send_column(snd2, rcv2, rows_at, token_row, a2_s, a2_r, dx)
    rcv2[token_row(me), :] = snd2[rows_at(me), :]

    whole(snd1, rcv1, a1_s, a1_r).wait_recv()
    every = dot(m_att[...], rcv1[...], 1, 0)
    for u in range(KV):
        up = every[u * D : (u + 1) * D]
        inv = invs[u].T
        for a in range(GR):
            cols = slice(a * D, (a + 1) * D)
            dos[u, :, cols] = (up[:, cols] * inv[:, a : a + 1]).astype(BF)

    def dq_copy(u):
        return remote(dqs.at[u], qg.at[x], dq_s.at[u], dq_r.at[x], z * KV + u)

    def add_part(part, u, term):
        accw[part, 4 + u] += term[0:D]
        for r in (1, 2, 3):
            later = flag[u * KV + r] > 0
            accw[part, 4 + u + r] += jnp.where(later, term[r * D : (r + 1) * D], 0.0)
            accw[part, u + r, 0:HALF, :] += jnp.where(later, 0.0, term[r * D : r * D + HALF])

    def g_copy(part, e):
        g, s = e & 3, g_s.at[part, e]
        if e < 4:
            return remote(gsend.at[part, e, 0:HALF], gdn.at[x, part], s, g_r.at[0, part, x], below + g)
        if e < 8:
            return remote(gsend.at[part, e], grow.at[x, part], s, g_r.at[1, part, x], z * KV + g)
        return remote(gsend.at[part, e], gup.at[x, part], s, g_r.at[2, part, x], above + g)

    def g_all(part, action):
        for e in (8, 9, 10, 1, 2, 3):
            action(g_copy(part, e))
        for e in range(4, 8):

            @pl.when(x != e - 4)
            def _():
                action(g_copy(part, e))

    def send_terms(part):
        for e in range(1, 11):
            gsend[part, e] = accw[part, e].astype(BF)
        g_all(part, lambda c: c.start())
        grow[x, part] = gsend[part, 4 + x]

    def value_terms(u, _):
        add_part(1, u, dot(prob[u], heads(dos[u]), 1, 0))
        return 0

    lax.fori_loop(0, KV, value_terms, 0)
    send_terms(1)

    def backward(i, _):
        u = (x + 1 + i) & 3
        keys, values = kall[u, :, 0:D], kall[u, :, D : 2 * D]
        sc[...] = dot(values, heads(dos[u]), 1, 1)

        blocks = [slice(b, b + STEP) for b in range(0, KEYS, STEP)]
        total = jnp.zeros((8, WIDE), F32)
        for rows in blocks:
            t = prob[u, rows, :].astype(F32) * sc[rows, :]
            total = total + jnp.sum(t.reshape(STEP // 8, 8, WIDE), axis=0)
        inv = jnp.concatenate([invs[u, a : a + 1, :] for a in range(GR)], axis=1)
        delta = jnp.sum(total, axis=0, keepdims=True) * inv

        for rows in blocks:
            dsb[rows, :] = (prob[u, rows, :].astype(F32) * (sc[rows, :] - delta)).astype(BF)
        dq = dot(keys.T, dsb[...], 1, 0) * scale
        for a in range(GR):
            cols = slice(a * D, (a + 1) * D)
            dqs[u, :, cols] = dq[:, cols].T.astype(BF)

        @pl.when(i < 3)
        def _():
            dq_copy(u).start()

        add_part(0, u, dot(dsb[...], heads(qst[u]), 1, 0) * scale)
        return 0

    lax.fori_loop(0, KV, backward, 0)
    qg[x] = dqs[x]

    send_terms(0)

    whole(snd2, rcv2, a2_s, a2_r).wait_recv()
    for part in (1, 0):
        for g in range(KV):
            pl.when(x != g)(
                remote(
                    gsend.at[0, 4], grow.at[g, part], g_s.at[0, 0], g_r.at[1, part, g], me ^ 1
                ).wait_recv
            )
            pl.when(x <= 2)(
                remote(
                    gsend.at[0, 4], gup.at[g, part], g_s.at[0, 0], g_r.at[2, part, g], me ^ 1
                ).wait_recv
            )
            pl.when(x >= 1)(
                remote(
                    gsend.at[0, 4, 0:HALF], gdn.at[g, part], g_s.at[0, 0], g_r.at[0, part, g], me ^ 1
                ).wait_recv
            )

    for i in (1, 2, 3):
        order_copy(i).wait_send()
        kv_copy(i).wait_send()
    for i in (1, 3):
        q_copy(i).wait_send()
    for k in range(4):
        far_copy(k).wait_send()
    kv_down.wait_send()
    kv_up.wait_send()
    whole(snd1, rcv1, a1_s, a1_r).wait_send()
    whole(snd2, rcv2, a2_s, a2_r).wait_send()
    for part in (0, 1):
        g_all(part, lambda c: c.wait_send())
    for u in range(KV):

        @pl.when(x != u)
        def _():
            dq_copy(u).wait_send()
            remote(dqs.at[u], qg.at[u], dq_s.at[u], dq_r.at[u], me ^ 1).wait_recv()


def finish(
    got, qg, grow, gup, gdn, p_ffn,
    out_hbm, qg_hbm, kg_hbm, vg_hbm,
    out_v, kg_v, vg_v, sem,
):
    x = lax.axis_index("ctx") & 3
    outs = []

    def send(src, dst):
        outs.append(pltpu.make_async_copy(src, dst, sem.at[len(outs)]))
        outs[-1].start()

    for g in range(KV):
        send(qg.at[g], qg_hbm.at[:, g * WIDE : (g + 1) * WIDE])
    for g in range(KV):
        cols = slice(g * D, (g + 1) * D)
        for part, ref in ((0, kg_v), (1, vg_v)):
            total = grow[g, part].astype(F32) + jnp.where(x <= 2, gup[g, part].astype(F32), 0.0)
            low = total[0:HALF] + jnp.where(x >= 1, gdn[g, part].astype(F32), 0.0)
            ref[0:HALF, cols] = low.astype(BF)
            ref[HALF:D, cols] = total[HALF:D].astype(BF)
    send(kg_v, kg_hbm)
    send(vg_v, vg_hbm)
    for g in range(KV):
        cols = slice(g * WIDE, (g + 1) * WIDE)
        out_v[:, cols] = dot(p_ffn[...], got[g * D : (g + 1) * D, :], 1, 0).astype(BF)
        send(out_v.at[:, cols], out_hbm.at[:, cols])
    for c in outs:
        c.wait()


def body(q, k, v, g, sizes, ffn_order, attn_order):
    hbm = pl.BlockSpec(memory_space=pltpu.HBM)
    vmem = pl.BlockSpec(memory_space=pltpu.VMEM)
    dma = pltpu.SemaphoreType.DMA
    vm = pltpu.VMEM
    got, qg, row, up, down, p_ffn = pl.pallas_call(
        kernel,
        out_shape=(
            vm((ROWS, WIDE), BF),
            vm((KV, D, WIDE), BF),
            vm((KV, 2, D, D), BF),
            vm((KV, 2, D, D), BF),
            vm((KV, 2, HALF, D), BF),
            vm((D, D), BF),
        ),
        in_specs=[hbm] * 7,
        out_specs=(vmem,) * 6,
        scratch_shapes=[
            pltpu.SMEM((16,), jnp.int32),
            vm((1, D), jnp.int32),
            vm((KV, 1, D), jnp.int32),
            vm((KV, D, WIDE), BF),
            vm((KV, D, 2 * D), BF),
            vm((KV, D, WIDE), BF),
            vm((12, D, 2 * D), BF),
            vm((KV, KEYS, 2 * D), BF),
            vm((KV, KEYS, WIDE), BF),
            vm((D, KV * WIDE), BF),
            vm((ROWS, WIDE), BF),
            vm((ROWS, WIDE), BF),
            vm((ROWS, WIDE), BF),
            vm((KV * D, ROWS), BF),
            vm((ROWS, KV * D), BF),
            vm((WIDE, KV * D), BF),
            vm((KV, D, WIDE), BF),
            vm((KEYS, WIDE), F32),
            vm((KEYS, WIDE), BF),
            vm((KV, D, WIDE), BF),
            vm((2, 12, D, D), F32),
            vm((2, 12, D, D), BF),
            vm((KV, KEYS, D), F32),
            vm((KV, 8, D), F32),
            pltpu.SMEM((KV * KV,), jnp.int32),
            dma((16,)),
            dma((4,)),
            dma((4,)),
            dma((4,)),
            dma((4,)),
            dma((2,)),
            dma((2,)),
            dma((4,)),
            dma((4,)),
            dma((4,)),
            dma((4,)),
            dma((4,)),
            dma((4,)),
            dma((2, 12)),
            dma((3, 2, 4)),
            dma,
            dma,
            dma,
            dma,
        ],
        compiler_params=pltpu.CompilerParams(
            collective_id=0, has_side_effects=True, vmem_limit_bytes=56 * 1024 * 1024
        ),
    )(q, k, v, g, sizes, ffn_order, attn_order)
    return pl.pallas_call(
        finish,
        out_shape=(
            jax.ShapeDtypeStruct((D, KV * WIDE), BF),
            jax.ShapeDtypeStruct((D, KV * WIDE), BF),
            jax.ShapeDtypeStruct((D, KV * D), BF),
            jax.ShapeDtypeStruct((D, KV * D), BF),
        ),
        in_specs=[vmem] * 6,
        out_specs=(hbm,) * 4,
        scratch_shapes=[
            vm((D, KV * WIDE), BF),
            vm((D, KV * D), BF),
            vm((D, KV * D), BF),
            dma((10,)),
        ],
        compiler_params=pltpu.CompilerParams(vmem_limit_bytes=8 * 1024 * 1024),
    )(got, qg, row, up, down, p_ffn)


def solution(mesh):
    rows = P(("dp", "ctx"), None)
    return jax.shard_map(
        body,
        mesh=mesh,
        in_specs=(rows, rows, rows, rows, P("dp"), rows, rows),
        out_specs=(rows,) * 4,
        check_vma=False,
    )
```

```python
import math

import jax
import jax.numpy as jnp
from jax import lax
from jax.experimental import pallas as pl
from jax.experimental.pallas import tpu as pltpu
from jax.sharding import PartitionSpec as P

MESH = pl.DeviceIdType.MESH
D = 128
HALF = 64
KV = 4
GR = 5
N = 32
CHUNK = 16
ROWS = N * CHUNK
WIDE = GR * D
KEYS = 4 * D
NEG = -1e30
STEP = 32
BF, F32 = jnp.bfloat16, jnp.float32


def dot(a, b, ca, cb):
    return lax.dot_general(a, b, (((ca,), (cb,)), ((), ())), preferred_element_type=F32)


def iota(shape, dim):
    return lax.broadcasted_iota(jnp.int32, shape, dim)


def picks():
    c, l = iota((ROWS, D), 0), iota((ROWS, D), 1)
    entry = (l == (c >> 4) * 4 + (c & 3)).astype(F32)
    device = (c >> 2) & 3
    return jnp.concatenate(
        [jnp.where(device == u, entry, 0.0).astype(BF) for u in range(KV)], axis=1
    )


def scatter_matrix(orders, pick):
    row, c = iota((D, ROWS), 0), iota((D, ROWS), 1)
    target = dot(orders, pick, 1, 1) + (((c >> 2) & 3) * D).astype(F32)
    row = row.astype(F32)
    return jnp.concatenate([(target == row + float(t * D)).astype(BF) for t in range(KV)], axis=0)


def gather_matrix(orders, pick):
    c, lane = iota((ROWS, D), 0), iota((ROWS, D), 1)
    target = dot(pick, orders, 1, 1) + (((c >> 2) & 3) * D).astype(F32)
    lane = lane.astype(F32)
    return jnp.concatenate([(target == lane + float(t * D)).astype(BF) for t in range(KV)], axis=1)


def heads(x):
    return jnp.concatenate([x[:, a * D : (a + 1) * D] for a in range(GR)], axis=0)


def kernel(
    q_hbm, k_hbm, v_hbm, g_hbm, sizes_hbm, ffn_hbm, att_hbm,
    rcv2, qg, grow, gup, gdn, p_out,
    sizes, ffn_ref, att_ref, qb, kvb, qst, kvw, kall, prob, gin, snd1, rcv1, snd2,
    m_att, mt_att, ott, dos, sc0, sc1, dsb0, dsb1, dqs, accw, gsend, bias, invs, flag,
    in_sem, att_s, att_r, kv_s, kv_r, kz_s, kz_r, q_s, q_r, dq_s, dq_r, g_s, g_r,
    a1_s, a1_r, a2_s, a2_r,
):
    dp = lax.axis_index("dp")
    me = lax.axis_index("ctx")
    z, x = me >> 2, me & 3
    above, below = ((z + 1) & 7) * KV, ((z + 7) & 7) * KV
    scale = 1.0 / math.sqrt(D)
    sc, dsb = (sc0, sc1), (dsb0, dsb1)

    def remote(src, dst, s, r, peer):
        return pltpu.make_async_remote_copy(
            src_ref=src, dst_ref=dst, send_sem=s, recv_sem=r,
            device_id=(dp, peer), device_id_type=MESH,
        )

    def lanes(i, width):
        return pl.ds(pl.multiple_of(i * width, D), width)

    barrier = pltpu.get_barrier_semaphore()

    def greet(i, _):
        pl.semaphore_signal(
            barrier, inc=1, device_id=(dp, lax.rem(me + i, N)), device_id_type=MESH
        )
        return 0

    lax.fori_loop(1, N, greet, 0)

    local = [
        pltpu.make_async_copy(ffn_hbm, ffn_ref, in_sem.at[0]),
        pltpu.make_async_copy(g_hbm, gin, in_sem.at[1]),
        pltpu.make_async_copy(att_hbm, att_ref.at[x], in_sem.at[2]),
        pltpu.make_async_copy(sizes_hbm, sizes, in_sem.at[3]),
    ]
    for g in range(KV):
        cols = slice(g * D, (g + 1) * D)
        local += [
            pltpu.make_async_copy(k_hbm.at[:, cols], kvb.at[g, :, 0:D], in_sem.at[4 + 3 * g]),
            pltpu.make_async_copy(v_hbm.at[:, cols], kvb.at[g, :, D:], in_sem.at[5 + 3 * g]),
            pltpu.make_async_copy(
                q_hbm.at[:, g * WIDE : (g + 1) * WIDE], qb.at[g], in_sem.at[6 + 3 * g]
            ),
        ]
    for c in local[4:] + local[:4]:
        c.start()

    local[0].wait()
    order = ffn_ref[...].astype(F32)
    p_ffn = (order == iota((D, D), 0).astype(F32)).astype(BF)
    p_out[...] = p_ffn
    gather_ffn = p_ffn.T
    local[1].wait()
    packed = dot(gather_ffn, gin[...], 1, 0).astype(BF)
    for g in range(KV):
        snd1[g * D : (g + 1) * D, :] = packed[:, g * WIDE : (g + 1) * WIDE]

    for c in local[2:]:
        c.wait()
    kvw[4 + x] = kvb[x]
    qst[x] = qb[x]

    pl.semaphore_wait(barrier, N - 1)

    def order_copy(i):
        return remote(att_ref.at[x], att_ref.at[x], att_s.at[i], att_r.at[i], z * KV + ((x + i) & 3))

    def order_arrived(i):
        u = (x + 4 - i) & 3
        return remote(att_ref.at[u], att_ref.at[u], att_s.at[i], att_r.at[i], me ^ 1)

    for i in (1, 2, 3):
        order_copy(i).start()

    def kv_copy(i):
        g = (x + i) & 3
        return remote(kvb.at[g], kvw.at[4 + x], kv_s.at[i], kv_r.at[x], z * KV + g)

    def kv_arrived(i):
        u = (x + i) & 3
        remote(kvb.at[u], kvw.at[4 + u], kv_s.at[i], kv_r.at[u], z * KV + u).wait_recv()

    kv_down = remote(kvw.at[4:7], kvw.at[8:11], kz_s.at[0], kz_r.at[0], below + x)
    kv_up = remote(kvw.at[5:8, 0:HALF], kvw.at[1:4, 0:HALF], kz_s.at[1], kz_r.at[1], above + x)

    for i in (2, 1, 3):
        kv_copy(i).start()

    def q_copy(i):
        g = (x + i) & 3
        return remote(qb.at[g], qst.at[x], q_s.at[i], q_r.at[x], z * KV + g)

    for i in (1, 3):
        q_copy(i).start()

    def rows_at(i):
        return pl.ds(pl.multiple_of(i * CHUNK, CHUNK), CHUNK)

    def token_row(peer):
        return pl.ds(pl.multiple_of((peer & 3) * D + (peer >> 2) * CHUNK, CHUNK), CHUNK)

    def send_column(src, dst, src_at, dst_at, s, r, dx):
        def one(i, _):
            peer = ((z + (0x07162534 >> (4 * i))) & 7) * KV + ((x + dx) & 3)
            remote(src.at[src_at(peer)], dst.at[dst_at(me)], s, r, peer).start()
            return 0

        lax.fori_loop(0, 8 if dx else 7, one, 0)

    def send1(dx):
        send_column(snd1, rcv1, token_row, rows_at, a1_s, a1_r, dx)

    send1(0)
    rcv1[rows_at(me), :] = snd1[token_row(me), :]

    def whole(src, dst, s, r):
        n = ROWS - CHUNK
        return remote(src.at[:n], dst.at[:n], s, r, lax.rem(me + 1, N))

    kk, qq = iota((D, D), 0), iota((D, D), 1)
    for u in range(KV):
        d = z * KV + u
        first, end, start = 0, 0, 0
        for t in range(16):
            stop = start + sizes[t]
            inside = (start <= d) & (d < stop)
            first = jnp.where(inside, start, first)
            end = jnp.where(inside, stop, end)
            start = stop
        bias[u, 0:D, :] = jnp.where(kk <= qq, 0.0, NEG)
        for r in (1, 2, 3):
            flag[u * KV + r] = jnp.where(d + r < end, 1, 0)
            later = jnp.where(d + r < end, 0.0, NEG)
            earlier = jnp.where(d + r - 4 >= first, 0.0, NEG)
            bias[u, r * D : (r + 1) * D, :] = jnp.maximum(
                jnp.where(qq >= HALF, later, NEG), jnp.where(kk < HALF, earlier, NEG)
            )
    for i in (1, 3, 2):
        kv_arrived(i)
    kv_down.start()
    kv_up.start()
    q_copy(2).start()
    for dx in (1, 3, 2):
        send1(dx)
    accw[...] = jnp.zeros_like(accw)
    invs[...] = jnp.zeros_like(invs)

    for i in (1, 2, 3):
        order_arrived(i).wait_recv()
    orders = jnp.concatenate([att_ref[u] for u in range(KV)], axis=1)
    orders = jnp.broadcast_to(orders.astype(F32).astype(BF), (D, KV * D))
    pick = picks()
    m_att[...] = scatter_matrix(orders, pick)
    mt_att[...] = gather_matrix(orders, pick)

    kv_down.wait_recv()
    kv_up.wait_recv()

    order_u = [(x + dx) & 3 for dx in (0, 1, 3, 2)]
    halves = [slice(b, b + STEP) for b in range(0, KEYS, STEP)]

    def scores(i):
        u = order_u[i]
        kall[i, 0:D, :] = kvw[4 + u]
        for r in (1, 2, 3):
            kall[i, r * D : r * D + HALF, :] = jnp.where(
                flag[u * KV + r] > 0, kvw[4 + u + r, 0:HALF, :], kvw[u + r, 0:HALF, :]
            )
            kall[i, r * D + HALF : (r + 1) * D, :] = kvw[4 + u + r, HALF:D, :]
        sc[i % 2][...] = dot(kall[i, :, 0:D], heads(qst[u]), 1, 1)

    def soften(i):
        u = order_u[i]

        def masked(rows):
            return sc[i % 2][rows, :] + jnp.concatenate([bias[u, rows, :]] * GR, axis=1)

        top = jnp.full((8, WIDE), NEG, F32)
        for rows in halves:
            top = jnp.maximum(top, jnp.max(masked(rows).reshape(STEP // 8, 8, WIDE), axis=0))
        top = jnp.max(top, axis=0, keepdims=True)
        total = jnp.zeros((8, WIDE), F32)
        for rows in halves:
            p = jnp.exp2((masked(rows) - top) * (scale * math.log2(math.e)))
            prob[i, rows, :] = p.astype(BF)
            total = total + jnp.sum(p.reshape(STEP // 8, 8, WIDE), axis=0)
        inv = 1.0 / jnp.sum(total, axis=0, keepdims=True)
        o = (dot(kall[i, :, D : 2 * D].T, prob[i], 1, 0) * inv).astype(BF)
        for a in range(GR):
            cols = slice(a * D, (a + 1) * D)
            ott[cols, lanes(u, D)] = o[:, cols]
            invs[i, a : a + 1, :] = inv[:, cols]

    def q_arrived(i):
        u = order_u[i]
        remote(qb.at[0], qst.at[u], q_s.at[0], q_r.at[u], me ^ 1).wait_recv()

    scores(0)
    soften(0)
    q_arrived(1)
    scores(1)
    q_arrived(2)
    scores(2)
    soften(1)
    q_arrived(3)
    scores(3)
    soften(2)
    soften(3)

    snd2[...] = dot(mt_att[...], ott[...], 1, 1).astype(BF)

    for dx in (2, 1, 3, 0):
        send_column(snd2, rcv2, rows_at, token_row, a2_s, a2_r, dx)
    rcv2[token_row(me), :] = snd2[rows_at(me), :]

    whole(snd1, rcv1, a1_s, a1_r).wait_recv()
    every = dot(m_att[...], rcv1[...], 1, 0)
    for u in range(KV):
        up = every[u * D : (u + 1) * D]
        inv = invs[(0xB4 >> (2 * ((u - x) & 3))) & 3].T
        for a in range(GR):
            cols = slice(a * D, (a + 1) * D)
            dos[u, :, cols] = (up[:, cols] * inv[:, a : a + 1]).astype(BF)

    def dq_copy(u):
        return remote(dqs.at[u], qg.at[x], dq_s.at[u], dq_r.at[x], z * KV + u)

    def up_scores(i):
        sc[i % 2][...] = dot(kall[i, :, D : 2 * D], heads(dos[order_u[i]]), 1, 1)

    def slopes(i):
        total = jnp.zeros((8, WIDE), F32)
        for rows in halves:
            t = prob[i, rows, :].astype(F32) * sc[i % 2][rows, :]
            total = total + jnp.sum(t.reshape(STEP // 8, 8, WIDE), axis=0)
        inv = jnp.concatenate([invs[i, a : a + 1, :] for a in range(GR)], axis=1)
        delta = jnp.sum(total, axis=0, keepdims=True) * inv
        for rows in halves:
            dsb[i % 2][rows, :] = (
                prob[i, rows, :].astype(F32) * (sc[i % 2][rows, :] - delta)
            ).astype(BF)

    def gradients(i):
        u = order_u[i]
        ds = dsb[i % 2][...]
        dq = (dot(kall[i, :, 0:D].T, ds, 1, 0) * scale).astype(BF)
        for a in range(GR):
            cols = slice(a * D, (a + 1) * D)
            dqs[u, :, cols] = dq[:, cols].T
        kpart = dot(ds, heads(qst[u]), 1, 0) * scale
        vpart = dot(prob[i], heads(dos[u]), 1, 0)
        part = jnp.concatenate([kpart, vpart], axis=1)
        accw[4 + u] += part[0:D]
        for r in (1, 2, 3):
            later = flag[u * KV + r] > 0
            accw[4 + u + r] += jnp.where(later, part[r * D : (r + 1) * D], 0.0)
            accw[u + r, 0:HALF, :] += jnp.where(later, 0.0, part[r * D : r * D + HALF])

    up_scores(3)
    up_scores(2)
    slopes(3)
    for i in (3, 2, 1):
        gradients(i)
        if i > 1:
            up_scores(i - 2)
        slopes(i - 1)
        dq_copy(order_u[i]).start()
    gradients(0)
    qg[x] = dqs[x]

    for e in range(1, 11):
        gsend[e] = accw[e].astype(BF)

    def g_copy(e):
        g = e & 3
        if e < 4:
            return remote(gsend.at[e, 0:HALF], gdn.at[x], g_s.at[e], g_r.at[0, x], below + g)
        if e < 8:
            return remote(gsend.at[e], grow.at[x], g_s.at[e], g_r.at[1, x], z * KV + g)
        return remote(gsend.at[e], gup.at[x], g_s.at[e], g_r.at[2, x], above + g)

    for e in (8, 9, 10, 1, 2, 3):
        g_copy(e).start()
    for e in range(4, 8):
        pl.when(x != e - 4)(g_copy(e).start)
    grow[x] = gsend[4 + x]

    whole(snd2, rcv2, a2_s, a2_r).wait_recv()
    for g in range(KV):
        pl.when(x != g)(
            remote(gsend.at[4], grow.at[g], g_s.at[0], g_r.at[1, g], me ^ 1).wait_recv
        )
        pl.when(x <= 2)(remote(gsend.at[4], gup.at[g], g_s.at[0], g_r.at[2, g], me ^ 1).wait_recv)
        pl.when(x >= 1)(
            remote(gsend.at[4, 0:HALF], gdn.at[g], g_s.at[0], g_r.at[0, g], me ^ 1).wait_recv
        )

    for i in (1, 2, 3):
        order_copy(i).wait_send()
        kv_copy(i).wait_send()
        q_copy(i).wait_send()
    kv_down.wait_send()
    kv_up.wait_send()
    whole(snd1, rcv1, a1_s, a1_r).wait_send()
    whole(snd2, rcv2, a2_s, a2_r).wait_send()
    for e in (8, 9, 10, 1, 2, 3):
        g_copy(e).wait_send()
    for u in range(KV):

        @pl.when(x != u)
        def _():
            g_copy(4 + u).wait_send()
            dq_copy(u).wait_send()
            remote(dqs.at[u], qg.at[u], dq_s.at[u], dq_r.at[u], me ^ 1).wait_recv()


def finish(
    got, qg, grow, gup, gdn, p_ffn,
    out_hbm, qg_hbm, kg_hbm, vg_hbm,
    out_v, kg_v, vg_v, sem,
):
    x = lax.axis_index("ctx") & 3
    outs = []

    def send(src, dst):
        outs.append(pltpu.make_async_copy(src, dst, sem.at[len(outs)]))
        outs[-1].start()

    for g in range(KV):
        send(qg.at[g], qg_hbm.at[:, g * WIDE : (g + 1) * WIDE])
    for g in range(KV):
        total = grow[g].astype(F32) + jnp.where(x <= 2, gup[g].astype(F32), 0.0)
        low = total[0:HALF] + jnp.where(x >= 1, gdn[g].astype(F32), 0.0)
        high = total[HALF:D]
        cols = slice(g * D, (g + 1) * D)
        for ref, lane in ((kg_v, 0), (vg_v, D)):
            ref[0:HALF, cols] = low[:, lane : lane + D].astype(BF)
            ref[HALF:D, cols] = high[:, lane : lane + D].astype(BF)
    send(kg_v, kg_hbm)
    send(vg_v, vg_hbm)
    for g in range(KV):
        cols = slice(g * WIDE, (g + 1) * WIDE)
        out_v[:, cols] = dot(p_ffn[...], got[g * D : (g + 1) * D, :], 1, 0).astype(BF)
        send(out_v.at[:, cols], out_hbm.at[:, cols])
    for c in outs:
        c.wait()


def body(q, k, v, g, sizes, ffn_order, attn_order):
    hbm = pl.BlockSpec(memory_space=pltpu.HBM)
    vmem = pl.BlockSpec(memory_space=pltpu.VMEM)
    dma = pltpu.SemaphoreType.DMA
    vm = pltpu.VMEM
    got, qg, row, up, down, p_ffn = pl.pallas_call(
        kernel,
        out_shape=(
            vm((ROWS, WIDE), BF),
            vm((KV, D, WIDE), BF),
            vm((KV, D, 2 * D), BF),
            vm((KV, D, 2 * D), BF),
            vm((KV, HALF, 2 * D), BF),
            vm((D, D), BF),
        ),
        in_specs=[hbm] * 7,
        out_specs=(vmem,) * 6,
        scratch_shapes=[
            pltpu.SMEM((16,), jnp.int32),
            vm((1, D), jnp.int32),
            vm((KV, 1, D), jnp.int32),
            vm((KV, D, WIDE), BF),
            vm((KV, D, 2 * D), BF),
            vm((KV, D, WIDE), BF),
            vm((12, D, 2 * D), BF),
            vm((KV, KEYS, 2 * D), BF),
            vm((KV, KEYS, WIDE), BF),
            vm((D, KV * WIDE), BF),
            vm((ROWS, WIDE), BF),
            vm((ROWS, WIDE), BF),
            vm((ROWS, WIDE), BF),
            vm((KV * D, ROWS), BF),
            vm((ROWS, KV * D), BF),
            vm((WIDE, KV * D), BF),
            vm((KV, D, WIDE), BF),
            vm((KEYS, WIDE), F32),
            vm((KEYS, WIDE), F32),
            vm((KEYS, WIDE), BF),
            vm((KEYS, WIDE), BF),
            vm((KV, D, WIDE), BF),
            vm((12, D, 2 * D), F32),
            vm((12, D, 2 * D), BF),
            vm((KV, KEYS, D), F32),
            vm((KV, 8, D), F32),
            pltpu.SMEM((KV * KV,), jnp.int32),
            dma((16,)),
            dma((4,)),
            dma((4,)),
            dma((4,)),
            dma((4,)),
            dma((2,)),
            dma((2,)),
            dma((4,)),
            dma((4,)),
            dma((4,)),
            dma((4,)),
            dma((12,)),
            dma((3, 4)),
            dma,
            dma,
            dma,
            dma,
        ],
        compiler_params=pltpu.CompilerParams(
            collective_id=0, has_side_effects=True, vmem_limit_bytes=56 * 1024 * 1024
        ),
    )(q, k, v, g, sizes, ffn_order, attn_order)
    return pl.pallas_call(
        finish,
        out_shape=(
            jax.ShapeDtypeStruct((D, KV * WIDE), BF),
            jax.ShapeDtypeStruct((D, KV * WIDE), BF),
            jax.ShapeDtypeStruct((D, KV * D), BF),
            jax.ShapeDtypeStruct((D, KV * D), BF),
        ),
        in_specs=[vmem] * 6,
        out_specs=(hbm,) * 4,
        scratch_shapes=[
            vm((D, KV * WIDE), BF),
            vm((D, KV * D), BF),
            vm((D, KV * D), BF),
            dma((10,)),
        ],
        compiler_params=pltpu.CompilerParams(vmem_limit_bytes=8 * 1024 * 1024),
    )(got, qg, row, up, down, p_ffn)


def solution(mesh):
    rows = P(("dp", "ctx"), None)
    return jax.shard_map(
        body,
        mesh=mesh,
        in_specs=(rows, rows, rows, rows, P("dp"), rows, rows),
        out_specs=(rows,) * 4,
        check_vma=False,
    )
```

```python
import math

import jax
import jax.numpy as jnp
from jax import lax
from jax.experimental import pallas as pl
from jax.experimental.pallas import tpu as pltpu
from jax.sharding import PartitionSpec as P

MESH = pl.DeviceIdType.MESH
D = 128
HALF = 64
KV = 4
GR = 5
N = 32
CHUNK = 16
ROWS = N * CHUNK
WIDE = GR * D
KEYS = 4 * D
NEG = -1e30
STEP = 32
BF, F32 = jnp.bfloat16, jnp.float32


def dot(a, b, ca, cb):
    return lax.dot_general(a, b, (((ca,), (cb,)), ((), ())), preferred_element_type=F32)


def iota(shape, dim):
    return lax.broadcasted_iota(jnp.int32, shape, dim)


def picks():
    c, l = iota((ROWS, D), 0), iota((ROWS, D), 1)
    entry = (l == (c >> 4) * 4 + (c & 3)).astype(F32)
    device = (c >> 2) & 3
    return jnp.concatenate(
        [jnp.where(device == u, entry, 0.0).astype(BF) for u in range(KV)], axis=1
    )


def scatter_matrix(orders, pick):
    row, c = iota((D, ROWS), 0), iota((D, ROWS), 1)
    target = dot(orders, pick, 1, 1) + (((c >> 2) & 3) * D).astype(F32)
    row = row.astype(F32)
    return jnp.concatenate([(target == row + float(t * D)).astype(BF) for t in range(KV)], axis=0)


def gather_matrix(orders, pick):
    c, lane = iota((ROWS, D), 0), iota((ROWS, D), 1)
    target = dot(pick, orders, 1, 1) + (((c >> 2) & 3) * D).astype(F32)
    lane = lane.astype(F32)
    return jnp.concatenate([(target == lane + float(t * D)).astype(BF) for t in range(KV)], axis=1)


def heads(x):
    return jnp.concatenate([x[:, a * D : (a + 1) * D] for a in range(GR)], axis=0)


def kernel(
    q_hbm, k_hbm, v_hbm, g_hbm, sizes_hbm, ffn_hbm, att_hbm,
    rcv2, qg, grow, gup, gdn, p_out,
    sizes, ffn_ref, att_ref, qb, kvb, qst, kvw, kall, prob, gin, snd1, rcv1, snd2,
    m_att, mt_att, ott, dos, sc, dsb, dqs, accw, gsend, bias, invs, flag,
    in_sem, att_s, att_r, kv_s, kv_r, kz_s, kz_r, q_s, q_r, dq_s, dq_r, g_s, g_r,
    a1_s, a1_r, a2_s, a2_r,
):
    dp = lax.axis_index("dp")
    me = lax.axis_index("ctx")
    z, x = me >> 2, me & 3
    above, below = ((z + 1) & 7) * KV, ((z + 7) & 7) * KV
    scale = 1.0 / math.sqrt(D)

    def remote(src, dst, s, r, peer):
        return pltpu.make_async_remote_copy(
            src_ref=src, dst_ref=dst, send_sem=s, recv_sem=r,
            device_id=(dp, peer), device_id_type=MESH,
        )

    def lanes(i, width):
        return pl.ds(pl.multiple_of(i * width, D), width)

    barrier = pltpu.get_barrier_semaphore()

    def greet(i, _):
        pl.semaphore_signal(
            barrier, inc=1, device_id=(dp, lax.rem(me + i, N)), device_id_type=MESH
        )
        return 0

    lax.fori_loop(1, N, greet, 0)

    local = [
        pltpu.make_async_copy(ffn_hbm, ffn_ref, in_sem.at[0]),
        pltpu.make_async_copy(g_hbm, gin, in_sem.at[1]),
        pltpu.make_async_copy(att_hbm, att_ref.at[x], in_sem.at[2]),
        pltpu.make_async_copy(sizes_hbm, sizes, in_sem.at[3]),
    ]
    for g in range(KV):
        cols = slice(g * D, (g + 1) * D)
        local += [
            pltpu.make_async_copy(k_hbm.at[:, cols], kvb.at[g, :, 0:D], in_sem.at[4 + 3 * g]),
            pltpu.make_async_copy(v_hbm.at[:, cols], kvb.at[g, :, D:], in_sem.at[5 + 3 * g]),
            pltpu.make_async_copy(
                q_hbm.at[:, g * WIDE : (g + 1) * WIDE], qb.at[g], in_sem.at[6 + 3 * g]
            ),
        ]
    for c in local[4:] + local[:4]:
        c.start()

    local[0].wait()
    order = ffn_ref[...].astype(F32)
    p_ffn = (order == iota((D, D), 0).astype(F32)).astype(BF)
    p_out[...] = p_ffn
    gather_ffn = p_ffn.T
    local[1].wait()
    packed = dot(gather_ffn, gin[...], 1, 0).astype(BF)
    for g in range(KV):
        snd1[g * D : (g + 1) * D, :] = packed[:, g * WIDE : (g + 1) * WIDE]

    for c in local[2:]:
        c.wait()
    kvw[4 + x] = kvb[x]
    qst[x] = qb[x]

    pl.semaphore_wait(barrier, N - 1)

    def order_copy(i):
        return remote(att_ref.at[x], att_ref.at[x], att_s.at[i], att_r.at[i], z * KV + ((x + i) & 3))

    def order_arrived(i):
        u = (x + 4 - i) & 3
        return remote(att_ref.at[u], att_ref.at[u], att_s.at[i], att_r.at[i], me ^ 1)

    for i in (1, 2, 3):
        order_copy(i).start()

    def kv_copy(i):
        g = (x + i) & 3
        return remote(kvb.at[g], kvw.at[4 + x], kv_s.at[i], kv_r.at[x], z * KV + g)

    def kv_arrived(i):
        u = (x + i) & 3
        remote(kvb.at[u], kvw.at[4 + u], kv_s.at[i], kv_r.at[u], z * KV + u).wait_recv()

    def kv_pieces(action):
        for k in range(D // STEP):
            rows = slice(k * STEP, (k + 1) * STEP)
            for e in (4, 5, 6):
                action(
                    remote(
                        kvw.at[e, rows], kvw.at[e + 4, rows], kz_s.at[0, e - 4, k],
                        kz_r.at[0, e - 4, k], below + x,
                    )
                )
            if k >= HALF // STEP:
                continue
            for e in (5, 6, 7):
                action(
                    remote(
                        kvw.at[e, rows], kvw.at[e - 4, rows], kz_s.at[1, e - 5, k],
                        kz_r.at[1, e - 5, k], above + x,
                    )
                )

    for i in (2, 1, 3):
        kv_copy(i).start()

    def q_copy(i):
        g = (x + i) & 3
        return remote(qb.at[g], qst.at[x], q_s.at[i], q_r.at[x], z * KV + g)

    for i in (1, 3):
        q_copy(i).start()

    def rows_at(i):
        return pl.ds(pl.multiple_of(i * CHUNK, CHUNK), CHUNK)

    def token_row(peer):
        return pl.ds(pl.multiple_of((peer & 3) * D + (peer >> 2) * CHUNK, CHUNK), CHUNK)

    def send_column(src, dst, src_at, dst_at, s, r, dx):
        def one(i, _):
            peer = ((z + (0x07162534 >> (4 * i))) & 7) * KV + ((x + dx) & 3)
            remote(src.at[src_at(peer)], dst.at[dst_at(me)], s, r, peer).start()
            return 0

        lax.fori_loop(0, 8 if dx else 7, one, 0)

    def send1(dx):
        send_column(snd1, rcv1, token_row, rows_at, a1_s, a1_r, dx)

    for dx in (0, 1, 3, 2):
        send1(dx)
    rcv1[rows_at(me), :] = snd1[token_row(me), :]

    def whole(src, dst, s, r):
        n = ROWS - CHUNK
        return remote(src.at[:n], dst.at[:n], s, r, lax.rem(me + 1, N))

    kk, qq = iota((D, D), 0), iota((D, D), 1)
    for u in range(KV):
        d = z * KV + u
        first, end, start = 0, 0, 0
        for t in range(16):
            stop = start + sizes[t]
            inside = (start <= d) & (d < stop)
            first = jnp.where(inside, start, first)
            end = jnp.where(inside, stop, end)
            start = stop
        bias[u, 0:D, :] = jnp.where(kk <= qq, 0.0, NEG)
        for r in (1, 2, 3):
            flag[u * KV + r] = jnp.where(d + r < end, 1, 0)
            later = jnp.where(d + r < end, 0.0, NEG)
            earlier = jnp.where(d + r - 4 >= first, 0.0, NEG)
            bias[u, r * D : (r + 1) * D, :] = jnp.maximum(
                jnp.where(qq >= HALF, later, NEG), jnp.where(kk < HALF, earlier, NEG)
            )
    for i in (1, 3, 2):
        kv_arrived(i)
    kv_pieces(lambda c: c.start())
    q_copy(2).start()
    accw[...] = jnp.zeros_like(accw)
    invs[...] = jnp.zeros_like(invs)

    for i in (1, 2, 3):
        order_arrived(i).wait_recv()
    orders = jnp.concatenate([att_ref[u] for u in range(KV)], axis=1)
    orders = jnp.broadcast_to(orders.astype(F32).astype(BF), (D, KV * D))
    pick = picks()
    m_att[...] = scatter_matrix(orders, pick)
    mt_att[...] = gather_matrix(orders, pick)

    kv_pieces(lambda c: c.wait_recv())

    def forward(i, _):
        u = (x + (0xB4 >> (2 * i))) & 3

        @pl.when(i > 0)
        def _():
            remote(qb.at[0], qst.at[u], q_s.at[0], q_r.at[u], me ^ 1).wait_recv()

        kall[u, 0:D, :] = kvw[4 + u]
        for r in (1, 2, 3):
            kall[u, r * D : r * D + HALF, :] = jnp.where(
                flag[u * KV + r] > 0, kvw[4 + u + r, 0:HALF, :], kvw[u + r, 0:HALF, :]
            )
            kall[u, r * D + HALF : (r + 1) * D, :] = kvw[4 + u + r, HALF:D, :]
        keys, values = kall[u, :, 0:D], kall[u, :, D : 2 * D]
        sc[...] = dot(keys, heads(qst[u]), 1, 1)

        blocks = [slice(b, b + STEP) for b in range(0, KEYS, STEP)]

        def masked(rows):
            return sc[rows, :] + jnp.concatenate([bias[u, rows, :]] * GR, axis=1)

        top = jnp.full((8, WIDE), NEG, F32)
        for rows in blocks:
            top = jnp.maximum(top, jnp.max(masked(rows).reshape(STEP // 8, 8, WIDE), axis=0))
        top = jnp.max(top, axis=0, keepdims=True)
        total = jnp.zeros((8, WIDE), F32)
        for rows in blocks:
            p = jnp.exp2((masked(rows) - top) * (scale * math.log2(math.e)))
            prob[u, rows, :] = p.astype(BF)
            total = total + jnp.sum(p.reshape(STEP // 8, 8, WIDE), axis=0)
        inv = 1.0 / jnp.sum(total, axis=0, keepdims=True)
        o = (dot(values.T, prob[u], 1, 0) * inv).astype(BF)
        for a in range(GR):
            cols = slice(a * D, (a + 1) * D)
            ott[cols, lanes(u, D)] = o[:, cols]
            invs[u, a : a + 1, :] = inv[:, cols]
        return 0

    lax.fori_loop(0, KV, forward, 0)

    snd2[...] = dot(mt_att[...], ott[...], 1, 1).astype(BF)

    for dx in (2, 1, 3, 0):
        send_column(snd2, rcv2, rows_at, token_row, a2_s, a2_r, dx)
    rcv2[token_row(me), :] = snd2[rows_at(me), :]

    whole(snd1, rcv1, a1_s, a1_r).wait_recv()
    every = dot(m_att[...], rcv1[...], 1, 0)
    for u in range(KV):
        up = every[u * D : (u + 1) * D]
        inv = invs[u].T
        for a in range(GR):
            cols = slice(a * D, (a + 1) * D)
            dos[u, :, cols] = (up[:, cols] * inv[:, a : a + 1]).astype(BF)

    def dq_copy(u):
        return remote(dqs.at[u], qg.at[x], dq_s.at[u], dq_r.at[x], z * KV + u)

    def backward(i, _):
        u = (x + 1 + i) & 3
        keys, values = kall[u, :, 0:D], kall[u, :, D : 2 * D]
        sc[...] = dot(values, heads(dos[u]), 1, 1)

        blocks = [slice(b, b + STEP) for b in range(0, KEYS, STEP)]
        total = jnp.zeros((8, WIDE), F32)
        for rows in blocks:
            t = prob[u, rows, :].astype(F32) * sc[rows, :]
            total = total + jnp.sum(t.reshape(STEP // 8, 8, WIDE), axis=0)
        inv = jnp.concatenate([invs[u, a : a + 1, :] for a in range(GR)], axis=1)
        delta = jnp.sum(total, axis=0, keepdims=True) * inv

        for rows in blocks:
            dsb[rows, :] = (prob[u, rows, :].astype(F32) * (sc[rows, :] - delta)).astype(BF)
        dq = dot(keys.T, dsb[...], 1, 0) * scale
        for a in range(GR):
            cols = slice(a * D, (a + 1) * D)
            dqs[u, :, cols] = dq[:, cols].T.astype(BF)

        @pl.when(i < 3)
        def _():
            dq_copy(u).start()

        kpart = dot(dsb[...], heads(qst[u]), 1, 0) * scale
        vpart = dot(prob[u], heads(dos[u]), 1, 0)
        part = jnp.concatenate([kpart, vpart], axis=1)
        accw[4 + u] += part[0:D]
        for r in (1, 2, 3):
            later = flag[u * KV + r] > 0
            accw[4 + u + r] += jnp.where(later, part[r * D : (r + 1) * D], 0.0)
            accw[u + r, 0:HALF, :] += jnp.where(later, 0.0, part[r * D : r * D + HALF])
        return 0

    lax.fori_loop(0, KV, backward, 0)
    qg[x] = dqs[x]

    for e in range(1, 11):
        gsend[e] = accw[e].astype(BF)

    def g_copy(e):
        g = e & 3
        if e < 4:
            return remote(gsend.at[e, 0:HALF], gdn.at[x], g_s.at[e], g_r.at[0, x], below + g)
        if e < 8:
            return remote(gsend.at[e], grow.at[x], g_s.at[e], g_r.at[1, x], z * KV + g)
        return remote(gsend.at[e], gup.at[x], g_s.at[e], g_r.at[2, x], above + g)

    for e in (8, 9, 10, 1, 2, 3):
        g_copy(e).start()
    for e in range(4, 8):
        pl.when(x != e - 4)(g_copy(e).start)
    grow[x] = gsend[4 + x]

    whole(snd2, rcv2, a2_s, a2_r).wait_recv()
    for g in range(KV):
        pl.when(x != g)(
            remote(gsend.at[4], grow.at[g], g_s.at[0], g_r.at[1, g], me ^ 1).wait_recv
        )
        pl.when(x <= 2)(remote(gsend.at[4], gup.at[g], g_s.at[0], g_r.at[2, g], me ^ 1).wait_recv)
        pl.when(x >= 1)(
            remote(gsend.at[4, 0:HALF], gdn.at[g], g_s.at[0], g_r.at[0, g], me ^ 1).wait_recv
        )

    for i in (1, 2, 3):
        order_copy(i).wait_send()
        kv_copy(i).wait_send()
        q_copy(i).wait_send()
    kv_pieces(lambda c: c.wait_send())
    whole(snd1, rcv1, a1_s, a1_r).wait_send()
    whole(snd2, rcv2, a2_s, a2_r).wait_send()
    for e in (8, 9, 10, 1, 2, 3):
        g_copy(e).wait_send()
    for u in range(KV):

        @pl.when(x != u)
        def _():
            g_copy(4 + u).wait_send()
            dq_copy(u).wait_send()
            remote(dqs.at[u], qg.at[u], dq_s.at[u], dq_r.at[u], me ^ 1).wait_recv()


def finish(
    got, qg, grow, gup, gdn, p_ffn,
    out_hbm, qg_hbm, kg_hbm, vg_hbm,
    out_v, kg_v, vg_v, sem,
):
    x = lax.axis_index("ctx") & 3
    outs = []

    def send(src, dst):
        outs.append(pltpu.make_async_copy(src, dst, sem.at[len(outs)]))
        outs[-1].start()

    for g in range(KV):
        send(qg.at[g], qg_hbm.at[:, g * WIDE : (g + 1) * WIDE])
    for g in range(KV):
        total = grow[g].astype(F32) + jnp.where(x <= 2, gup[g].astype(F32), 0.0)
        low = total[0:HALF] + jnp.where(x >= 1, gdn[g].astype(F32), 0.0)
        high = total[HALF:D]
        cols = slice(g * D, (g + 1) * D)
        for ref, lane in ((kg_v, 0), (vg_v, D)):
            ref[0:HALF, cols] = low[:, lane : lane + D].astype(BF)
            ref[HALF:D, cols] = high[:, lane : lane + D].astype(BF)
    send(kg_v, kg_hbm)
    send(vg_v, vg_hbm)
    for g in range(KV):
        cols = slice(g * WIDE, (g + 1) * WIDE)
        out_v[:, cols] = dot(p_ffn[...], got[g * D : (g + 1) * D, :], 1, 0).astype(BF)
        send(out_v.at[:, cols], out_hbm.at[:, cols])
    for c in outs:
        c.wait()


def body(q, k, v, g, sizes, ffn_order, attn_order):
    hbm = pl.BlockSpec(memory_space=pltpu.HBM)
    vmem = pl.BlockSpec(memory_space=pltpu.VMEM)
    dma = pltpu.SemaphoreType.DMA
    vm = pltpu.VMEM
    got, qg, row, up, down, p_ffn = pl.pallas_call(
        kernel,
        out_shape=(
            vm((ROWS, WIDE), BF),
            vm((KV, D, WIDE), BF),
            vm((KV, D, 2 * D), BF),
            vm((KV, D, 2 * D), BF),
            vm((KV, HALF, 2 * D), BF),
            vm((D, D), BF),
        ),
        in_specs=[hbm] * 7,
        out_specs=(vmem,) * 6,
        scratch_shapes=[
            pltpu.SMEM((16,), jnp.int32),
            vm((1, D), jnp.int32),
            vm((KV, 1, D), jnp.int32),
            vm((KV, D, WIDE), BF),
            vm((KV, D, 2 * D), BF),
            vm((KV, D, WIDE), BF),
            vm((12, D, 2 * D), BF),
            vm((KV, KEYS, 2 * D), BF),
            vm((KV, KEYS, WIDE), BF),
            vm((D, KV * WIDE), BF),
            vm((ROWS, WIDE), BF),
            vm((ROWS, WIDE), BF),
            vm((ROWS, WIDE), BF),
            vm((KV * D, ROWS), BF),
            vm((ROWS, KV * D), BF),
            vm((WIDE, KV * D), BF),
            vm((KV, D, WIDE), BF),
            vm((KEYS, WIDE), F32),
            vm((KEYS, WIDE), BF),
            vm((KV, D, WIDE), BF),
            vm((12, D, 2 * D), F32),
            vm((12, D, 2 * D), BF),
            vm((KV, KEYS, D), F32),
            vm((KV, 8, D), F32),
            pltpu.SMEM((KV * KV,), jnp.int32),
            dma((16,)),
            dma((4,)),
            dma((4,)),
            dma((4,)),
            dma((4,)),
            dma((2, 3, 4)),
            dma((2, 3, 4)),
            dma((4,)),
            dma((4,)),
            dma((4,)),
            dma((4,)),
            dma((12,)),
            dma((3, 4)),
            dma,
            dma,
            dma,
            dma,
        ],
        compiler_params=pltpu.CompilerParams(
            collective_id=0, has_side_effects=True, vmem_limit_bytes=56 * 1024 * 1024
        ),
    )(q, k, v, g, sizes, ffn_order, attn_order)
    return pl.pallas_call(
        finish,
        out_shape=(
            jax.ShapeDtypeStruct((D, KV * WIDE), BF),
            jax.ShapeDtypeStruct((D, KV * WIDE), BF),
            jax.ShapeDtypeStruct((D, KV * D), BF),
            jax.ShapeDtypeStruct((D, KV * D), BF),
        ),
        in_specs=[vmem] * 6,
        out_specs=(hbm,) * 4,
        scratch_shapes=[
            vm((D, KV * WIDE), BF),
            vm((D, KV * D), BF),
            vm((D, KV * D), BF),
            dma((10,)),
        ],
        compiler_params=pltpu.CompilerParams(vmem_limit_bytes=8 * 1024 * 1024),
    )(got, qg, row, up, down, p_ffn)


def solution(mesh):
    rows = P(("dp", "ctx"), None)
    return jax.shard_map(
        body,
        mesh=mesh,
        in_specs=(rows, rows, rows, rows, P("dp"), rows, rows),
        out_specs=(rows,) * 4,
        check_vma=False,
    )
```

```python
import math

import jax
import jax.numpy as jnp
from jax import lax
from jax.experimental import pallas as pl
from jax.experimental.pallas import tpu as pltpu
from jax.sharding import PartitionSpec as P

MESH = pl.DeviceIdType.MESH
D = 128
HALF = 64
KV = 4
GR = 5
N = 32
CHUNK = 16
ROWS = N * CHUNK
WIDE = GR * D
KEYS = 4 * D
NEG = -1e30
STEP = 32
BF, F32 = jnp.bfloat16, jnp.float32


def dot(a, b, ca, cb):
    return lax.dot_general(a, b, (((ca,), (cb,)), ((), ())), preferred_element_type=F32)


def iota(shape, dim):
    return lax.broadcasted_iota(jnp.int32, shape, dim)


def picks():
    c, l = iota((ROWS, D), 0), iota((ROWS, D), 1)
    entry = (l == (c >> 4) * 4 + (c & 3)).astype(F32)
    device = (c >> 2) & 3
    return jnp.concatenate(
        [jnp.where(device == u, entry, 0.0).astype(BF) for u in range(KV)], axis=1
    )


def scatter_matrix(orders, pick):
    row, c = iota((D, ROWS), 0), iota((D, ROWS), 1)
    target = dot(orders, pick, 1, 1) + (((c >> 2) & 3) * D).astype(F32)
    row = row.astype(F32)
    return jnp.concatenate([(target == row + float(t * D)).astype(BF) for t in range(KV)], axis=0)


def gather_matrix(orders, pick):
    c, lane = iota((ROWS, D), 0), iota((ROWS, D), 1)
    target = dot(pick, orders, 1, 1) + (((c >> 2) & 3) * D).astype(F32)
    lane = lane.astype(F32)
    return jnp.concatenate([(target == lane + float(t * D)).astype(BF) for t in range(KV)], axis=1)


def heads(x):
    return jnp.concatenate([x[:, a * D : (a + 1) * D] for a in range(GR)], axis=0)


def kernel(
    q_hbm, k_hbm, v_hbm, g_hbm, sizes_hbm, ffn_hbm, att_hbm,
    rcv2, qg, grow, gup, gdn, p_out,
    sizes, ffn_ref, att_ref, qb, kvb, qst, kvw, kall, prob, gin, snd1, rcv1, snd2,
    m_att, mt_att, ott, dos, sc, dsb, dqs, accw, gsend, bias, invs, flag,
    in_sem, att_s, att_r, kv_s, kv_r, kz_s, kz_r, f_s, f_r, q_s, q_r, dq_s, dq_r, g_s, g_r,
    a1_s, a1_r, a2_s, a2_r,
):
    dp = lax.axis_index("dp")
    me = lax.axis_index("ctx")
    z, x = me >> 2, me & 3
    above, below = ((z + 1) & 7) * KV, ((z + 7) & 7) * KV
    scale = 1.0 / math.sqrt(D)

    def remote(src, dst, s, r, peer):
        return pltpu.make_async_remote_copy(
            src_ref=src, dst_ref=dst, send_sem=s, recv_sem=r,
            device_id=(dp, peer), device_id_type=MESH,
        )

    def lanes(i, width):
        return pl.ds(pl.multiple_of(i * width, D), width)

    barrier = pltpu.get_barrier_semaphore()

    def greet(i, _):
        pl.semaphore_signal(
            barrier, inc=1, device_id=(dp, lax.rem(me + i, N)), device_id_type=MESH
        )
        return 0

    lax.fori_loop(1, N, greet, 0)

    local = [
        pltpu.make_async_copy(ffn_hbm, ffn_ref, in_sem.at[0]),
        pltpu.make_async_copy(g_hbm, gin, in_sem.at[1]),
        pltpu.make_async_copy(att_hbm, att_ref.at[x], in_sem.at[2]),
        pltpu.make_async_copy(sizes_hbm, sizes, in_sem.at[3]),
    ]
    for g in range(KV):
        cols = slice(g * D, (g + 1) * D)
        local += [
            pltpu.make_async_copy(k_hbm.at[:, cols], kvb.at[g, :, 0:D], in_sem.at[4 + 3 * g]),
            pltpu.make_async_copy(v_hbm.at[:, cols], kvb.at[g, :, D:], in_sem.at[5 + 3 * g]),
            pltpu.make_async_copy(
                q_hbm.at[:, g * WIDE : (g + 1) * WIDE], qb.at[g], in_sem.at[6 + 3 * g]
            ),
        ]
    for c in local[4:] + local[:4]:
        c.start()

    local[0].wait()
    order = ffn_ref[...].astype(F32)
    p_ffn = (order == iota((D, D), 0).astype(F32)).astype(BF)
    p_out[...] = p_ffn
    gather_ffn = p_ffn.T
    local[1].wait()
    packed = dot(gather_ffn, gin[...], 1, 0).astype(BF)
    for g in range(KV):
        snd1[g * D : (g + 1) * D, :] = packed[:, g * WIDE : (g + 1) * WIDE]

    for c in local[2:]:
        c.wait()
    kvw[4 + x] = kvb[x]
    qst[x] = qb[x]

    pl.semaphore_wait(barrier, N - 1)

    def order_copy(i):
        return remote(att_ref.at[x], att_ref.at[x], att_s.at[i], att_r.at[i], z * KV + ((x + i) & 3))

    def order_arrived(i):
        u = (x + 4 - i) & 3
        return remote(att_ref.at[u], att_ref.at[u], att_s.at[i], att_r.at[i], me ^ 1)

    for i in (1, 2, 3):
        order_copy(i).start()

    def kv_copy(i):
        g = (x + i) & 3
        return remote(kvb.at[g], kvw.at[4 + x], kv_s.at[i], kv_r.at[x], z * KV + g)

    def kv_arrived(i):
        u = (x + i) & 3
        remote(kvb.at[u], kvw.at[4 + u], kv_s.at[i], kv_r.at[u], z * KV + u).wait_recv()

    def kv_pieces(action):
        for k in range(D // STEP):
            rows = slice(k * STEP, (k + 1) * STEP)
            for e in (4, 5, 6):
                action(
                    remote(
                        kvw.at[e, rows], kvw.at[e + 4, rows], kz_s.at[0, e - 4, k],
                        kz_r.at[0, e - 4, k], below + x,
                    )
                )
            if k >= HALF // STEP:
                continue
            for e in (5, 6, 7):
                action(
                    remote(
                        kvw.at[e, rows], kvw.at[e - 4, rows], kz_s.at[1, e - 5, k],
                        kz_r.at[1, e - 5, k], above + x,
                    )
                )

    for i in (2, 1, 3):
        kv_copy(i).start()

    def q_copy(i):
        g = (x + i) & 3
        return remote(qb.at[g], qst.at[x], q_s.at[i], q_r.at[x], z * KV + g)

    QUARTER = D // 4

    def far_copy(k):
        rows = slice(k * QUARTER, (k + 1) * QUARTER)
        g = x ^ 2
        return remote(qb.at[g, rows], qst.at[x, rows], f_s.at[k], f_r.at[k], z * KV + g)

    for i in (1, 3):
        q_copy(i).start()

    def rows_at(i):
        return pl.ds(pl.multiple_of(i * CHUNK, CHUNK), CHUNK)

    def token_row(peer):
        return pl.ds(pl.multiple_of((peer & 3) * D + (peer >> 2) * CHUNK, CHUNK), CHUNK)

    def send_column(src, dst, src_at, dst_at, s, r, dx):
        def one(i, _):
            peer = ((z + (0x07162534 >> (4 * i))) & 7) * KV + ((x + dx) & 3)
            remote(src.at[src_at(peer)], dst.at[dst_at(me)], s, r, peer).start()
            return 0

        lax.fori_loop(0, 8 if dx else 7, one, 0)

    def send1(dx):
        send_column(snd1, rcv1, token_row, rows_at, a1_s, a1_r, dx)

    send1(0)
    rcv1[rows_at(me), :] = snd1[token_row(me), :]

    def whole(src, dst, s, r):
        n = ROWS - CHUNK
        return remote(src.at[:n], dst.at[:n], s, r, lax.rem(me + 1, N))

    kk, qq = iota((D, D), 0), iota((D, D), 1)
    for u in range(KV):
        d = z * KV + u
        first, end, start = 0, 0, 0
        for t in range(16):
            stop = start + sizes[t]
            inside = (start <= d) & (d < stop)
            first = jnp.where(inside, start, first)
            end = jnp.where(inside, stop, end)
            start = stop
        bias[u, 0:D, :] = jnp.where(kk <= qq, 0.0, NEG)
        for r in (1, 2, 3):
            flag[u * KV + r] = jnp.where(d + r < end, 1, 0)
            later = jnp.where(d + r < end, 0.0, NEG)
            earlier = jnp.where(d + r - 4 >= first, 0.0, NEG)
            bias[u, r * D : (r + 1) * D, :] = jnp.maximum(
                jnp.where(qq >= HALF, later, NEG), jnp.where(kk < HALF, earlier, NEG)
            )
    for i in (1, 3, 2):
        kv_arrived(i)
    kv_pieces(lambda c: c.start())
    for k in range(4):
        far_copy(k).start()
    for i in (1, 3):
        u = (x + i) & 3
        remote(qb.at[0], qst.at[u], q_s.at[0], q_r.at[u], me ^ 1).wait_recv()
    for dx in (1, 3, 2):
        send1(dx)
    accw[...] = jnp.zeros_like(accw)
    invs[...] = jnp.zeros_like(invs)

    for i in (1, 2, 3):
        order_arrived(i).wait_recv()
    orders = jnp.concatenate([att_ref[u] for u in range(KV)], axis=1)
    orders = jnp.broadcast_to(orders.astype(F32).astype(BF), (D, KV * D))
    pick = picks()
    m_att[...] = scatter_matrix(orders, pick)
    mt_att[...] = gather_matrix(orders, pick)

    kv_pieces(lambda c: c.wait_recv())

    def forward(i, _):
        u = (x + (0xB4 >> (2 * i))) & 3

        @pl.when(i == 3)
        def _():
            for k in range(4):
                far_copy(k).wait_recv()

        kall[u, 0:D, :] = kvw[4 + u]
        for r in (1, 2, 3):
            kall[u, r * D : r * D + HALF, :] = jnp.where(
                flag[u * KV + r] > 0, kvw[4 + u + r, 0:HALF, :], kvw[u + r, 0:HALF, :]
            )
            kall[u, r * D + HALF : (r + 1) * D, :] = kvw[4 + u + r, HALF:D, :]
        keys, values = kall[u, :, 0:D], kall[u, :, D : 2 * D]
        sc[...] = dot(keys, heads(qst[u]), 1, 1)

        blocks = [slice(b, b + STEP) for b in range(0, KEYS, STEP)]

        def masked(rows):
            return sc[rows, :] + jnp.concatenate([bias[u, rows, :]] * GR, axis=1)

        top = jnp.full((8, WIDE), NEG, F32)
        for rows in blocks:
            top = jnp.maximum(top, jnp.max(masked(rows).reshape(STEP // 8, 8, WIDE), axis=0))
        top = jnp.max(top, axis=0, keepdims=True)
        total = jnp.zeros((8, WIDE), F32)
        for rows in blocks:
            p = jnp.exp2((masked(rows) - top) * (scale * math.log2(math.e)))
            prob[u, rows, :] = p.astype(BF)
            total = total + jnp.sum(p.reshape(STEP // 8, 8, WIDE), axis=0)
        inv = 1.0 / jnp.sum(total, axis=0, keepdims=True)
        o = (dot(values.T, prob[u], 1, 0) * inv).astype(BF)
        for a in range(GR):
            cols = slice(a * D, (a + 1) * D)
            ott[cols, lanes(u, D)] = o[:, cols]
            invs[u, a : a + 1, :] = inv[:, cols]
        return 0

    lax.fori_loop(0, KV, forward, 0)

    snd2[...] = dot(mt_att[...], ott[...], 1, 1).astype(BF)

    for dx in (2, 1, 3, 0):
        send_column(snd2, rcv2, rows_at, token_row, a2_s, a2_r, dx)
    rcv2[token_row(me), :] = snd2[rows_at(me), :]

    whole(snd1, rcv1, a1_s, a1_r).wait_recv()
    every = dot(m_att[...], rcv1[...], 1, 0)
    for u in range(KV):
        up = every[u * D : (u + 1) * D]
        inv = invs[u].T
        for a in range(GR):
            cols = slice(a * D, (a + 1) * D)
            dos[u, :, cols] = (up[:, cols] * inv[:, a : a + 1]).astype(BF)

    def dq_copy(u):
        return remote(dqs.at[u], qg.at[x], dq_s.at[u], dq_r.at[x], z * KV + u)

    def backward(i, _):
        u = (x + 1 + i) & 3
        keys, values = kall[u, :, 0:D], kall[u, :, D : 2 * D]
        sc[...] = dot(values, heads(dos[u]), 1, 1)

        blocks = [slice(b, b + STEP) for b in range(0, KEYS, STEP)]
        total = jnp.zeros((8, WIDE), F32)
        for rows in blocks:
            t = prob[u, rows, :].astype(F32) * sc[rows, :]
            total = total + jnp.sum(t.reshape(STEP // 8, 8, WIDE), axis=0)
        inv = jnp.concatenate([invs[u, a : a + 1, :] for a in range(GR)], axis=1)
        delta = jnp.sum(total, axis=0, keepdims=True) * inv

        for rows in blocks:
            dsb[rows, :] = (prob[u, rows, :].astype(F32) * (sc[rows, :] - delta)).astype(BF)
        dq = dot(keys.T, dsb[...], 1, 0) * scale
        for a in range(GR):
            cols = slice(a * D, (a + 1) * D)
            dqs[u, :, cols] = dq[:, cols].T.astype(BF)

        @pl.when(i < 3)
        def _():
            dq_copy(u).start()

        kpart = dot(dsb[...], heads(qst[u]), 1, 0) * scale
        vpart = dot(prob[u], heads(dos[u]), 1, 0)
        part = jnp.concatenate([kpart, vpart], axis=1)
        accw[4 + u] += part[0:D]
        for r in (1, 2, 3):
            later = flag[u * KV + r] > 0
            accw[4 + u + r] += jnp.where(later, part[r * D : (r + 1) * D], 0.0)
            accw[u + r, 0:HALF, :] += jnp.where(later, 0.0, part[r * D : r * D + HALF])
        return 0

    lax.fori_loop(0, KV, backward, 0)
    qg[x] = dqs[x]

    for e in range(1, 11):
        gsend[e] = accw[e].astype(BF)

    def g_copy(e):
        g = e & 3
        if e < 4:
            return remote(gsend.at[e, 0:HALF], gdn.at[x], g_s.at[e], g_r.at[0, x], below + g)
        if e < 8:
            return remote(gsend.at[e], grow.at[x], g_s.at[e], g_r.at[1, x], z * KV + g)
        return remote(gsend.at[e], gup.at[x], g_s.at[e], g_r.at[2, x], above + g)

    for e in (8, 9, 10, 1, 2, 3):
        g_copy(e).start()
    for e in range(4, 8):
        pl.when(x != e - 4)(g_copy(e).start)
    grow[x] = gsend[4 + x]

    whole(snd2, rcv2, a2_s, a2_r).wait_recv()
    for g in range(KV):
        pl.when(x != g)(
            remote(gsend.at[4], grow.at[g], g_s.at[0], g_r.at[1, g], me ^ 1).wait_recv
        )
        pl.when(x <= 2)(remote(gsend.at[4], gup.at[g], g_s.at[0], g_r.at[2, g], me ^ 1).wait_recv)
        pl.when(x >= 1)(
            remote(gsend.at[4, 0:HALF], gdn.at[g], g_s.at[0], g_r.at[0, g], me ^ 1).wait_recv
        )

    for i in (1, 2, 3):
        order_copy(i).wait_send()
        kv_copy(i).wait_send()
    for i in (1, 3):
        q_copy(i).wait_send()
    for k in range(4):
        far_copy(k).wait_send()
    kv_pieces(lambda c: c.wait_send())
    whole(snd1, rcv1, a1_s, a1_r).wait_send()
    whole(snd2, rcv2, a2_s, a2_r).wait_send()
    for e in (8, 9, 10, 1, 2, 3):
        g_copy(e).wait_send()
    for u in range(KV):

        @pl.when(x != u)
        def _():
            g_copy(4 + u).wait_send()
            dq_copy(u).wait_send()
            remote(dqs.at[u], qg.at[u], dq_s.at[u], dq_r.at[u], me ^ 1).wait_recv()


def finish(
    got, qg, grow, gup, gdn, p_ffn,
    out_hbm, qg_hbm, kg_hbm, vg_hbm,
    out_v, kg_v, vg_v, sem,
):
    x = lax.axis_index("ctx") & 3
    outs = []

    def send(src, dst):
        outs.append(pltpu.make_async_copy(src, dst, sem.at[len(outs)]))
        outs[-1].start()

    for g in range(KV):
        send(qg.at[g], qg_hbm.at[:, g * WIDE : (g + 1) * WIDE])
    for g in range(KV):
        total = grow[g].astype(F32) + jnp.where(x <= 2, gup[g].astype(F32), 0.0)
        low = total[0:HALF] + jnp.where(x >= 1, gdn[g].astype(F32), 0.0)
        high = total[HALF:D]
        cols = slice(g * D, (g + 1) * D)
        for ref, lane in ((kg_v, 0), (vg_v, D)):
            ref[0:HALF, cols] = low[:, lane : lane + D].astype(BF)
            ref[HALF:D, cols] = high[:, lane : lane + D].astype(BF)
    send(kg_v, kg_hbm)
    send(vg_v, vg_hbm)
    for g in range(KV):
        cols = slice(g * WIDE, (g + 1) * WIDE)
        out_v[:, cols] = dot(p_ffn[...], got[g * D : (g + 1) * D, :], 1, 0).astype(BF)
        send(out_v.at[:, cols], out_hbm.at[:, cols])
    for c in outs:
        c.wait()


def body(q, k, v, g, sizes, ffn_order, attn_order):
    hbm = pl.BlockSpec(memory_space=pltpu.HBM)
    vmem = pl.BlockSpec(memory_space=pltpu.VMEM)
    dma = pltpu.SemaphoreType.DMA
    vm = pltpu.VMEM
    got, qg, row, up, down, p_ffn = pl.pallas_call(
        kernel,
        out_shape=(
            vm((ROWS, WIDE), BF),
            vm((KV, D, WIDE), BF),
            vm((KV, D, 2 * D), BF),
            vm((KV, D, 2 * D), BF),
            vm((KV, HALF, 2 * D), BF),
            vm((D, D), BF),
        ),
        in_specs=[hbm] * 7,
        out_specs=(vmem,) * 6,
        scratch_shapes=[
            pltpu.SMEM((16,), jnp.int32),
            vm((1, D), jnp.int32),
            vm((KV, 1, D), jnp.int32),
            vm((KV, D, WIDE), BF),
            vm((KV, D, 2 * D), BF),
            vm((KV, D, WIDE), BF),
            vm((12, D, 2 * D), BF),
            vm((KV, KEYS, 2 * D), BF),
            vm((KV, KEYS, WIDE), BF),
            vm((D, KV * WIDE), BF),
            vm((ROWS, WIDE), BF),
            vm((ROWS, WIDE), BF),
            vm((ROWS, WIDE), BF),
            vm((KV * D, ROWS), BF),
            vm((ROWS, KV * D), BF),
            vm((WIDE, KV * D), BF),
            vm((KV, D, WIDE), BF),
            vm((KEYS, WIDE), F32),
            vm((KEYS, WIDE), BF),
            vm((KV, D, WIDE), BF),
            vm((12, D, 2 * D), F32),
            vm((12, D, 2 * D), BF),
            vm((KV, KEYS, D), F32),
            vm((KV, 8, D), F32),
            pltpu.SMEM((KV * KV,), jnp.int32),
            dma((16,)),
            dma((4,)),
            dma((4,)),
            dma((4,)),
            dma((4,)),
            dma((2, 3, 4)),
            dma((2, 3, 4)),
            dma((4,)),
            dma((4,)),
            dma((4,)),
            dma((4,)),
            dma((4,)),
            dma((4,)),
            dma((12,)),
            dma((3, 4)),
            dma,
            dma,
            dma,
            dma,
        ],
        compiler_params=pltpu.CompilerParams(
            collective_id=0, has_side_effects=True, vmem_limit_bytes=56 * 1024 * 1024
        ),
    )(q, k, v, g, sizes, ffn_order, attn_order)
    return pl.pallas_call(
        finish,
        out_shape=(
            jax.ShapeDtypeStruct((D, KV * WIDE), BF),
            jax.ShapeDtypeStruct((D, KV * WIDE), BF),
            jax.ShapeDtypeStruct((D, KV * D), BF),
            jax.ShapeDtypeStruct((D, KV * D), BF),
        ),
        in_specs=[vmem] * 6,
        out_specs=(hbm,) * 4,
        scratch_shapes=[
            vm((D, KV * WIDE), BF),
            vm((D, KV * D), BF),
            vm((D, KV * D), BF),
            dma((10,)),
        ],
        compiler_params=pltpu.CompilerParams(vmem_limit_bytes=8 * 1024 * 1024),
    )(got, qg, row, up, down, p_ffn)


def solution(mesh):
    rows = P(("dp", "ctx"), None)
    return jax.shard_map(
        body,
        mesh=mesh,
        in_specs=(rows, rows, rows, rows, P("dp"), rows, rows),
        out_specs=(rows,) * 4,
        check_vma=False,
    )
```

```python
import math

import jax
import jax.numpy as jnp
from jax import lax
from jax.experimental import pallas as pl
from jax.experimental.pallas import tpu as pltpu
from jax.sharding import PartitionSpec as P

MESH = pl.DeviceIdType.MESH
D = 128
HALF = 64
KV = 4
GR = 5
N = 32
CHUNK = 16
ROWS = N * CHUNK
WIDE = GR * D
KEYS = 4 * D
NEG = -1e30
STEP = 32
BF, F32 = jnp.bfloat16, jnp.float32


def dot(a, b, ca, cb):
    return lax.dot_general(a, b, (((ca,), (cb,)), ((), ())), preferred_element_type=F32)


def iota(shape, dim):
    return lax.broadcasted_iota(jnp.int32, shape, dim)


def picks():
    c, l = iota((ROWS, D), 0), iota((ROWS, D), 1)
    entry = (l == (c >> 4) * 4 + (c & 3)).astype(F32)
    device = (c >> 2) & 3
    return jnp.concatenate(
        [jnp.where(device == u, entry, 0.0).astype(BF) for u in range(KV)], axis=1
    )


def scatter_matrix(orders, pick):
    row, c = iota((D, ROWS), 0), iota((D, ROWS), 1)
    target = dot(orders, pick, 1, 1) + (((c >> 2) & 3) * D).astype(F32)
    row = row.astype(F32)
    return jnp.concatenate([(target == row + float(t * D)).astype(BF) for t in range(KV)], axis=0)


def gather_matrix(orders, pick):
    c, lane = iota((ROWS, D), 0), iota((ROWS, D), 1)
    target = dot(pick, orders, 1, 1) + (((c >> 2) & 3) * D).astype(F32)
    lane = lane.astype(F32)
    return jnp.concatenate([(target == lane + float(t * D)).astype(BF) for t in range(KV)], axis=1)


def heads(x):
    return jnp.concatenate([x[:, a * D : (a + 1) * D] for a in range(GR)], axis=0)


def kernel(
    q_hbm, k_hbm, v_hbm, g_hbm, sizes_hbm, ffn_hbm, att_hbm,
    rcv2, qg, grow, gup, gdn, p_out,
    sizes, ffn_ref, att_ref, qb, kvb, qst, kvw, kall, prob, gin, snd1, rcv1, snd2,
    m_att, mt_att, ott, dos, sc, dsb, dqs, accw, gsend, bias, invs, flag,
    in_sem, att_s, att_r, kv_s, kv_r, kz_s, kz_r, q_s, q_r, dq_s, dq_r, g_s, g_r,
    a1_s, a1_r, a2_s, a2_r,
):
    dp = lax.axis_index("dp")
    me = lax.axis_index("ctx")
    z, x = me >> 2, me & 3
    above, below = ((z + 1) & 7) * KV, ((z + 7) & 7) * KV
    scale = 1.0 / math.sqrt(D)

    def remote(src, dst, s, r, peer):
        return pltpu.make_async_remote_copy(
            src_ref=src, dst_ref=dst, send_sem=s, recv_sem=r,
            device_id=(dp, peer), device_id_type=MESH,
        )

    def lanes(i, width):
        return pl.ds(pl.multiple_of(i * width, D), width)

    barrier = pltpu.get_barrier_semaphore()

    def greet(i, _):
        pl.semaphore_signal(
            barrier, inc=1, device_id=(dp, lax.rem(me + i, N)), device_id_type=MESH
        )
        return 0

    lax.fori_loop(1, N, greet, 0)

    local = [
        pltpu.make_async_copy(ffn_hbm, ffn_ref, in_sem.at[0]),
        pltpu.make_async_copy(g_hbm, gin, in_sem.at[1]),
        pltpu.make_async_copy(att_hbm, att_ref.at[x], in_sem.at[2]),
        pltpu.make_async_copy(sizes_hbm, sizes, in_sem.at[3]),
    ]
    for g in range(KV):
        cols = slice(g * D, (g + 1) * D)
        local += [
            pltpu.make_async_copy(k_hbm.at[:, cols], kvb.at[g, :, 0:D], in_sem.at[4 + 3 * g]),
            pltpu.make_async_copy(v_hbm.at[:, cols], kvb.at[g, :, D:], in_sem.at[5 + 3 * g]),
            pltpu.make_async_copy(
                q_hbm.at[:, g * WIDE : (g + 1) * WIDE], qb.at[g], in_sem.at[6 + 3 * g]
            ),
        ]
    for c in local[4:] + local[:4]:
        c.start()

    for c in local[2:]:
        c.wait()
    kvw[4 + x] = kvb[x]
    qst[x] = qb[x]

    pl.semaphore_wait(barrier, N - 1)

    def order_copy(i):
        return remote(att_ref.at[x], att_ref.at[x], att_s.at[i], att_r.at[i], z * KV + ((x + i) & 3))

    def order_arrived(i):
        u = (x + 4 - i) & 3
        return remote(att_ref.at[u], att_ref.at[u], att_s.at[i], att_r.at[i], me ^ 1)

    for i in (1, 2, 3):
        order_copy(i).start()

    def kv_copy(i):
        g = (x + i) & 3
        return remote(kvb.at[g], kvw.at[4 + x], kv_s.at[i], kv_r.at[x], z * KV + g)

    def kv_arrived(i):
        u = (x + i) & 3
        remote(kvb.at[u], kvw.at[4 + u], kv_s.at[i], kv_r.at[u], z * KV + u).wait_recv()

    kv_down = remote(kvw.at[4:7], kvw.at[8:11], kz_s.at[0], kz_r.at[0], below + x)
    kv_up = remote(kvw.at[5:8, 0:HALF], kvw.at[1:4, 0:HALF], kz_s.at[1], kz_r.at[1], above + x)

    for i in (2, 1, 3):
        kv_copy(i).start()

    def q_copy(i):
        g = (x + i) & 3
        return remote(qb.at[g], qst.at[x], q_s.at[i], q_r.at[x], z * KV + g)

    for i in (1, 3):
        q_copy(i).start()

    local[0].wait()
    order = ffn_ref[...].astype(F32)
    p_ffn = (order == iota((D, D), 0).astype(F32)).astype(BF)
    p_out[...] = p_ffn
    gather_ffn = p_ffn.T
    local[1].wait()
    packed = dot(gather_ffn, gin[...], 1, 0).astype(BF)
    for g in range(KV):
        snd1[g * D : (g + 1) * D, :] = packed[:, g * WIDE : (g + 1) * WIDE]

    def rows_at(i):
        return pl.ds(pl.multiple_of(i * CHUNK, CHUNK), CHUNK)

    def token_row(peer):
        return pl.ds(pl.multiple_of((peer & 3) * D + (peer >> 2) * CHUNK, CHUNK), CHUNK)

    def send_column(src, dst, src_at, dst_at, s, r, dx):
        def one(i, _):
            peer = ((z + (0x07162534 >> (4 * i))) & 7) * KV + ((x + dx) & 3)
            remote(src.at[src_at(peer)], dst.at[dst_at(me)], s, r, peer).start()
            return 0

        lax.fori_loop(0, 8 if dx else 7, one, 0)

    def send1(dx):
        send_column(snd1, rcv1, token_row, rows_at, a1_s, a1_r, dx)

    send1(0)
    rcv1[rows_at(me), :] = snd1[token_row(me), :]

    def whole(src, dst, s, r):
        n = ROWS - CHUNK
        return remote(src.at[:n], dst.at[:n], s, r, lax.rem(me + 1, N))

    kk, qq = iota((D, D), 0), iota((D, D), 1)
    for u in range(KV):
        d = z * KV + u
        first, end, start = 0, 0, 0
        for t in range(16):
            stop = start + sizes[t]
            inside = (start <= d) & (d < stop)
            first = jnp.where(inside, start, first)
            end = jnp.where(inside, stop, end)
            start = stop
        bias[u, 0:D, :] = jnp.where(kk <= qq, 0.0, NEG)
        for r in (1, 2, 3):
            flag[u * KV + r] = jnp.where(d + r < end, 1, 0)
            later = jnp.where(d + r < end, 0.0, NEG)
            earlier = jnp.where(d + r - 4 >= first, 0.0, NEG)
            bias[u, r * D : (r + 1) * D, :] = jnp.maximum(
                jnp.where(qq >= HALF, later, NEG), jnp.where(kk < HALF, earlier, NEG)
            )
    for i in (1, 3, 2):
        kv_arrived(i)
    kv_down.start()
    kv_up.start()
    q_copy(2).start()
    for dx in (1, 3, 2):
        send1(dx)
    accw[...] = jnp.zeros_like(accw)
    invs[...] = jnp.zeros_like(invs)

    for i in (1, 2, 3):
        order_arrived(i).wait_recv()
    orders = jnp.concatenate([att_ref[u] for u in range(KV)], axis=1)
    orders = jnp.broadcast_to(orders.astype(F32).astype(BF), (D, KV * D))
    pick = picks()
    m_att[...] = scatter_matrix(orders, pick)
    mt_att[...] = gather_matrix(orders, pick)

    kv_down.wait_recv()
    kv_up.wait_recv()

    def forward(i, _):
        u = (x + (0xB4 >> (2 * i))) & 3

        @pl.when(i > 0)
        def _():
            remote(qb.at[0], qst.at[u], q_s.at[0], q_r.at[u], me ^ 1).wait_recv()

        kall[u, 0:D, :] = kvw[4 + u]
        for r in (1, 2, 3):
            kall[u, r * D : r * D + HALF, :] = jnp.where(
                flag[u * KV + r] > 0, kvw[4 + u + r, 0:HALF, :], kvw[u + r, 0:HALF, :]
            )
            kall[u, r * D + HALF : (r + 1) * D, :] = kvw[4 + u + r, HALF:D, :]
        keys, values = kall[u, :, 0:D], kall[u, :, D : 2 * D]
        sc[...] = dot(keys, heads(qst[u]), 1, 1)

        blocks = [slice(b, b + STEP) for b in range(0, KEYS, STEP)]

        def masked(rows):
            return sc[rows, :] + jnp.concatenate([bias[u, rows, :]] * GR, axis=1)

        top = jnp.full((8, WIDE), NEG, F32)
        for rows in blocks:
            top = jnp.maximum(top, jnp.max(masked(rows).reshape(STEP // 8, 8, WIDE), axis=0))
        top = jnp.max(top, axis=0, keepdims=True)
        total = jnp.zeros((8, WIDE), F32)
        for rows in blocks:
            p = jnp.exp2((masked(rows) - top) * (scale * math.log2(math.e)))
            prob[u, rows, :] = p.astype(BF)
            total = total + jnp.sum(p.reshape(STEP // 8, 8, WIDE), axis=0)
        inv = 1.0 / jnp.sum(total, axis=0, keepdims=True)
        o = (dot(values.T, prob[u], 1, 0) * inv).astype(BF)
        for a in range(GR):
            cols = slice(a * D, (a + 1) * D)
            ott[cols, lanes(u, D)] = o[:, cols]
            invs[u, a : a + 1, :] = inv[:, cols]
        return 0

    lax.fori_loop(0, KV, forward, 0)

    snd2[...] = dot(mt_att[...], ott[...], 1, 1).astype(BF)

    for dx in (2, 1, 3, 0):
        send_column(snd2, rcv2, rows_at, token_row, a2_s, a2_r, dx)
    rcv2[token_row(me), :] = snd2[rows_at(me), :]

    whole(snd1, rcv1, a1_s, a1_r).wait_recv()
    every = dot(m_att[...], rcv1[...], 1, 0)
    for u in range(KV):
        up = every[u * D : (u + 1) * D]
        inv = invs[u].T
        for a in range(GR):
            cols = slice(a * D, (a + 1) * D)
            dos[u, :, cols] = (up[:, cols] * inv[:, a : a + 1]).astype(BF)

    def dq_copy(u):
        return remote(dqs.at[u], qg.at[x], dq_s.at[u], dq_r.at[x], z * KV + u)

    def backward(i, _):
        u = (x + 1 + i) & 3
        keys, values = kall[u, :, 0:D], kall[u, :, D : 2 * D]
        sc[...] = dot(values, heads(dos[u]), 1, 1)

        blocks = [slice(b, b + STEP) for b in range(0, KEYS, STEP)]
        total = jnp.zeros((8, WIDE), F32)
        for rows in blocks:
            t = prob[u, rows, :].astype(F32) * sc[rows, :]
            total = total + jnp.sum(t.reshape(STEP // 8, 8, WIDE), axis=0)
        inv = jnp.concatenate([invs[u, a : a + 1, :] for a in range(GR)], axis=1)
        delta = jnp.sum(total, axis=0, keepdims=True) * inv

        for rows in blocks:
            dsb[rows, :] = (prob[u, rows, :].astype(F32) * (sc[rows, :] - delta)).astype(BF)
        dq = dot(keys.T, dsb[...], 1, 0) * scale
        for a in range(GR):
            cols = slice(a * D, (a + 1) * D)
            dqs[u, :, cols] = dq[:, cols].T.astype(BF)

        @pl.when(i < 3)
        def _():
            dq_copy(u).start()

        kpart = dot(dsb[...], heads(qst[u]), 1, 0) * scale
        vpart = dot(prob[u], heads(dos[u]), 1, 0)
        part = jnp.concatenate([kpart, vpart], axis=1)
        accw[4 + u] += part[0:D]
        for r in (1, 2, 3):
            later = flag[u * KV + r] > 0
            accw[4 + u + r] += jnp.where(later, part[r * D : (r + 1) * D], 0.0)
            accw[u + r, 0:HALF, :] += jnp.where(later, 0.0, part[r * D : r * D + HALF])
        return 0

    lax.fori_loop(0, KV, backward, 0)
    qg[x] = dqs[x]

    for e in range(1, 11):
        gsend[e] = accw[e].astype(BF)

    def g_copy(e):
        g = e & 3
        if e < 4:
            return remote(gsend.at[e, 0:HALF], gdn.at[x], g_s.at[e], g_r.at[0, x], below + g)
        if e < 8:
            return remote(gsend.at[e], grow.at[x], g_s.at[e], g_r.at[1, x], z * KV + g)
        return remote(gsend.at[e], gup.at[x], g_s.at[e], g_r.at[2, x], above + g)

    for e in (8, 9, 10, 1, 2, 3):
        g_copy(e).start()
    for e in range(4, 8):
        pl.when(x != e - 4)(g_copy(e).start)
    grow[x] = gsend[4 + x]

    whole(snd2, rcv2, a2_s, a2_r).wait_recv()
    for g in range(KV):
        pl.when(x != g)(
            remote(gsend.at[4], grow.at[g], g_s.at[0], g_r.at[1, g], me ^ 1).wait_recv
        )
        pl.when(x <= 2)(remote(gsend.at[4], gup.at[g], g_s.at[0], g_r.at[2, g], me ^ 1).wait_recv)
        pl.when(x >= 1)(
            remote(gsend.at[4, 0:HALF], gdn.at[g], g_s.at[0], g_r.at[0, g], me ^ 1).wait_recv
        )

    for i in (1, 2, 3):
        order_copy(i).wait_send()
        kv_copy(i).wait_send()
        q_copy(i).wait_send()
    kv_down.wait_send()
    kv_up.wait_send()
    whole(snd1, rcv1, a1_s, a1_r).wait_send()
    whole(snd2, rcv2, a2_s, a2_r).wait_send()
    for e in (8, 9, 10, 1, 2, 3):
        g_copy(e).wait_send()
    for u in range(KV):

        @pl.when(x != u)
        def _():
            g_copy(4 + u).wait_send()
            dq_copy(u).wait_send()
            remote(dqs.at[u], qg.at[u], dq_s.at[u], dq_r.at[u], me ^ 1).wait_recv()


def finish(
    got, qg, grow, gup, gdn, p_ffn,
    out_hbm, qg_hbm, kg_hbm, vg_hbm,
    out_v, kg_v, vg_v, sem,
):
    x = lax.axis_index("ctx") & 3
    outs = []

    def send(src, dst):
        outs.append(pltpu.make_async_copy(src, dst, sem.at[len(outs)]))
        outs[-1].start()

    for g in range(KV):
        send(qg.at[g], qg_hbm.at[:, g * WIDE : (g + 1) * WIDE])
    for g in range(KV):
        total = grow[g].astype(F32) + jnp.where(x <= 2, gup[g].astype(F32), 0.0)
        low = total[0:HALF] + jnp.where(x >= 1, gdn[g].astype(F32), 0.0)
        high = total[HALF:D]
        cols = slice(g * D, (g + 1) * D)
        for ref, lane in ((kg_v, 0), (vg_v, D)):
            ref[0:HALF, cols] = low[:, lane : lane + D].astype(BF)
            ref[HALF:D, cols] = high[:, lane : lane + D].astype(BF)
    send(kg_v, kg_hbm)
    send(vg_v, vg_hbm)
    for g in range(KV):
        cols = slice(g * WIDE, (g + 1) * WIDE)
        out_v[:, cols] = dot(p_ffn[...], got[g * D : (g + 1) * D, :], 1, 0).astype(BF)
        send(out_v.at[:, cols], out_hbm.at[:, cols])
    for c in outs:
        c.wait()


def body(q, k, v, g, sizes, ffn_order, attn_order):
    hbm = pl.BlockSpec(memory_space=pltpu.HBM)
    vmem = pl.BlockSpec(memory_space=pltpu.VMEM)
    dma = pltpu.SemaphoreType.DMA
    vm = pltpu.VMEM
    got, qg, row, up, down, p_ffn = pl.pallas_call(
        kernel,
        out_shape=(
            vm((ROWS, WIDE), BF),
            vm((KV, D, WIDE), BF),
            vm((KV, D, 2 * D), BF),
            vm((KV, D, 2 * D), BF),
            vm((KV, HALF, 2 * D), BF),
            vm((D, D), BF),
        ),
        in_specs=[hbm] * 7,
        out_specs=(vmem,) * 6,
        scratch_shapes=[
            pltpu.SMEM((16,), jnp.int32),
            vm((1, D), jnp.int32),
            vm((KV, 1, D), jnp.int32),
            vm((KV, D, WIDE), BF),
            vm((KV, D, 2 * D), BF),
            vm((KV, D, WIDE), BF),
            vm((12, D, 2 * D), BF),
            vm((KV, KEYS, 2 * D), BF),
            vm((KV, KEYS, WIDE), BF),
            vm((D, KV * WIDE), BF),
            vm((ROWS, WIDE), BF),
            vm((ROWS, WIDE), BF),
            vm((ROWS, WIDE), BF),
            vm((KV * D, ROWS), BF),
            vm((ROWS, KV * D), BF),
            vm((WIDE, KV * D), BF),
            vm((KV, D, WIDE), BF),
            vm((KEYS, WIDE), F32),
            vm((KEYS, WIDE), BF),
            vm((KV, D, WIDE), BF),
            vm((12, D, 2 * D), F32),
            vm((12, D, 2 * D), BF),
            vm((KV, KEYS, D), F32),
            vm((KV, 8, D), F32),
            pltpu.SMEM((KV * KV,), jnp.int32),
            dma((16,)),
            dma((4,)),
            dma((4,)),
            dma((4,)),
            dma((4,)),
            dma((2,)),
            dma((2,)),
            dma((4,)),
            dma((4,)),
            dma((4,)),
            dma((4,)),
            dma((12,)),
            dma((3, 4)),
            dma,
            dma,
            dma,
            dma,
        ],
        compiler_params=pltpu.CompilerParams(
            collective_id=0, has_side_effects=True, vmem_limit_bytes=56 * 1024 * 1024
        ),
    )(q, k, v, g, sizes, ffn_order, attn_order)
    return pl.pallas_call(
        finish,
        out_shape=(
            jax.ShapeDtypeStruct((D, KV * WIDE), BF),
            jax.ShapeDtypeStruct((D, KV * WIDE), BF),
            jax.ShapeDtypeStruct((D, KV * D), BF),
            jax.ShapeDtypeStruct((D, KV * D), BF),
        ),
        in_specs=[vmem] * 6,
        out_specs=(hbm,) * 4,
        scratch_shapes=[
            vm((D, KV * WIDE), BF),
            vm((D, KV * D), BF),
            vm((D, KV * D), BF),
            dma((10,)),
        ],
        compiler_params=pltpu.CompilerParams(vmem_limit_bytes=8 * 1024 * 1024),
    )(got, qg, row, up, down, p_ffn)


def solution(mesh):
    rows = P(("dp", "ctx"), None)
    return jax.shard_map(
        body,
        mesh=mesh,
        in_specs=(rows, rows, rows, rows, P("dp"), rows, rows),
        out_specs=(rows,) * 4,
        check_vma=False,
    )
```

```python
import math

import jax
import jax.numpy as jnp
from jax import lax
from jax.experimental import pallas as pl
from jax.experimental.pallas import tpu as pltpu
from jax.sharding import PartitionSpec as P

MESH = pl.DeviceIdType.MESH
D = 128
HALF = 64
KV = 4
GR = 5
N = 32
CHUNK = 16
ROWS = N * CHUNK
WIDE = GR * D
KEYS = 4 * D
NEG = -1e30
STEP = 32
BF, F32 = jnp.bfloat16, jnp.float32


def dot(a, b, ca, cb):
    return lax.dot_general(a, b, (((ca,), (cb,)), ((), ())), preferred_element_type=F32)


def iota(shape, dim):
    return lax.broadcasted_iota(jnp.int32, shape, dim)


def picks():
    c, l = iota((ROWS, D), 0), iota((ROWS, D), 1)
    entry = (l == (c >> 4) * 4 + (c & 3)).astype(F32)
    device = (c >> 2) & 3
    return jnp.concatenate(
        [jnp.where(device == u, entry, 0.0).astype(BF) for u in range(KV)], axis=1
    )


def scatter_matrix(orders, pick):
    row, c = iota((D, ROWS), 0), iota((D, ROWS), 1)
    target = dot(orders, pick, 1, 1) + (((c >> 2) & 3) * D).astype(F32)
    row = row.astype(F32)
    return jnp.concatenate([(target == row + float(t * D)).astype(BF) for t in range(KV)], axis=0)


def gather_matrix(orders, pick):
    c, lane = iota((ROWS, D), 0), iota((ROWS, D), 1)
    target = dot(pick, orders, 1, 1) + (((c >> 2) & 3) * D).astype(F32)
    lane = lane.astype(F32)
    return jnp.concatenate([(target == lane + float(t * D)).astype(BF) for t in range(KV)], axis=1)


def heads(x):
    return jnp.concatenate([x[:, a * D : (a + 1) * D] for a in range(GR)], axis=0)


def kernel(
    q_hbm, k_hbm, v_hbm, g_hbm, sizes_hbm, ffn_hbm, att_hbm,
    rcv2, qg, grow, p_out,
    sizes, ffn_ref, att_ref, qb, kvb, qst, kvw, kall, prob, gin, snd1, rcv1, snd2,
    m_att, mt_att, ott, dos, sc, dsb, dqs, accw, gsend, gup, gdn, bias, invs, flag,
    in_sem, att_s, att_r, kv_s, kv_r, kz_s, kz_r, q_s, q_r, dq_s, dq_r, g_s, g_r, gz_s, gz_r,
    a1_s, a1_r, a2_s, a2_r,
):
    dp = lax.axis_index("dp")
    me = lax.axis_index("ctx")
    z, x = me >> 2, me & 3
    above, below = ((z + 1) & 7) * KV, ((z + 7) & 7) * KV
    scale = 1.0 / math.sqrt(D)

    def remote(src, dst, s, r, peer):
        return pltpu.make_async_remote_copy(
            src_ref=src, dst_ref=dst, send_sem=s, recv_sem=r,
            device_id=(dp, peer), device_id_type=MESH,
        )

    def lanes(i, width):
        return pl.ds(pl.multiple_of(i * width, D), width)

    barrier = pltpu.get_barrier_semaphore()

    def greet(i, _):
        pl.semaphore_signal(
            barrier, inc=1, device_id=(dp, lax.rem(me + i, N)), device_id_type=MESH
        )
        return 0

    lax.fori_loop(1, N, greet, 0)

    local = [
        pltpu.make_async_copy(ffn_hbm, ffn_ref, in_sem.at[0]),
        pltpu.make_async_copy(g_hbm, gin, in_sem.at[1]),
        pltpu.make_async_copy(att_hbm, att_ref.at[x], in_sem.at[2]),
        pltpu.make_async_copy(sizes_hbm, sizes, in_sem.at[3]),
    ]
    for g in range(KV):
        cols = slice(g * D, (g + 1) * D)
        local += [
            pltpu.make_async_copy(k_hbm.at[:, cols], kvb.at[g, :, 0:D], in_sem.at[4 + 3 * g]),
            pltpu.make_async_copy(v_hbm.at[:, cols], kvb.at[g, :, D:], in_sem.at[5 + 3 * g]),
            pltpu.make_async_copy(
                q_hbm.at[:, g * WIDE : (g + 1) * WIDE], qb.at[g], in_sem.at[6 + 3 * g]
            ),
        ]
    for c in local[4:] + local[:4]:
        c.start()

    local[0].wait()
    order = ffn_ref[...].astype(F32)
    p_ffn = (order == iota((D, D), 0).astype(F32)).astype(BF)
    p_out[...] = p_ffn
    gather_ffn = p_ffn.T
    local[1].wait()
    packed = dot(gather_ffn, gin[...], 1, 0).astype(BF)
    for g in range(KV):
        snd1[g * D : (g + 1) * D, :] = packed[:, g * WIDE : (g + 1) * WIDE]

    for c in local[2:]:
        c.wait()
    kvw[4 + x] = kvb[x]
    qst[x] = qb[x]

    pl.semaphore_wait(barrier, N - 1)

    def order_copy(i):
        return remote(att_ref.at[x], att_ref.at[x], att_s.at[i], att_r.at[i], z * KV + ((x + i) & 3))

    def order_arrived(i):
        u = (x + 4 - i) & 3
        return remote(att_ref.at[u], att_ref.at[u], att_s.at[i], att_r.at[i], me ^ 1)

    for i in (1, 2, 3):
        order_copy(i).start()

    def kv_copy(i):
        g = (x + i) & 3
        return remote(kvb.at[g], kvw.at[4 + x], kv_s.at[i], kv_r.at[x], z * KV + g)

    def kv_arrived(i):
        u = (x + i) & 3
        remote(kvb.at[u], kvw.at[4 + u], kv_s.at[i], kv_r.at[u], z * KV + u).wait_recv()

    kv_down = remote(kvw.at[4:7], kvw.at[8:11], kz_s.at[0], kz_r.at[0], below + x)
    kv_up = remote(kvw.at[5:8, 0:HALF], kvw.at[1:4, 0:HALF], kz_s.at[1], kz_r.at[1], above + x)

    for i in (2, 1, 3):
        kv_copy(i).start()

    def q_copy(i):
        g = (x + i) & 3
        return remote(qb.at[g], qst.at[x], q_s.at[i], q_r.at[x], z * KV + g)

    for i in (1, 3):
        q_copy(i).start()

    def rows_at(i):
        return pl.ds(pl.multiple_of(i * CHUNK, CHUNK), CHUNK)

    def token_row(peer):
        return pl.ds(pl.multiple_of((peer & 3) * D + (peer >> 2) * CHUNK, CHUNK), CHUNK)

    def send_column(src, dst, src_at, dst_at, s, r, dx):
        def one(i, _):
            peer = ((z + (0x07162534 >> (4 * i))) & 7) * KV + ((x + dx) & 3)
            remote(src.at[src_at(peer)], dst.at[dst_at(me)], s, r, peer).start()
            return 0

        lax.fori_loop(0, 8 if dx else 7, one, 0)

    def send1(dx):
        send_column(snd1, rcv1, token_row, rows_at, a1_s, a1_r, dx)

    send1(0)
    rcv1[rows_at(me), :] = snd1[token_row(me), :]

    def whole(src, dst, s, r):
        n = ROWS - CHUNK
        return remote(src.at[:n], dst.at[:n], s, r, lax.rem(me + 1, N))

    kk, qq = iota((D, D), 0), iota((D, D), 1)
    for u in range(KV):
        d = z * KV + u
        first, end, start = 0, 0, 0
        for t in range(16):
            stop = start + sizes[t]
            inside = (start <= d) & (d < stop)
            first = jnp.where(inside, start, first)
            end = jnp.where(inside, stop, end)
            start = stop
        bias[u, 0:D, :] = jnp.where(kk <= qq, 0.0, NEG)
        for r in (1, 2, 3):
            flag[u * KV + r] = jnp.where(d + r < end, 1, 0)
            later = jnp.where(d + r < end, 0.0, NEG)
            earlier = jnp.where(d + r - 4 >= first, 0.0, NEG)
            bias[u, r * D : (r + 1) * D, :] = jnp.maximum(
                jnp.where(qq >= HALF, later, NEG), jnp.where(kk < HALF, earlier, NEG)
            )
    for i in (1, 3, 2):
        kv_arrived(i)
    kv_down.start()
    kv_up.start()
    q_copy(2).start()
    for dx in (1, 3, 2):
        send1(dx)
    accw[...] = jnp.zeros_like(accw)
    invs[...] = jnp.zeros_like(invs)

    for i in (1, 2, 3):
        order_arrived(i).wait_recv()
    orders = jnp.concatenate([att_ref[u] for u in range(KV)], axis=1)
    orders = jnp.broadcast_to(orders.astype(F32).astype(BF), (D, KV * D))
    pick = picks()
    m_att[...] = scatter_matrix(orders, pick)
    mt_att[...] = gather_matrix(orders, pick)

    kv_down.wait_recv()
    kv_up.wait_recv()

    def forward(i, _):
        u = (x + (0xB4 >> (2 * i))) & 3

        @pl.when(i > 0)
        def _():
            remote(qb.at[0], qst.at[u], q_s.at[0], q_r.at[u], me ^ 1).wait_recv()

        kall[u, 0:D, :] = kvw[4 + u]
        for r in (1, 2, 3):
            kall[u, r * D : r * D + HALF, :] = jnp.where(
                flag[u * KV + r] > 0, kvw[4 + u + r, 0:HALF, :], kvw[u + r, 0:HALF, :]
            )
            kall[u, r * D + HALF : (r + 1) * D, :] = kvw[4 + u + r, HALF:D, :]
        keys, values = kall[u, :, 0:D], kall[u, :, D : 2 * D]
        sc[...] = dot(keys, heads(qst[u]), 1, 1)

        blocks = [slice(b, b + STEP) for b in range(0, KEYS, STEP)]

        def masked(rows):
            return sc[rows, :] + jnp.concatenate([bias[u, rows, :]] * GR, axis=1)

        top = jnp.full((8, WIDE), NEG, F32)
        for rows in blocks:
            top = jnp.maximum(top, jnp.max(masked(rows).reshape(STEP // 8, 8, WIDE), axis=0))
        top = jnp.max(top, axis=0, keepdims=True)
        total = jnp.zeros((8, WIDE), F32)
        for rows in blocks:
            p = jnp.exp2((masked(rows) - top) * (scale * math.log2(math.e)))
            prob[u, rows, :] = p.astype(BF)
            total = total + jnp.sum(p.reshape(STEP // 8, 8, WIDE), axis=0)
        inv = 1.0 / jnp.sum(total, axis=0, keepdims=True)
        o = (dot(values.T, prob[u], 1, 0) * inv).astype(BF)
        for a in range(GR):
            cols = slice(a * D, (a + 1) * D)
            ott[cols, lanes(u, D)] = o[:, cols]
            invs[u, a : a + 1, :] = inv[:, cols]
        return 0

    lax.fori_loop(0, KV, forward, 0)

    snd2[...] = dot(mt_att[...], ott[...], 1, 1).astype(BF)

    for dx in (2, 1, 3, 0):
        send_column(snd2, rcv2, rows_at, token_row, a2_s, a2_r, dx)
    rcv2[token_row(me), :] = snd2[rows_at(me), :]

    whole(snd1, rcv1, a1_s, a1_r).wait_recv()
    every = dot(m_att[...], rcv1[...], 1, 0)
    for u in range(KV):
        up = every[u * D : (u + 1) * D]
        inv = invs[u].T
        for a in range(GR):
            cols = slice(a * D, (a + 1) * D)
            dos[u, :, cols] = (up[:, cols] * inv[:, a : a + 1]).astype(BF)

    def dq_copy(u):
        return remote(dqs.at[u], qg.at[x], dq_s.at[u], dq_r.at[x], z * KV + u)

    def backward(i, _):
        u = (x + 1 + i) & 3
        keys, values = kall[u, :, 0:D], kall[u, :, D : 2 * D]
        sc[...] = dot(values, heads(dos[u]), 1, 1)

        blocks = [slice(b, b + STEP) for b in range(0, KEYS, STEP)]
        total = jnp.zeros((8, WIDE), F32)
        for rows in blocks:
            t = prob[u, rows, :].astype(F32) * sc[rows, :]
            total = total + jnp.sum(t.reshape(STEP // 8, 8, WIDE), axis=0)
        inv = jnp.concatenate([invs[u, a : a + 1, :] for a in range(GR)], axis=1)
        delta = jnp.sum(total, axis=0, keepdims=True) * inv

        for rows in blocks:
            dsb[rows, :] = (prob[u, rows, :].astype(F32) * (sc[rows, :] - delta)).astype(BF)
        dq = dot(keys.T, dsb[...], 1, 0) * scale
        for a in range(GR):
            cols = slice(a * D, (a + 1) * D)
            dqs[u, :, cols] = dq[:, cols].T.astype(BF)

        @pl.when(i < 3)
        def _():
            dq_copy(u).start()

        kpart = dot(dsb[...], heads(qst[u]), 1, 0) * scale
        vpart = dot(prob[u], heads(dos[u]), 1, 0)
        part = jnp.concatenate([kpart, vpart], axis=1)
        accw[4 + u] += part[0:D]
        for r in (1, 2, 3):
            later = flag[u * KV + r] > 0
            accw[4 + u + r] += jnp.where(later, part[r * D : (r + 1) * D], 0.0)
            accw[u + r, 0:HALF, :] += jnp.where(later, 0.0, part[r * D : r * D + HALF])
        return 0

    lax.fori_loop(0, KV, backward, 0)
    qg[x] = dqs[x]

    for e in (8, 9, 10, 1, 2, 3):
        gsend[e] = accw[e].astype(BF)
    g_up = remote(gsend.at[8:11], gup, gz_s.at[0], gz_r.at[0], above + x)
    g_down = remote(gsend.at[1:4, 0:HALF], gdn, gz_s.at[1], gz_r.at[1], below + x)
    g_up.start()
    g_down.start()
    g_up.wait_recv()
    g_down.wait_recv()
    for u in range(KV):
        total = accw[4 + u]
        if u < 3:
            total = total + gup[u].astype(F32)
        low = total[0:HALF]
        if u > 0:
            low = low + gdn[u - 1].astype(F32)
        gsend[4 + u, 0:HALF, :] = low.astype(BF)
        gsend[4 + u, HALF:D, :] = total[HALF:D].astype(BF)

    def g_copy(i):
        u = (x + i) & 3
        return remote(gsend.at[4 + u], grow.at[x], g_s.at[i], g_r.at[x], z * KV + u)

    for i in (2, 1, 3):
        g_copy(i).start()
    grow[x] = gsend[4 + x]

    whole(snd2, rcv2, a2_s, a2_r).wait_recv()
    for i in (1, 2, 3):
        u = (x + i) & 3
        remote(gsend.at[4], grow.at[u], g_s.at[i], g_r.at[u], me ^ 1).wait_recv()
        g_copy(i).wait_send()
    g_up.wait_send()
    g_down.wait_send()

    for i in (1, 2, 3):
        order_copy(i).wait_send()
        kv_copy(i).wait_send()
        q_copy(i).wait_send()
    kv_down.wait_send()
    kv_up.wait_send()
    whole(snd1, rcv1, a1_s, a1_r).wait_send()
    whole(snd2, rcv2, a2_s, a2_r).wait_send()
    for u in range(KV):

        @pl.when(x != u)
        def _():
            dq_copy(u).wait_send()
            remote(dqs.at[u], qg.at[u], dq_s.at[u], dq_r.at[u], me ^ 1).wait_recv()


def finish(
    got, qg, grow, p_ffn,
    out_hbm, qg_hbm, kg_hbm, vg_hbm,
    out_v, sem,
):
    outs = []

    def send(src, dst):
        outs.append(pltpu.make_async_copy(src, dst, sem.at[len(outs)]))
        outs[-1].start()

    for g in range(KV):
        send(qg.at[g], qg_hbm.at[:, g * WIDE : (g + 1) * WIDE])
        send(grow.at[g, :, 0:D], kg_hbm.at[:, g * D : (g + 1) * D])
        send(grow.at[g, :, D:], vg_hbm.at[:, g * D : (g + 1) * D])
    for g in range(KV):
        cols = slice(g * WIDE, (g + 1) * WIDE)
        rows = got[g * D : (g + 1) * D, :]
        out_v[:, cols] = dot(p_ffn[...], rows, 1, 0).astype(BF)
        send(out_v.at[:, cols], out_hbm.at[:, cols])
    for c in outs:
        c.wait()


def body(q, k, v, g, sizes, ffn_order, attn_order):
    hbm = pl.BlockSpec(memory_space=pltpu.HBM)
    vmem = pl.BlockSpec(memory_space=pltpu.VMEM)
    dma = pltpu.SemaphoreType.DMA
    vm = pltpu.VMEM
    got, qg, row, p_ffn = pl.pallas_call(
        kernel,
        out_shape=(
            vm((ROWS, WIDE), BF),
            vm((KV, D, WIDE), BF),
            vm((KV, D, 2 * D), BF),
            vm((D, D), BF),
        ),
        in_specs=[hbm] * 7,
        out_specs=(vmem,) * 4,
        scratch_shapes=[
            pltpu.SMEM((16,), jnp.int32),
            vm((1, D), jnp.int32),
            vm((KV, 1, D), jnp.int32),
            vm((KV, D, WIDE), BF),
            vm((KV, D, 2 * D), BF),
            vm((KV, D, WIDE), BF),
            vm((12, D, 2 * D), BF),
            vm((KV, KEYS, 2 * D), BF),
            vm((KV, KEYS, WIDE), BF),
            vm((D, KV * WIDE), BF),
            vm((ROWS, WIDE), BF),
            vm((ROWS, WIDE), BF),
            vm((ROWS, WIDE), BF),
            vm((KV * D, ROWS), BF),
            vm((ROWS, KV * D), BF),
            vm((WIDE, KV * D), BF),
            vm((KV, D, WIDE), BF),
            vm((KEYS, WIDE), F32),
            vm((KEYS, WIDE), BF),
            vm((KV, D, WIDE), BF),
            vm((12, D, 2 * D), F32),
            vm((12, D, 2 * D), BF),
            vm((3, D, 2 * D), BF),
            vm((3, HALF, 2 * D), BF),
            vm((KV, KEYS, D), F32),
            vm((KV, 8, D), F32),
            pltpu.SMEM((KV * KV,), jnp.int32),
            dma((16,)),
            dma((4,)),
            dma((4,)),
            dma((4,)),
            dma((4,)),
            dma((2,)),
            dma((2,)),
            dma((4,)),
            dma((4,)),
            dma((4,)),
            dma((4,)),
            dma((4,)),
            dma((4,)),
            dma((2,)),
            dma((2,)),
            dma,
            dma,
            dma,
            dma,
        ],
        compiler_params=pltpu.CompilerParams(
            collective_id=0, has_side_effects=True, vmem_limit_bytes=56 * 1024 * 1024
        ),
    )(q, k, v, g, sizes, ffn_order, attn_order)
    return pl.pallas_call(
        finish,
        out_shape=(
            jax.ShapeDtypeStruct((D, KV * WIDE), BF),
            jax.ShapeDtypeStruct((D, KV * WIDE), BF),
            jax.ShapeDtypeStruct((D, KV * D), BF),
            jax.ShapeDtypeStruct((D, KV * D), BF),
        ),
        in_specs=[vmem] * 4,
        out_specs=(hbm,) * 4,
        scratch_shapes=[
            vm((D, KV * WIDE), BF),
            dma((16,)),
        ],
        compiler_params=pltpu.CompilerParams(vmem_limit_bytes=8 * 1024 * 1024),
    )(got, qg, row, p_ffn)


def solution(mesh):
    rows = P(("dp", "ctx"), None)
    return jax.shard_map(
        body,
        mesh=mesh,
        in_specs=(rows, rows, rows, rows, P("dp"), rows, rows),
        out_specs=(rows,) * 4,
        check_vma=False,
    )
```

```python
import math

import jax
import jax.numpy as jnp
from jax import lax
from jax.experimental import pallas as pl
from jax.experimental.pallas import tpu as pltpu
from jax.sharding import PartitionSpec as P

MESH = pl.DeviceIdType.MESH
D = 128
HALF = 64
KV = 4
GR = 5
N = 32
CHUNK = 16
ROWS = N * CHUNK
WIDE = GR * D
KEYS = 4 * D
NEG = -1e30
STEP = 32
BF, F32 = jnp.bfloat16, jnp.float32


def dot(a, b, ca, cb):
    return lax.dot_general(a, b, (((ca,), (cb,)), ((), ())), preferred_element_type=F32)


def iota(shape, dim):
    return lax.broadcasted_iota(jnp.int32, shape, dim)


def picks():
    c, l = iota((ROWS, D), 0), iota((ROWS, D), 1)
    entry = (l == (c >> 4) * 4 + (c & 3)).astype(F32)
    device = (c >> 2) & 3
    return jnp.concatenate(
        [jnp.where(device == u, entry, 0.0).astype(BF) for u in range(KV)], axis=1
    )


def scatter_matrix(orders, pick):
    row, c = iota((D, ROWS), 0), iota((D, ROWS), 1)
    target = dot(orders, pick, 1, 1) + (((c >> 2) & 3) * D).astype(F32)
    row = row.astype(F32)
    return jnp.concatenate([(target == row + float(t * D)).astype(BF) for t in range(KV)], axis=0)


def gather_matrix(orders, pick):
    c, lane = iota((ROWS, D), 0), iota((ROWS, D), 1)
    target = dot(pick, orders, 1, 1) + (((c >> 2) & 3) * D).astype(F32)
    lane = lane.astype(F32)
    return jnp.concatenate([(target == lane + float(t * D)).astype(BF) for t in range(KV)], axis=1)


def heads(x):
    return jnp.concatenate([x[:, a * D : (a + 1) * D] for a in range(GR)], axis=0)


def kernel(
    q_hbm, k_hbm, v_hbm, g_hbm, sizes_hbm, ffn_hbm, att_hbm,
    rcv2, qg, grow, gup, gdn, p_out,
    sizes, ffn_ref, att_ref, qb, kvb, qst, kvw, kall, prob, gin, snd1, rcv1, snd2,
    m_att, mt_att, ott, dos, sc, dsb, dqs, accw, gsend, bias, invs, flag,
    in_sem, att_s, att_r, kv_s, kv_r, kz_s, kz_r, q_s, q_r, dq_s, dq_r, g_s, g_r,
    a1_s, a1_r, a2_s, a2_r,
):
    dp = lax.axis_index("dp")
    me = lax.axis_index("ctx")
    z, x = me >> 2, me & 3
    above, below = ((z + 1) & 7) * KV, ((z + 7) & 7) * KV
    scale = 1.0 / math.sqrt(D)

    def remote(src, dst, s, r, peer):
        return pltpu.make_async_remote_copy(
            src_ref=src, dst_ref=dst, send_sem=s, recv_sem=r,
            device_id=(dp, peer), device_id_type=MESH,
        )

    def lanes(i, width):
        return pl.ds(pl.multiple_of(i * width, D), width)

    barrier = pltpu.get_barrier_semaphore()

    def greet(i, _):
        pl.semaphore_signal(
            barrier, inc=1, device_id=(dp, lax.rem(me + i, N)), device_id_type=MESH
        )
        return 0

    lax.fori_loop(1, N, greet, 0)

    local = [
        pltpu.make_async_copy(ffn_hbm, ffn_ref, in_sem.at[0]),
        pltpu.make_async_copy(g_hbm, gin, in_sem.at[1]),
        pltpu.make_async_copy(att_hbm, att_ref.at[x], in_sem.at[2]),
        pltpu.make_async_copy(sizes_hbm, sizes, in_sem.at[3]),
    ]
    for g in range(KV):
        cols = slice(g * D, (g + 1) * D)
        local += [
            pltpu.make_async_copy(k_hbm.at[:, cols], kvb.at[g, :, 0:D], in_sem.at[4 + 3 * g]),
            pltpu.make_async_copy(v_hbm.at[:, cols], kvb.at[g, :, D:], in_sem.at[5 + 3 * g]),
            pltpu.make_async_copy(
                q_hbm.at[:, g * WIDE : (g + 1) * WIDE], qb.at[g], in_sem.at[6 + 3 * g]
            ),
        ]
    for c in local[4:] + local[:4]:
        c.start()

    for c in local[2:]:
        c.wait()
    kvw[4 + x] = kvb[x]
    qst[x] = qb[x]

    pl.semaphore_wait(barrier, N - 1)

    def order_copy(i):
        return remote(att_ref.at[x], att_ref.at[x], att_s.at[i], att_r.at[i], z * KV + ((x + i) & 3))

    def order_arrived(i):
        u = (x + 4 - i) & 3
        return remote(att_ref.at[u], att_ref.at[u], att_s.at[i], att_r.at[i], me ^ 1)

    for i in (1, 2, 3):
        order_copy(i).start()

    def kv_copy(i):
        g = (x + i) & 3
        return remote(kvb.at[g], kvw.at[4 + x], kv_s.at[i], kv_r.at[x], z * KV + g)

    def kv_arrived(i):
        u = (x + i) & 3
        remote(kvb.at[u], kvw.at[4 + u], kv_s.at[i], kv_r.at[u], z * KV + u).wait_recv()

    kv_down = remote(kvw.at[4:7], kvw.at[8:11], kz_s.at[0], kz_r.at[0], below + x)
    kv_up = remote(kvw.at[5:8, 0:HALF], kvw.at[1:4, 0:HALF], kz_s.at[1], kz_r.at[1], above + x)

    for i in (2, 1, 3):
        kv_copy(i).start()

    def q_copy(i):
        g = (x + i) & 3
        return remote(qb.at[g], qst.at[x], q_s.at[i], q_r.at[x], z * KV + g)

    for i in (1, 3):
        q_copy(i).start()

    local[0].wait()
    order = ffn_ref[...].astype(F32)
    p_ffn = (order == iota((D, D), 0).astype(F32)).astype(BF)
    p_out[...] = p_ffn
    gather_ffn = p_ffn.T
    local[1].wait()
    packed = dot(gather_ffn, gin[...], 1, 0).astype(BF)
    for g in range(KV):
        snd1[g * D : (g + 1) * D, :] = packed[:, g * WIDE : (g + 1) * WIDE]

    def rows_at(i):
        return pl.ds(pl.multiple_of(i * CHUNK, CHUNK), CHUNK)

    def token_row(peer):
        return pl.ds(pl.multiple_of((peer & 3) * D + (peer >> 2) * CHUNK, CHUNK), CHUNK)

    def send_column(src, dst, src_at, dst_at, s, r, dx):
        def one(i, _):
            peer = ((z + (0x07162534 >> (4 * i))) & 7) * KV + ((x + dx) & 3)
            remote(src.at[src_at(peer)], dst.at[dst_at(me)], s, r, peer).start()
            return 0

        lax.fori_loop(0, 8 if dx else 7, one, 0)

    def send1(dx):
        send_column(snd1, rcv1, token_row, rows_at, a1_s, a1_r, dx)

    send1(0)
    rcv1[rows_at(me), :] = snd1[token_row(me), :]

    def whole(src, dst, s, r):
        n = ROWS - CHUNK
        return remote(src.at[:n], dst.at[:n], s, r, lax.rem(me + 1, N))

    kk, qq = iota((D, D), 0), iota((D, D), 1)
    for u in range(KV):
        d = z * KV + u
        first, end, start = 0, 0, 0
        for t in range(16):
            stop = start + sizes[t]
            inside = (start <= d) & (d < stop)
            first = jnp.where(inside, start, first)
            end = jnp.where(inside, stop, end)
            start = stop
        bias[u, 0:D, :] = jnp.where(kk <= qq, 0.0, NEG)
        for r in (1, 2, 3):
            flag[u * KV + r] = jnp.where(d + r < end, 1, 0)
            later = jnp.where(d + r < end, 0.0, NEG)
            earlier = jnp.where(d + r - 4 >= first, 0.0, NEG)
            bias[u, r * D : (r + 1) * D, :] = jnp.maximum(
                jnp.where(qq >= HALF, later, NEG), jnp.where(kk < HALF, earlier, NEG)
            )
    for i in (1, 3, 2):
        kv_arrived(i)
    kv_down.start()
    kv_up.start()
    q_copy(2).start()
    for dx in (1, 3, 2):
        send1(dx)
    accw[...] = jnp.zeros_like(accw)
    invs[...] = jnp.zeros_like(invs)

    for i in (1, 2, 3):
        order_arrived(i).wait_recv()
    orders = jnp.concatenate([att_ref[u] for u in range(KV)], axis=1)
    orders = jnp.broadcast_to(orders.astype(F32).astype(BF), (D, KV * D))
    pick = picks()
    m_att[...] = scatter_matrix(orders, pick)
    mt_att[...] = gather_matrix(orders, pick)

    kv_down.wait_recv()
    kv_up.wait_recv()

    def forward(i, _):
        u = (x + (0xB4 >> (2 * i))) & 3

        @pl.when(i > 0)
        def _():
            remote(qb.at[0], qst.at[u], q_s.at[0], q_r.at[u], me ^ 1).wait_recv()

        kall[u, 0:D, :] = kvw[4 + u]
        for r in (1, 2, 3):
            kall[u, r * D : r * D + HALF, :] = jnp.where(
                flag[u * KV + r] > 0, kvw[4 + u + r, 0:HALF, :], kvw[u + r, 0:HALF, :]
            )
            kall[u, r * D + HALF : (r + 1) * D, :] = kvw[4 + u + r, HALF:D, :]
        keys, values = kall[u, :, 0:D], kall[u, :, D : 2 * D]
        sc[...] = dot(keys, heads(qst[u]), 1, 1)

        blocks = [slice(b, b + STEP) for b in range(0, KEYS, STEP)]

        def masked(rows):
            return sc[rows, :] + jnp.concatenate([bias[u, rows, :]] * GR, axis=1)

        top = jnp.full((8, WIDE), NEG, F32)
        for rows in blocks:
            top = jnp.maximum(top, jnp.max(masked(rows).reshape(STEP // 8, 8, WIDE), axis=0))
        top = jnp.max(top, axis=0, keepdims=True)
        total = jnp.zeros((8, WIDE), F32)
        for rows in blocks:
            p = jnp.exp2((masked(rows) - top) * (scale * math.log2(math.e)))
            prob[u, rows, :] = p.astype(BF)
            total = total + jnp.sum(p.reshape(STEP // 8, 8, WIDE), axis=0)
        inv = 1.0 / jnp.sum(total, axis=0, keepdims=True)
        o = (dot(values.T, prob[u], 1, 0) * inv).astype(BF)
        for a in range(GR):
            cols = slice(a * D, (a + 1) * D)
            ott[cols, lanes(u, D)] = o[:, cols]
            invs[u, a : a + 1, :] = inv[:, cols]
        return 0

    lax.fori_loop(0, KV, forward, 0)

    snd2[...] = dot(mt_att[...], ott[...], 1, 1).astype(BF)

    for dx in (2, 1, 3, 0):
        send_column(snd2, rcv2, rows_at, token_row, a2_s, a2_r, dx)
    rcv2[token_row(me), :] = snd2[rows_at(me), :]

    whole(snd1, rcv1, a1_s, a1_r).wait_recv()
    every = dot(m_att[...], rcv1[...], 1, 0)
    for u in range(KV):
        up = every[u * D : (u + 1) * D]
        inv = invs[u].T
        for a in range(GR):
            cols = slice(a * D, (a + 1) * D)
            dos[u, :, cols] = (up[:, cols] * inv[:, a : a + 1]).astype(BF)

    def dq_copy(u):
        return remote(dqs.at[u], qg.at[x], dq_s.at[u], dq_r.at[x], z * KV + u)

    def add_part(part, u, term):
        accw[part, 4 + u] += term[0:D]
        for r in (1, 2, 3):
            later = flag[u * KV + r] > 0
            accw[part, 4 + u + r] += jnp.where(later, term[r * D : (r + 1) * D], 0.0)
            accw[part, u + r, 0:HALF, :] += jnp.where(later, 0.0, term[r * D : r * D + HALF])

    def g_copy(part, e):
        g, s = e & 3, g_s.at[part, e]
        if e < 4:
            return remote(gsend.at[part, e, 0:HALF], gdn.at[x, part], s, g_r.at[0, part, x], below + g)
        if e < 8:
            return remote(gsend.at[part, e], grow.at[x, part], s, g_r.at[1, part, x], z * KV + g)
        return remote(gsend.at[part, e], gup.at[x, part], s, g_r.at[2, part, x], above + g)

    def g_all(part, action):
        for e in (8, 9, 10, 1, 2, 3):
            action(g_copy(part, e))
        for e in range(4, 8):

            @pl.when(x != e - 4)
            def _():
                action(g_copy(part, e))

    def send_terms(part):
        for e in range(1, 11):
            gsend[part, e] = accw[part, e].astype(BF)
        g_all(part, lambda c: c.start())
        grow[x, part] = gsend[part, 4 + x]

    def value_terms(u, _):
        add_part(1, u, dot(prob[u], heads(dos[u]), 1, 0))
        return 0

    lax.fori_loop(0, KV, value_terms, 0)
    send_terms(1)

    def backward(i, _):
        u = (x + 1 + i) & 3
        keys, values = kall[u, :, 0:D], kall[u, :, D : 2 * D]
        sc[...] = dot(values, heads(dos[u]), 1, 1)

        blocks = [slice(b, b + STEP) for b in range(0, KEYS, STEP)]
        total = jnp.zeros((8, WIDE), F32)
        for rows in blocks:
            t = prob[u, rows, :].astype(F32) * sc[rows, :]
            total = total + jnp.sum(t.reshape(STEP // 8, 8, WIDE), axis=0)
        inv = jnp.concatenate([invs[u, a : a + 1, :] for a in range(GR)], axis=1)
        delta = jnp.sum(total, axis=0, keepdims=True) * inv

        for rows in blocks:
            dsb[rows, :] = (prob[u, rows, :].astype(F32) * (sc[rows, :] - delta)).astype(BF)
        dq = dot(keys.T, dsb[...], 1, 0) * scale
        for a in range(GR):
            cols = slice(a * D, (a + 1) * D)
            dqs[u, :, cols] = dq[:, cols].T.astype(BF)

        @pl.when(i < 3)
        def _():
            dq_copy(u).start()

        add_part(0, u, dot(dsb[...], heads(qst[u]), 1, 0) * scale)
        return 0

    lax.fori_loop(0, KV, backward, 0)
    qg[x] = dqs[x]

    send_terms(0)

    whole(snd2, rcv2, a2_s, a2_r).wait_recv()
    for part in (1, 0):
        for g in range(KV):
            pl.when(x != g)(
                remote(
                    gsend.at[0, 4], grow.at[g, part], g_s.at[0, 0], g_r.at[1, part, g], me ^ 1
                ).wait_recv
            )
            pl.when(x <= 2)(
                remote(
                    gsend.at[0, 4], gup.at[g, part], g_s.at[0, 0], g_r.at[2, part, g], me ^ 1
                ).wait_recv
            )
            pl.when(x >= 1)(
                remote(
                    gsend.at[0, 4, 0:HALF], gdn.at[g, part], g_s.at[0, 0], g_r.at[0, part, g], me ^ 1
                ).wait_recv
            )

    for i in (1, 2, 3):
        order_copy(i).wait_send()
        kv_copy(i).wait_send()
        q_copy(i).wait_send()
    kv_down.wait_send()
    kv_up.wait_send()
    whole(snd1, rcv1, a1_s, a1_r).wait_send()
    whole(snd2, rcv2, a2_s, a2_r).wait_send()
    for part in (0, 1):
        g_all(part, lambda c: c.wait_send())
    for u in range(KV):

        @pl.when(x != u)
        def _():
            dq_copy(u).wait_send()
            remote(dqs.at[u], qg.at[u], dq_s.at[u], dq_r.at[u], me ^ 1).wait_recv()


def finish(
    got, qg, grow, gup, gdn, p_ffn,
    out_hbm, qg_hbm, kg_hbm, vg_hbm,
    out_v, kg_v, vg_v, sem,
):
    x = lax.axis_index("ctx") & 3
    outs = []

    def send(src, dst):
        outs.append(pltpu.make_async_copy(src, dst, sem.at[len(outs)]))
        outs[-1].start()

    for g in range(KV):
        send(qg.at[g], qg_hbm.at[:, g * WIDE : (g + 1) * WIDE])
    for g in range(KV):
        cols = slice(g * D, (g + 1) * D)
        for part, ref in ((0, kg_v), (1, vg_v)):
            total = grow[g, part].astype(F32) + jnp.where(x <= 2, gup[g, part].astype(F32), 0.0)
            low = total[0:HALF] + jnp.where(x >= 1, gdn[g, part].astype(F32), 0.0)
            ref[0:HALF, cols] = low.astype(BF)
            ref[HALF:D, cols] = total[HALF:D].astype(BF)
    send(kg_v, kg_hbm)
    send(vg_v, vg_hbm)
    for g in range(KV):
        cols = slice(g * WIDE, (g + 1) * WIDE)
        out_v[:, cols] = dot(p_ffn[...], got[g * D : (g + 1) * D, :], 1, 0).astype(BF)
        send(out_v.at[:, cols], out_hbm.at[:, cols])
    for c in outs:
        c.wait()


def body(q, k, v, g, sizes, ffn_order, attn_order):
    hbm = pl.BlockSpec(memory_space=pltpu.HBM)
    vmem = pl.BlockSpec(memory_space=pltpu.VMEM)
    dma = pltpu.SemaphoreType.DMA
    vm = pltpu.VMEM
    got, qg, row, up, down, p_ffn = pl.pallas_call(
        kernel,
        out_shape=(
            vm((ROWS, WIDE), BF),
            vm((KV, D, WIDE), BF),
            vm((KV, 2, D, D), BF),
            vm((KV, 2, D, D), BF),
            vm((KV, 2, HALF, D), BF),
            vm((D, D), BF),
        ),
        in_specs=[hbm] * 7,
        out_specs=(vmem,) * 6,
        scratch_shapes=[
            pltpu.SMEM((16,), jnp.int32),
            vm((1, D), jnp.int32),
            vm((KV, 1, D), jnp.int32),
            vm((KV, D, WIDE), BF),
            vm((KV, D, 2 * D), BF),
            vm((KV, D, WIDE), BF),
            vm((12, D, 2 * D), BF),
            vm((KV, KEYS, 2 * D), BF),
            vm((KV, KEYS, WIDE), BF),
            vm((D, KV * WIDE), BF),
            vm((ROWS, WIDE), BF),
            vm((ROWS, WIDE), BF),
            vm((ROWS, WIDE), BF),
            vm((KV * D, ROWS), BF),
            vm((ROWS, KV * D), BF),
            vm((WIDE, KV * D), BF),
            vm((KV, D, WIDE), BF),
            vm((KEYS, WIDE), F32),
            vm((KEYS, WIDE), BF),
            vm((KV, D, WIDE), BF),
            vm((2, 12, D, D), F32),
            vm((2, 12, D, D), BF),
            vm((KV, KEYS, D), F32),
            vm((KV, 8, D), F32),
            pltpu.SMEM((KV * KV,), jnp.int32),
            dma((16,)),
            dma((4,)),
            dma((4,)),
            dma((4,)),
            dma((4,)),
            dma((2,)),
            dma((2,)),
            dma((4,)),
            dma((4,)),
            dma((4,)),
            dma((4,)),
            dma((2, 12)),
            dma((3, 2, 4)),
            dma,
            dma,
            dma,
            dma,
        ],
        compiler_params=pltpu.CompilerParams(
            collective_id=0, has_side_effects=True, vmem_limit_bytes=56 * 1024 * 1024
        ),
    )(q, k, v, g, sizes, ffn_order, attn_order)
    return pl.pallas_call(
        finish,
        out_shape=(
            jax.ShapeDtypeStruct((D, KV * WIDE), BF),
            jax.ShapeDtypeStruct((D, KV * WIDE), BF),
            jax.ShapeDtypeStruct((D, KV * D), BF),
            jax.ShapeDtypeStruct((D, KV * D), BF),
        ),
        in_specs=[vmem] * 6,
        out_specs=(hbm,) * 4,
        scratch_shapes=[
            vm((D, KV * WIDE), BF),
            vm((D, KV * D), BF),
            vm((D, KV * D), BF),
            dma((10,)),
        ],
        compiler_params=pltpu.CompilerParams(vmem_limit_bytes=8 * 1024 * 1024),
    )(got, qg, row, up, down, p_ffn)


def solution(mesh):
    rows = P(("dp", "ctx"), None)
    return jax.shard_map(
        body,
        mesh=mesh,
        in_specs=(rows, rows, rows, rows, P("dp"), rows, rows),
        out_specs=(rows,) * 4,
        check_vma=False,
    )
```

```python
import math

import jax
import jax.numpy as jnp
from jax import lax
from jax.experimental import pallas as pl
from jax.experimental.pallas import tpu as pltpu
from jax.sharding import PartitionSpec as P

MESH = pl.DeviceIdType.MESH
D = 128
HALF = 64
KV = 4
GR = 5
N = 32
CHUNK = 16
ROWS = N * CHUNK
WIDE = GR * D
KEYS = 4 * D
NEG = -1e30
STEP = 32
BF, F32 = jnp.bfloat16, jnp.float32


def dot(a, b, ca, cb):
    return lax.dot_general(a, b, (((ca,), (cb,)), ((), ())), preferred_element_type=F32)


def iota(shape, dim):
    return lax.broadcasted_iota(jnp.int32, shape, dim)


def picks():
    c, l = iota((ROWS, D), 0), iota((ROWS, D), 1)
    entry = (l == (c >> 4) * 4 + (c & 3)).astype(F32)
    device = (c >> 2) & 3
    return jnp.concatenate(
        [jnp.where(device == u, entry, 0.0).astype(BF) for u in range(KV)], axis=1
    )


def scatter_matrix(orders, pick):
    row, c = iota((D, ROWS), 0), iota((D, ROWS), 1)
    target = dot(orders, pick, 1, 1) + (((c >> 2) & 3) * D).astype(F32)
    row = row.astype(F32)
    return jnp.concatenate([(target == row + float(t * D)).astype(BF) for t in range(KV)], axis=0)


def gather_matrix(orders, pick):
    c, lane = iota((ROWS, D), 0), iota((ROWS, D), 1)
    target = dot(pick, orders, 1, 1) + (((c >> 2) & 3) * D).astype(F32)
    lane = lane.astype(F32)
    return jnp.concatenate([(target == lane + float(t * D)).astype(BF) for t in range(KV)], axis=1)


def heads(x):
    return jnp.concatenate([x[:, a * D : (a + 1) * D] for a in range(GR)], axis=0)


def kernel(
    q_hbm, k_hbm, v_hbm, g_hbm, sizes_hbm, ffn_hbm, att_hbm,
    rcv2, qg, grow, gup, gdn, p_out,
    sizes, ffn_ref, att_ref, qb, kvb, qst, kvw, kall, prob, gin, snd1, rcv1, snd2,
    m_att, mt_att, ott, dos, sc, dsb, dqs, accw, gsend, bias, invs, flag,
    in_sem, att_s, att_r, kv_s, kv_r, kz_s, kz_r, q_s, q_r, dq_s, dq_r, g_s, g_r,
    a1_s, a1_r, a2_s, a2_r,
):
    dp = lax.axis_index("dp")
    me = lax.axis_index("ctx")
    z, x = me >> 2, me & 3
    above, below = ((z + 1) & 7) * KV, ((z + 7) & 7) * KV
    scale = 1.0 / math.sqrt(D)

    def remote(src, dst, s, r, peer):
        return pltpu.make_async_remote_copy(
            src_ref=src, dst_ref=dst, send_sem=s, recv_sem=r,
            device_id=(dp, peer), device_id_type=MESH,
        )

    def lanes(i, width):
        return pl.ds(pl.multiple_of(i * width, D), width)

    barrier = pltpu.get_barrier_semaphore()

    def greet(i, _):
        pl.semaphore_signal(
            barrier, inc=1, device_id=(dp, lax.rem(me + i, N)), device_id_type=MESH
        )
        return 0

    lax.fori_loop(1, N, greet, 0)

    local = [
        pltpu.make_async_copy(ffn_hbm, ffn_ref, in_sem.at[0]),
        pltpu.make_async_copy(g_hbm, gin, in_sem.at[1]),
        pltpu.make_async_copy(att_hbm, att_ref.at[x], in_sem.at[2]),
        pltpu.make_async_copy(sizes_hbm, sizes, in_sem.at[3]),
    ]
    for g in range(KV):
        cols = slice(g * D, (g + 1) * D)
        local += [
            pltpu.make_async_copy(k_hbm.at[:, cols], kvb.at[g, :, 0:D], in_sem.at[4 + 3 * g]),
            pltpu.make_async_copy(v_hbm.at[:, cols], kvb.at[g, :, D:], in_sem.at[5 + 3 * g]),
            pltpu.make_async_copy(
                q_hbm.at[:, g * WIDE : (g + 1) * WIDE], qb.at[g], in_sem.at[6 + 3 * g]
            ),
        ]
    for c in local[4:] + local[:4]:
        c.start()

    local[0].wait()
    order = ffn_ref[...].astype(F32)
    p_ffn = (order == iota((D, D), 0).astype(F32)).astype(BF)
    p_out[...] = p_ffn
    gather_ffn = p_ffn.T
    local[1].wait()
    packed = dot(gather_ffn, gin[...], 1, 0).astype(BF)
    for g in range(KV):
        snd1[g * D : (g + 1) * D, :] = packed[:, g * WIDE : (g + 1) * WIDE]

    for c in local[2:]:
        c.wait()
    kvw[4 + x] = kvb[x]
    qst[x] = qb[x]

    pl.semaphore_wait(barrier, N - 1)

    def order_copy(i):
        return remote(att_ref.at[x], att_ref.at[x], att_s.at[i], att_r.at[i], z * KV + ((x + i) & 3))

    def order_arrived(i):
        u = (x + 4 - i) & 3
        return remote(att_ref.at[u], att_ref.at[u], att_s.at[i], att_r.at[i], me ^ 1)

    for i in (1, 2, 3):
        order_copy(i).start()

    def kv_copy(i):
        g = (x + i) & 3
        return remote(kvb.at[g], kvw.at[4 + x], kv_s.at[i], kv_r.at[x], z * KV + g)

    def kv_arrived(i):
        u = (x + i) & 3
        remote(kvb.at[u], kvw.at[4 + u], kv_s.at[i], kv_r.at[u], z * KV + u).wait_recv()

    kv_down = remote(kvw.at[4:7], kvw.at[8:11], kz_s.at[0], kz_r.at[0], below + x)
    kv_up = remote(kvw.at[5:8, 0:HALF], kvw.at[1:4, 0:HALF], kz_s.at[1], kz_r.at[1], above + x)

    for i in (2, 1, 3):
        kv_copy(i).start()

    def q_copy(i):
        g = (x + i) & 3
        return remote(qb.at[g], qst.at[x], q_s.at[i], q_r.at[x], z * KV + g)

    for i in (1, 3):
        q_copy(i).start()

    def rows_at(i):
        return pl.ds(pl.multiple_of(i * CHUNK, CHUNK), CHUNK)

    def token_row(peer):
        return pl.ds(pl.multiple_of((peer & 3) * D + (peer >> 2) * CHUNK, CHUNK), CHUNK)

    def send_column(src, dst, src_at, dst_at, s, r, dx):
        def one(i, _):
            peer = ((z + (0x07162534 >> (4 * i))) & 7) * KV + ((x + dx) & 3)
            remote(src.at[src_at(peer)], dst.at[dst_at(me)], s, r, peer).start()
            return 0

        lax.fori_loop(0, 8 if dx else 7, one, 0)

    def send1(dx):
        send_column(snd1, rcv1, token_row, rows_at, a1_s, a1_r, dx)

    send1(0)
    rcv1[rows_at(me), :] = snd1[token_row(me), :]

    def whole(src, dst, s, r):
        n = ROWS - CHUNK
        return remote(src.at[:n], dst.at[:n], s, r, lax.rem(me + 1, N))

    kk, qq = iota((D, D), 0), iota((D, D), 1)
    for u in range(KV):
        d = z * KV + u
        first, end, start = 0, 0, 0
        for t in range(16):
            stop = start + sizes[t]
            inside = (start <= d) & (d < stop)
            first = jnp.where(inside, start, first)
            end = jnp.where(inside, stop, end)
            start = stop
        bias[u, 0:D, :] = jnp.where(kk <= qq, 0.0, NEG)
        for r in (1, 2, 3):
            flag[u * KV + r] = jnp.where(d + r < end, 1, 0)
            later = jnp.where(d + r < end, 0.0, NEG)
            earlier = jnp.where(d + r - 4 >= first, 0.0, NEG)
            bias[u, r * D : (r + 1) * D, :] = jnp.maximum(
                jnp.where(qq >= HALF, later, NEG), jnp.where(kk < HALF, earlier, NEG)
            )
    for i in (1, 3, 2):
        kv_arrived(i)
    kv_down.start()
    kv_up.start()
    q_copy(2).start()
    for dx in (1, 3, 2):
        send1(dx)
    accw[...] = jnp.zeros_like(accw)
    invs[...] = jnp.zeros_like(invs)

    for i in (1, 2, 3):
        order_arrived(i).wait_recv()
    orders = jnp.concatenate([att_ref[u] for u in range(KV)], axis=1)
    orders = jnp.broadcast_to(orders.astype(F32).astype(BF), (D, KV * D))
    pick = picks()
    m_att[...] = scatter_matrix(orders, pick)
    mt_att[...] = gather_matrix(orders, pick)

    kv_down.wait_recv()
    kv_up.wait_recv()

    def forward(i, _):
        u = (x + (0xB4 >> (2 * i))) & 3

        @pl.when(i > 0)
        def _():
            remote(qb.at[0], qst.at[u], q_s.at[0], q_r.at[u], me ^ 1).wait_recv()

        kall[u, 0:D, :] = kvw[4 + u]
        for r in (1, 2, 3):
            kall[u, r * D : r * D + HALF, :] = jnp.where(
                flag[u * KV + r] > 0, kvw[4 + u + r, 0:HALF, :], kvw[u + r, 0:HALF, :]
            )
            kall[u, r * D + HALF : (r + 1) * D, :] = kvw[4 + u + r, HALF:D, :]
        keys, values = kall[u, :, 0:D], kall[u, :, D : 2 * D]
        sc[...] = dot(keys, heads(qst[u]), 1, 1)

        blocks = [slice(b, b + STEP) for b in range(0, KEYS, STEP)]

        def masked(rows):
            return sc[rows, :] + jnp.concatenate([bias[u, rows, :]] * GR, axis=1)

        top = jnp.full((8, WIDE), NEG, F32)
        for rows in blocks:
            top = jnp.maximum(top, jnp.max(masked(rows).reshape(STEP // 8, 8, WIDE), axis=0))
        top = jnp.max(top, axis=0, keepdims=True)
        total = jnp.zeros((8, WIDE), F32)
        for rows in blocks:
            p = jnp.exp2((masked(rows) - top) * (scale * math.log2(math.e)))
            prob[u, rows, :] = p.astype(BF)
            total = total + jnp.sum(p.reshape(STEP // 8, 8, WIDE), axis=0)
        inv = 1.0 / jnp.sum(total, axis=0, keepdims=True)
        o = (dot(values.T, prob[u], 1, 0) * inv).astype(BF)
        for a in range(GR):
            cols = slice(a * D, (a + 1) * D)
            ott[cols, lanes(u, D)] = o[:, cols]
            invs[u, a : a + 1, :] = inv[:, cols]
        return 0

    lax.fori_loop(0, KV, forward, 0)

    snd2[...] = dot(mt_att[...], ott[...], 1, 1).astype(BF)

    for dx in (2, 1, 3, 0):
        send_column(snd2, rcv2, rows_at, token_row, a2_s, a2_r, dx)
    rcv2[token_row(me), :] = snd2[rows_at(me), :]

    whole(snd1, rcv1, a1_s, a1_r).wait_recv()
    every = dot(m_att[...], rcv1[...], 1, 0)
    for u in range(KV):
        up = every[u * D : (u + 1) * D]
        inv = invs[u].T
        for a in range(GR):
            cols = slice(a * D, (a + 1) * D)
            dos[u, :, cols] = (up[:, cols] * inv[:, a : a + 1]).astype(BF)

    def dq_copy(u):
        return remote(dqs.at[u], qg.at[x], dq_s.at[u], dq_r.at[x], z * KV + u)

    def backward(i, _):
        u = (x + 1 + i) & 3
        keys, values = kall[u, :, 0:D], kall[u, :, D : 2 * D]
        sc[...] = dot(values, heads(dos[u]), 1, 1)

        blocks = [slice(b, b + STEP) for b in range(0, KEYS, STEP)]
        total = jnp.zeros((8, WIDE), F32)
        for rows in blocks:
            t = prob[u, rows, :].astype(F32) * sc[rows, :]
            total = total + jnp.sum(t.reshape(STEP // 8, 8, WIDE), axis=0)
        inv = jnp.concatenate([invs[u, a : a + 1, :] for a in range(GR)], axis=1)
        delta = jnp.sum(total, axis=0, keepdims=True) * inv

        for rows in blocks:
            dsb[rows, :] = (prob[u, rows, :].astype(F32) * (sc[rows, :] - delta)).astype(BF)
        dq = (dot(keys.T, dsb[...], 1, 0) * scale).astype(BF)
        for a in range(GR):
            cols = slice(a * D, (a + 1) * D)
            dqs[u, :, cols] = dq[:, cols].T

        @pl.when(i < 3)
        def _():
            dq_copy(u).start()

        kpart = dot(dsb[...], heads(qst[u]), 1, 0) * scale
        vpart = dot(prob[u], heads(dos[u]), 1, 0)
        part = jnp.concatenate([kpart, vpart], axis=1)
        accw[4 + u] += part[0:D]
        for r in (1, 2, 3):
            later = flag[u * KV + r] > 0
            accw[4 + u + r] += jnp.where(later, part[r * D : (r + 1) * D], 0.0)
            accw[u + r, 0:HALF, :] += jnp.where(later, 0.0, part[r * D : r * D + HALF])
        return 0

    lax.fori_loop(0, KV, backward, 0)
    qg[x] = dqs[x]

    for e in range(1, 11):
        gsend[e] = accw[e].astype(BF)

    def g_copy(e):
        g = e & 3
        if e < 4:
            return remote(gsend.at[e, 0:HALF], gdn.at[x], g_s.at[e], g_r.at[0, x], below + g)
        if e < 8:
            return remote(gsend.at[e], grow.at[x], g_s.at[e], g_r.at[1, x], z * KV + g)
        return remote(gsend.at[e], gup.at[x], g_s.at[e], g_r.at[2, x], above + g)

    for e in (8, 9, 10, 1, 2, 3):
        g_copy(e).start()
    for e in range(4, 8):
        pl.when(x != e - 4)(g_copy(e).start)
    grow[x] = gsend[4 + x]

    whole(snd2, rcv2, a2_s, a2_r).wait_recv()
    for g in range(KV):
        pl.when(x != g)(
            remote(gsend.at[4], grow.at[g], g_s.at[0], g_r.at[1, g], me ^ 1).wait_recv
        )
        pl.when(x <= 2)(remote(gsend.at[4], gup.at[g], g_s.at[0], g_r.at[2, g], me ^ 1).wait_recv)
        pl.when(x >= 1)(
            remote(gsend.at[4, 0:HALF], gdn.at[g], g_s.at[0], g_r.at[0, g], me ^ 1).wait_recv
        )

    for i in (1, 2, 3):
        order_copy(i).wait_send()
        kv_copy(i).wait_send()
        q_copy(i).wait_send()
    kv_down.wait_send()
    kv_up.wait_send()
    whole(snd1, rcv1, a1_s, a1_r).wait_send()
    whole(snd2, rcv2, a2_s, a2_r).wait_send()
    for e in (8, 9, 10, 1, 2, 3):
        g_copy(e).wait_send()
    for u in range(KV):

        @pl.when(x != u)
        def _():
            g_copy(4 + u).wait_send()
            dq_copy(u).wait_send()
            remote(dqs.at[u], qg.at[u], dq_s.at[u], dq_r.at[u], me ^ 1).wait_recv()


def finish(
    got, qg, grow, gup, gdn, p_ffn,
    out_hbm, qg_hbm, kg_hbm, vg_hbm,
    out_v, kg_v, vg_v, sem,
):
    x = lax.axis_index("ctx") & 3
    outs = []

    def send(src, dst):
        outs.append(pltpu.make_async_copy(src, dst, sem.at[len(outs)]))
        outs[-1].start()

    for g in range(KV):
        send(qg.at[g], qg_hbm.at[:, g * WIDE : (g + 1) * WIDE])
    for g in range(KV):
        total = grow[g].astype(F32) + jnp.where(x <= 2, gup[g].astype(F32), 0.0)
        low = total[0:HALF] + jnp.where(x >= 1, gdn[g].astype(F32), 0.0)
        high = total[HALF:D]
        cols = slice(g * D, (g + 1) * D)
        for ref, lane in ((kg_v, 0), (vg_v, D)):
            ref[0:HALF, cols] = low[:, lane : lane + D].astype(BF)
            ref[HALF:D, cols] = high[:, lane : lane + D].astype(BF)
    send(kg_v, kg_hbm)
    send(vg_v, vg_hbm)
    for g in range(KV):
        cols = slice(g * WIDE, (g + 1) * WIDE)
        out_v[:, cols] = dot(p_ffn[...], got[g * D : (g + 1) * D, :], 1, 0).astype(BF)
        send(out_v.at[:, cols], out_hbm.at[:, cols])
    for c in outs:
        c.wait()


def body(q, k, v, g, sizes, ffn_order, attn_order):
    hbm = pl.BlockSpec(memory_space=pltpu.HBM)
    vmem = pl.BlockSpec(memory_space=pltpu.VMEM)
    dma = pltpu.SemaphoreType.DMA
    vm = pltpu.VMEM
    got, qg, row, up, down, p_ffn = pl.pallas_call(
        kernel,
        out_shape=(
            vm((ROWS, WIDE), BF),
            vm((KV, D, WIDE), BF),
            vm((KV, D, 2 * D), BF),
            vm((KV, D, 2 * D), BF),
            vm((KV, HALF, 2 * D), BF),
            vm((D, D), BF),
        ),
        in_specs=[hbm] * 7,
        out_specs=(vmem,) * 6,
        scratch_shapes=[
            pltpu.SMEM((16,), jnp.int32),
            vm((1, D), jnp.int32),
            vm((KV, 1, D), jnp.int32),
            vm((KV, D, WIDE), BF),
            vm((KV, D, 2 * D), BF),
            vm((KV, D, WIDE), BF),
            vm((12, D, 2 * D), BF),
            vm((KV, KEYS, 2 * D), BF),
            vm((KV, KEYS, WIDE), BF),
            vm((D, KV * WIDE), BF),
            vm((ROWS, WIDE), BF),
            vm((ROWS, WIDE), BF),
            vm((ROWS, WIDE), BF),
            vm((KV * D, ROWS), BF),
            vm((ROWS, KV * D), BF),
            vm((WIDE, KV * D), BF),
            vm((KV, D, WIDE), BF),
            vm((KEYS, WIDE), F32),
            vm((KEYS, WIDE), BF),
            vm((KV, D, WIDE), BF),
            vm((12, D, 2 * D), F32),
            vm((12, D, 2 * D), BF),
            vm((KV, KEYS, D), F32),
            vm((KV, 8, D), F32),
            pltpu.SMEM((KV * KV,), jnp.int32),
            dma((16,)),
            dma((4,)),
            dma((4,)),
            dma((4,)),
            dma((4,)),
            dma((2,)),
            dma((2,)),
            dma((4,)),
            dma((4,)),
            dma((4,)),
            dma((4,)),
            dma((12,)),
            dma((3, 4)),
            dma,
            dma,
            dma,
            dma,
        ],
        compiler_params=pltpu.CompilerParams(
            collective_id=0, has_side_effects=True, vmem_limit_bytes=56 * 1024 * 1024
        ),
    )(q, k, v, g, sizes, ffn_order, attn_order)
    return pl.pallas_call(
        finish,
        out_shape=(
            jax.ShapeDtypeStruct((D, KV * WIDE), BF),
            jax.ShapeDtypeStruct((D, KV * WIDE), BF),
            jax.ShapeDtypeStruct((D, KV * D), BF),
            jax.ShapeDtypeStruct((D, KV * D), BF),
        ),
        in_specs=[vmem] * 6,
        out_specs=(hbm,) * 4,
        scratch_shapes=[
            vm((D, KV * WIDE), BF),
            vm((D, KV * D), BF),
            vm((D, KV * D), BF),
            dma((10,)),
        ],
        compiler_params=pltpu.CompilerParams(vmem_limit_bytes=8 * 1024 * 1024),
    )(got, qg, row, up, down, p_ffn)


def solution(mesh):
    rows = P(("dp", "ctx"), None)
    return jax.shard_map(
        body,
        mesh=mesh,
        in_specs=(rows, rows, rows, rows, P("dp"), rows, rows),
        out_specs=(rows,) * 4,
        check_vma=False,
    )
```
